32 devices in a mesh: dp: 4 (over z), seq: 4 (over y, x), tensor: 2 (over core).
Axes of the slice: x: 2, y: 2, z: 4, core: 2. Of those that a mesh axis runs over, the one named last changes fastest.
Arguments:
- tokens: bfloat16 [2, 4, 1024, 1536], P(None, 'dp', 'seq'), may hold values from -6 to 6
- cotangent: bfloat16 [2, 4, 1024, 1536], P(None, 'dp', 'seq'), may hold values from -6 to 6
- norm_gain: float32 [2, 1536], replicated, may hold values from 0.1 to 1.9
- inner_weight: bfloat16 [2, 1536, 2, 3072], P(None, ('dp', 'seq'), None, 'tensor'), may hold values from -0.15625 to 0.15625
- rate_weight: bfloat16 [2, 1536, 48], P(None, ('dp', 'seq'), 'tensor'), may hold values from -0.15625 to 0.15625
- state_weight: bfloat16 [2, 1536, 256], P(None, ('dp', 'seq', 'tensor')), may hold values from -0.15625 to 0.15625
- conv_inner: float32 [2, 4, 3072], P(None, None, 'tensor'), may hold values from -3 to 3
- bias_inner: float32 [2, 3072], P(None, 'tensor'), may hold values from -0.5 to 0.5
- conv_state: float32 [2, 4, 256], replicated, may hold values from -3 to 3
- bias_state: float32 [2, 256], replicated, may hold values from -0.5 to 0.5
- rate_bias: float32 [2, 48], P(None, 'tensor'), may hold values from -8 to -3
- decay_log: float32 [2, 48], P(None, 'tensor'), may hold values from -1.5 to 0.5
- skip_gain: float32 [2, 48], P(None, 'tensor'), may hold values from 0.5 to 1.5
- gate_gain: float32 [2, 3072], P(None, 'tensor'), may hold values from 0.1 to 1.9
- out_weight: bfloat16 [2, 3072, 1536], P(None, 'tensor', ('dp', 'seq')), may hold values from -0.109375 to 0.109375
Outputs:
- output: float32 [2, 4, 1024, 1536], P(None, 'dp', 'seq')
- input_grad: float32 [2, 4, 1024, 1536], P(None, 'dp', 'seq')
- grad_norm_gain: float32 [2, 1536], replicated
- grad_inner_weight: float32 [2, 1536, 2, 3072], P(None, ('dp', 'seq'), None, 'tensor')
- grad_rate_weight: float32 [2, 1536, 48], P(None, ('dp', 'seq'), 'tensor')
- grad_state_weight: float32 [2, 1536, 256], P(None, ('dp', 'seq', 'tensor'))
- grad_conv_inner: float32 [2, 4, 3072], P(None, None, 'tensor')
- grad_bias_inner: float32 [2, 3072], P(None, 'tensor')
- grad_conv_state: float32 [2, 4, 256], replicated
- grad_bias_state: float32 [2, 256], replicated
- grad_rate_bias: float32 [2, 48], P(None, 'tensor')
- grad_decay_log: float32 [2, 48], P(None, 'tensor')
- grad_skip_gain: float32 [2, 48], P(None, 'tensor')
- grad_gate_gain: float32 [2, 3072], P(None, 'tensor')
- grad_out_weight: float32 [2, 3072, 1536], P(None, 'tensor', ('dp', 'seq'))
The draws below stay inside these ranges and needn't reach their ends.
All inputs are finite; a program needn't handle non-finite values.
Results may differ from the reference program's by a relative error of at most 0.019.
Values may be sent and summed in bfloat16 or wider, within the bound.
No kernel may reach another device: no remote copies, remote signals or barrier semaphores. Data moves between devices by JAX's collectives and lax.ppermute only.
A program may use at most 512 MiB of HBM per device.

```python
import jax
import jax.numpy as jnp
from jax import lax

D = 1536
DI = 3072
N = 128
P_SIZE = 64
K = 4
H = 48
STRETCH = 128
MB = 2
L = 2
SEQS = 4
LEN = 1024


def block_scale(key, dims, shards, least, high):
    factor_of = 1.0
    for dim, parts in shards:
        draws = jax.random.uniform(jax.random.fold_in(jax.random.fold_in(key, 6), dim), (parts,), jnp.float32, least / len(shards), high / len(shards))
        factor_of = factor_of * jnp.repeat(jnp.exp(draws), dims[dim] // parts).reshape((-1,) + (1,) * (len(dims) - 1 - dim))
    return factor_of


def gaussian(stream_key, shape, deviation, limit, cuts=(), dtype=jnp.bfloat16):
    drawn = jax.random.normal(stream_key, shape, jnp.float32) * deviation
    if len(cuts) > 0:
        drawn = block_scale(stream_key, shape, cuts, -0.22, 0.18) * drawn
    return jnp.clip(drawn, min=-limit, max=limit).astype(dtype)


def setup_inputs(seed: int = 0) -> dict:
    key_of = jax.random.split(jax.random.key(seed), 16)
    tokens = gaussian(key_of[0], (MB, SEQS, LEN, D), 1.0, 6.0, ((1, 4), (2, 4)))
    cotangent = gaussian(key_of[1], (MB, SEQS, LEN, D), 1.0, 6.0, ((1, 4), (2, 4)))
    norm_gain = jnp.clip(1.0 + 0.18 * jax.random.normal(key_of[2], (L, D), jnp.float32), 0.1, 1.9)
    inner_weight = gaussian(key_of[3], (L, D, 2, DI), D ** -0.5, 0.15625, ((1, 16), (3, 2)))
    rate_weight = gaussian(key_of[4], (L, D, H), D ** -0.5, 0.15625, ((1, 16), (2, 2)))
    state_weight = gaussian(key_of[5], (L, D, 2 * N), D ** -0.5, 0.15625, ((1, 32),))
    conv_inner = gaussian(key_of[6], (L, K, DI), 0.5, 3.0, ((2, 2),), jnp.float32)
    bias_inner = jnp.clip(jax.random.uniform(key_of[7], (L, DI), jnp.float32, -0.5, 0.5) * block_scale(key_of[7], (L, DI), ((1, 2),), -0.4, 0.0), -0.5, 0.5)
    conv_state = gaussian(key_of[8], (L, K, 2 * N), 0.5, 3.0, (), jnp.float32)
    bias_state = jnp.clip(jax.random.uniform(key_of[9], (L, 2 * N), jnp.float32, -0.5, 0.5), -0.5, 0.5)
    rate_bias = jnp.clip(-8.0 + 5.0 * jax.random.uniform(key_of[10], (L, H), jnp.float32) ** block_scale(key_of[10], (L, H), ((1, 2),), -0.2, 0.2), -8.0, -3.0)
    decay_log = jnp.clip(-1.5 + 2.0 * jax.random.uniform(key_of[11], (L, H), jnp.float32) ** block_scale(key_of[11], (L, H), ((1, 2),), -0.2, 0.2), -1.5, 0.5)
    skip_gain = jnp.clip(0.5 + 1.0 * jax.random.uniform(key_of[12], (L, H), jnp.float32) ** block_scale(key_of[12], (L, H), ((1, 2),), -0.2, 0.2), 0.5, 1.5)
    gate_gain = jnp.clip(1.0 + 0.18 * jax.random.normal(key_of[13], (L, DI), jnp.float32), 0.1, 1.9)
    out_weight = gaussian(key_of[14], (L, DI, D), DI ** -0.5, 0.109375, ((1, 2), (2, 16)))
    return dict(tokens=tokens, cotangent=cotangent, norm_gain=norm_gain, inner_weight=inner_weight, rate_weight=rate_weight, state_weight=state_weight, conv_inner=conv_inner, bias_inner=bias_inner, conv_state=conv_state, bias_state=bias_state, rate_bias=rate_bias, decay_log=decay_log, skip_gain=skip_gain, gate_gain=gate_gain, out_weight=out_weight)


EPSILON = 1e-05
HIGHEST = lax.Precision.HIGHEST

@jax.custom_vjp
def low(v):
    return lax.optimization_barrier(v.astype(jnp.bfloat16)).astype(jnp.float32)

@jax.custom_vjp
def low_back(v):
    return v

def low_keep(v):
    return (low(v), None)

def low_pass(kept, grad):
    return (grad,)

def back_keep(v):
    return (v, None)

def back_low(kept, grad):
    return (low(grad),)
low.defvjp(low_keep, low_pass)
low_back.defvjp(back_keep, back_low)

def product(left_side, right_side):
    return jnp.dot(left_side, right_side, precision=HIGHEST, preferred_element_type=jnp.float32)

def conv_silu(padded, weight, conv_bias):
    conv_width = weight.shape[0]
    out_rows = padded.shape[0] - conv_width + 1
    summed = conv_bias[None, :] + weight[0][None, :] * padded[0:out_rows]
    for offset in range(1, conv_width):
        summed = summed + weight[offset][None, :] * padded[offset:offset + out_rows]
    return jax.nn.silu(summed)

def block_step(carry_state, pieces):
    inputs, keys_b, queries_c, step_rates, decays = pieces
    running = jnp.cumsum(decays, axis=0)
    block_len = inputs.shape[0]
    causal = jnp.arange(block_len)[:, None] >= jnp.arange(block_len)[None, :]
    spread = running.T[:, :, None] - running.T[:, None, :]
    weights = jnp.exp(jnp.where(causal[None, :, :], spread, -jnp.inf))
    scores = product(queries_c, keys_b.T)
    mixing = scores[None, :, :] * weights * step_rates.T[:, None, :]
    inside = jnp.einsum('hts,shp->thp', mixing, inputs, precision=HIGHEST)
    carried = jnp.einsum('tn,hpn->thp', queries_c, carry_state, precision=HIGHEST) * jnp.exp(running)[:, :, None]
    tail_weight = jnp.exp(running[-1][None, :] - running) * step_rates
    update = jnp.einsum('shp,sn->hpn', tail_weight[:, :, None] * inputs, keys_b, precision=HIGHEST)
    return (jnp.exp(running[-1])[:, None, None] * carry_state + update, inside + carried)

def to_blocks(values):
    return values.reshape((values.shape[0] // STRETCH, STRETCH) + values.shape[1:])

def mixer_layer(hidden, params):
    norm_gain, inner_weight, rate_weight, state_weight, conv_inner, bias_inner, conv_state, bias_state, rate_bias, decay_log, skip_gain, gate_gain, out_weight = params
    seq_rows = hidden.shape[0]
    row_scale = lax.rsqrt(lax.optimization_barrier(jnp.mean(hidden * hidden, axis=1, keepdims=True)) + EPSILON)
    normed = low(hidden * row_scale * norm_gain[None, :])
    gate_inner = low_back(product(normed, inner_weight.reshape(inner_weight.shape[0], -1)))
    rate_raw = low_back(product(normed, rate_weight))
    state_raw = product(normed, state_weight)
    gate_part = gate_inner[:, :DI]
    conv_input = low(jnp.concatenate([gate_inner[:, DI:], state_raw], axis=1))
    padded = jnp.concatenate([jnp.zeros((K - 1, conv_input.shape[1]), jnp.float32), conv_input], axis=0)
    conv_weight = jnp.concatenate([conv_inner, conv_state], axis=1)
    conv_bias = jnp.concatenate([bias_inner, bias_state])
    activated = conv_silu(padded, conv_weight, conv_bias)
    inputs = activated[:, :DI].reshape(seq_rows, H, P_SIZE)
    keys_b = activated[:, DI:DI + N]
    queries_c = activated[:, DI + N:]
    step_rates = jax.nn.softplus(rate_raw + rate_bias[None, :])
    decays = -jnp.exp(decay_log)[None, :] * step_rates
    zero_state = jnp.zeros((H, P_SIZE, N), jnp.float32)
    _, block_out = lax.scan(jax.checkpoint(block_step), zero_state, (to_blocks(inputs), to_blocks(keys_b), to_blocks(queries_c), to_blocks(step_rates), to_blocks(decays)))
    mixed_out = block_out.reshape(seq_rows, H, P_SIZE) + skip_gain[None, :, None] * inputs
    gated_out = mixed_out.reshape(seq_rows, DI) * jax.nn.silu(gate_part)
    gate_scale = lax.rsqrt(lax.optimization_barrier(jnp.mean(gated_out * gated_out, axis=1, keepdims=True)) + EPSILON)
    normed_out = low(gated_out * gate_scale * gate_gain[None, :])
    return hidden + low_back(product(normed_out, out_weight))

def network(sequence, params):
    hidden = sequence
    for layer_index in range(L):
        hidden = mixer_layer(hidden, tuple((stacked[layer_index] for stacked in params)))
    return hidden

def reference(tokens, cotangent, norm_gain, inner_weight, rate_weight, state_weight, conv_inner, bias_inner, conv_state, bias_state, rate_bias, decay_log, skip_gain, gate_gain, out_weight):
    params = tuple((stacked.astype(jnp.float32) for stacked in (norm_gain, inner_weight, rate_weight, state_weight, conv_inner, bias_inner, conv_state, bias_state, rate_bias, decay_log, skip_gain, gate_gain, out_weight)))
    sequences = tokens.astype(jnp.float32).reshape(-1, LEN, D)
    cotangents = cotangent.astype(jnp.float32).reshape(-1, LEN, D)

    def one_sequence(totals, seq_pair):
        result, pullback = jax.vjp(network, seq_pair[0], params)
        seq_grad, param_grads = pullback(seq_pair[1])
        return (jax.tree.map(jnp.add, totals, param_grads), (result, seq_grad))
    initial = jax.tree.map(jnp.zeros_like, params)
    totals, (results, seq_grads) = lax.scan(one_sequence, initial, (sequences, cotangents))
    full_shape = tokens.shape
    return (results.reshape(full_shape), seq_grads.reshape(full_shape), totals[0], totals[1], totals[2], totals[3], totals[4], totals[5], totals[6], totals[7], totals[8], totals[9], totals[10], totals[11], totals[12])
```

```python
import jax
import jax.numpy as jnp
from jax import lax
from jax.experimental import pallas as pl
from jax.experimental.pallas import tpu as pltpu
from jax.sharding import PartitionSpec as P

DI = 3072
STRETCH = 128


EPSILON = 1e-05
HIGHEST = lax.Precision.HIGHEST


def shifted(value, axis, steps):
    count = lax.axis_size(axis)
    leading, last = (max(0, -steps), min(count, count - steps))
    return lax.ppermute(value, axis, [(source, source + steps) for source in range(leading, last)])


def carried_in(array, axis, combine, identity):
    length, place = (lax.axis_size(axis), lax.axis_index(axis))
    everything = jax.tree.map(
        lambda part, kind: lax.all_gather(part.astype(kind), axis),
        array,
        (jnp.bfloat16, jnp.bfloat16),
    )
    start = jax.tree.map(
        lambda part, zero: jnp.broadcast_to(jnp.asarray(zero, part.dtype), part.shape),
        array,
        identity,
    )

    def turn(k, before):
        reached = k < place
        new = combine(
            before, jax.tree.map(lambda part, own: part[k].astype(own.dtype), everything, array)
        )
        return jax.tree.map(lambda a, b: jnp.where(reached, a, b), new, before)

    return lax.fori_loop(0, length, turn, start)


def carried_in_2(array, axis, join, neutral):
    count = lax.axis_size(axis)
    place = lax.axis_index(axis)
    ahead = count - 1 - place
    gathered = jax.tree.map(
        lambda a, kind: lax.all_gather(a.astype(kind), axis),
        array,
        jax.tree.map(lambda a: jnp.bfloat16 if a.dtype == jnp.float32 else a.dtype, array),
    )
    state = jax.tree.map(lambda a, e: jnp.zeros_like(a) + jnp.asarray(e, a.dtype), array, neutral)

    def one(turn, state):
        source = count - 1 - turn
        return join(
            state,
            jax.tree.map(
                lambda a, own: lax.dynamic_index_in_dim(a, source, 0, False).astype(own.dtype),
                gathered,
                array,
            ),
        )

    return lax.fori_loop(0, ahead, one, state)


def product(left_side, right_side):
    return jnp.dot(left_side, right_side, precision=HIGHEST, preferred_element_type=jnp.float32)


def conv_silu(padded, weight, conv_bias):
    conv_width = weight.shape[0]
    out_rows = padded.shape[0] - conv_width + 1
    summed = conv_bias[None, :] + weight[0][None, :] * padded[0:out_rows]
    for offset in range(1, conv_width):
        summed = summed + weight[offset][None, :] * padded[offset : offset + out_rows]
    return jax.nn.silu(summed)


def block_step(carry_state, pieces):
    inputs, keys_b, queries_c, step_rates, decays = pieces
    running = jnp.cumsum(decays, axis=0)
    block_len = inputs.shape[0]
    causal = jnp.arange(block_len)[:, None] >= jnp.arange(block_len)[None, :]
    spread = running.T[:, :, None] - running.T[:, None, :]
    weights = jnp.exp(jnp.where(causal[None, :, :], spread, -jnp.inf))
    scores = product(queries_c, keys_b.T)
    mixing = scores[None, :, :] * weights * step_rates.T[:, None, :]
    inside = jnp.einsum("hts,shp->thp", mixing, inputs, precision=HIGHEST)
    carried = (
        jnp.einsum("tn,hpn->thp", queries_c, carry_state, precision=HIGHEST)
        * jnp.exp(running)[:, :, None]
    )
    tail_weight = jnp.exp(running[-1][None, :] - running) * step_rates
    update = jnp.einsum("shp,sn->hpn", tail_weight[:, :, None] * inputs, keys_b, precision=HIGHEST)
    return (jnp.exp(running[-1])[:, None, None] * carry_state + update, inside + carried)


def state_step(carry_state, pieces):
    inputs, keys_b, step_rates, decays = pieces
    running = jnp.cumsum(decays, axis=0)
    tail_weight = jnp.exp(running[-1][None, :] - running) * step_rates
    update = jnp.einsum("shp,sn->hpn", tail_weight[:, :, None] * inputs, keys_b, precision=HIGHEST)
    return (jnp.exp(running[-1])[:, None, None] * carry_state + update, None)


def to_blocks(values):
    return values.reshape((values.shape[0] // STRETCH, STRETCH) + values.shape[1:])


def span_summary(inputs, keys_b, step_rates, decays):
    zero_state = jnp.zeros((inputs.shape[1], inputs.shape[2], keys_b.shape[1]), jnp.float32)
    end_state, _ = lax.scan(
        state_step,
        zero_state,
        (to_blocks(inputs), to_blocks(keys_b), to_blocks(step_rates), to_blocks(decays)),
    )
    return (jnp.exp(jnp.sum(decays, axis=0)), end_state)


def span_output(inputs, keys_b, queries_c, step_rates, decays, entry_state, skip_gain):
    _, block_out = lax.scan(
        block_step,
        entry_state,
        (
            to_blocks(inputs),
            to_blocks(keys_b),
            to_blocks(queries_c),
            to_blocks(step_rates),
            to_blocks(decays),
        ),
    )
    mixed_out = block_out.reshape(inputs.shape) + skip_gain[None, :, None] * inputs
    return mixed_out.reshape(inputs.shape[0], -1)


def rate_piece(rate_raw, rate_bias, decay_log):
    step_rates = jax.nn.softplus(rate_raw + rate_bias[None, :])
    return (step_rates, -jnp.exp(decay_log)[None, :] * step_rates)


def norm_piece(hidden, norm_gain):
    row_scale = lax.rsqrt(jnp.mean(hidden * hidden, axis=1, keepdims=True) + EPSILON)
    return hidden * row_scale * norm_gain[None, :]


def chain_combine(earlier, following):
    return (earlier[0] * following[0], following[1] + following[0][:, None, None] * earlier[1])


def gather_layer(inner_weight, rate_weight, state_weight, out_weight, layer_index):
    inner_full, rate_full, out_full = (
        lax.all_gather(inner_weight[layer_index], ("dp", "seq"), axis=0, tiled=True),
        lax.all_gather(rate_weight[layer_index], ("dp", "seq"), axis=0, tiled=True),
        lax.all_gather(out_weight[layer_index], ("dp", "seq"), axis=1, tiled=True),
    )
    state_full = lax.all_gather(
        state_weight[layer_index], ("dp", "seq", "tensor"), axis=0, tiled=True
    )
    return (inner_full.reshape(inner_full.shape[0], -1), rate_full, state_full, out_full)


def forward_layer(hidden, weights, small_params, layer_index):
    inner_full, rate_full, state_full, out_full = weights
    (
        norm_gain,
        conv_inner,
        bias_inner,
        conv_state,
        bias_state,
        rate_bias,
        decay_log,
        skip_gain,
        gate_gain,
    ) = small_params
    seq_rows = hidden.shape[0]
    normed_full, norm_pull = jax.vjp(norm_piece, hidden, norm_gain[layer_index])
    normed = normed_full.astype(jnp.bfloat16)
    gate_inner = jnp.dot(normed, inner_full, preferred_element_type=jnp.float32)
    rate_raw = jnp.dot(normed, rate_full, preferred_element_type=jnp.float32)
    state_raw = jnp.dot(normed, state_full, preferred_element_type=jnp.float32)
    local_width = gate_inner.shape[1] // 2
    gate_part = gate_inner[:, :local_width]
    conv_input = jnp.concatenate([gate_inner[:, local_width:], state_raw], axis=1).astype(
        jnp.bfloat16
    )
    edge_count = conv_inner.shape[1] - 1
    edge_rows = shifted(conv_input[seq_rows - edge_count :], "seq", 1)
    padded = jnp.concatenate([edge_rows, conv_input], axis=0).astype(jnp.float32)
    conv_weight = jnp.concatenate([conv_inner[layer_index], conv_state[layer_index]], axis=1)
    conv_bias = jnp.concatenate([bias_inner[layer_index], bias_state[layer_index]])
    activated, conv_pull = jax.vjp(conv_silu, padded, conv_weight, conv_bias)
    state_size = state_raw.shape[1] // 2
    head_count = rate_bias.shape[1]
    inputs = activated[:, :local_width].reshape(seq_rows, head_count, local_width // head_count)
    keys_b = activated[:, local_width : local_width + state_size]
    queries_c = activated[:, local_width + state_size :]
    (step_rates, decays), rate_pull = jax.vjp(
        rate_piece, rate_raw, rate_bias[layer_index], decay_log[layer_index]
    )
    (span_decay, span_state), summary_pull = jax.vjp(
        span_summary, inputs, keys_b, step_rates, decays
    )
    identity = (jnp.ones_like(span_decay), jnp.zeros_like(span_state))
    entry_state = carried_in((span_decay, span_state), "seq", chain_combine, identity)[1]
    mixed_out, output_pull = jax.vjp(
        span_output,
        inputs,
        keys_b,
        queries_c,
        step_rates,
        decays,
        entry_state,
        skip_gain[layer_index],
    )
    gate_silu, silu_pull = jax.vjp(jax.nn.silu, gate_part)
    gated_out = mixed_out * gate_silu
    square_sum = lax.psum(jnp.sum(gated_out * gated_out, axis=1), "tensor")
    gate_scale = lax.rsqrt(square_sum / DI + EPSILON)[:, None]
    normed_out = (gated_out * gate_scale * gate_gain[layer_index][None, :]).astype(jnp.bfloat16)
    partial_out = jnp.dot(normed_out, out_full, preferred_element_type=jnp.float32)
    new_hidden = hidden + lax.psum(partial_out, "tensor")
    kept_values = (
        norm_pull,
        normed,
        silu_pull,
        gate_silu,
        mixed_out,
        gated_out,
        gate_scale,
        normed_out,
        conv_pull,
        rate_pull,
        summary_pull,
        output_pull,
        span_decay,
        entry_state,
        identity,
        local_width,
        edge_count,
    )
    return (new_hidden, kept_values)


def backward_layer(grad_hidden, weights, small_params, kept_values, layer_index):
    inner_full, rate_full, state_full, out_full = weights
    gate_gain = small_params[8]
    (
        norm_pull,
        normed,
        silu_pull,
        gate_silu,
        mixed_out,
        gated_out,
        gate_scale,
        normed_out,
        conv_pull,
        rate_pull,
        summary_pull,
        output_pull,
        span_decay,
        entry_state,
        identity,
        local_width,
        edge_count,
    ) = kept_values
    seq_rows = normed.shape[0]
    grad_low = grad_hidden.astype(jnp.bfloat16)
    grad_out_weight = jnp.dot(normed_out.T, grad_low, preferred_element_type=jnp.float32)
    grad_normed_out = jnp.dot(grad_low, out_full.T, preferred_element_type=jnp.float32)
    grad_gate_gain = jnp.sum(grad_normed_out * gated_out * gate_scale, axis=0)
    scaled_grad = grad_normed_out * gate_gain[layer_index][None, :]
    inner_sum = lax.psum(jnp.sum(scaled_grad * gated_out, axis=1), "tensor")
    scale_cube = gate_scale * gate_scale * gate_scale
    grad_gated = gate_scale * scaled_grad - gated_out * scale_cube * (inner_sum[:, None] / DI)
    grad_mixed = grad_gated * gate_silu
    grad_gate = silu_pull(grad_gated * mixed_out)[0]
    grad_inputs, grad_keys, grad_queries, grad_rates, grad_decays, grad_entry, grad_skip_gain = (
        output_pull(grad_mixed)
    )
    end_grads = carried_in_2((span_decay, grad_entry), "seq", chain_combine, identity)[1]
    grad_span_decay = jnp.sum(end_grads * entry_state, axis=(1, 2))
    more_inputs, more_keys, more_rates, more_decays = summary_pull((grad_span_decay, end_grads))
    grad_raw, grad_rate_bias, grad_decay_log = rate_pull(
        (grad_rates + more_rates, grad_decays + more_decays)
    )
    grad_activated = jnp.concatenate(
        [(grad_inputs + more_inputs).reshape(seq_rows, -1), grad_keys + more_keys, grad_queries],
        axis=1,
    )
    grad_padded, grad_conv_weight, grad_conv_bias = conv_pull(grad_activated)
    edge_back = shifted(grad_padded[:edge_count], "seq", -1)
    grad_conv_input = grad_padded[edge_count:]
    grad_conv_input = jnp.concatenate(
        [
            grad_conv_input[: seq_rows - edge_count],
            grad_conv_input[seq_rows - edge_count :] + edge_back,
        ],
        axis=0,
    )
    grad_inner_low = jnp.concatenate([grad_gate, grad_conv_input[:, :local_width]], axis=1).astype(
        jnp.bfloat16
    )
    grad_state_raw = grad_conv_input[:, local_width:]
    grad_rate_low = grad_raw.astype(jnp.bfloat16)
    grad_inner_weight = jnp.dot(normed.T, grad_inner_low, preferred_element_type=jnp.float32)
    grad_rate_weight = jnp.dot(normed.T, grad_rate_low, preferred_element_type=jnp.float32)
    grad_state_weight = product(normed.astype(jnp.float32).T, grad_state_raw)
    grad_normed_part = (
        jnp.dot(grad_inner_low, inner_full.T, preferred_element_type=jnp.float32)
        + jnp.dot(grad_rate_low, rate_full.T, preferred_element_type=jnp.float32)
        + product(grad_state_raw, state_full.astype(jnp.float32).T)
    )
    grad_normed, grad_conv_state, grad_bias_state = (
        lax.psum(grad_normed_part.astype(jnp.bfloat16), "tensor").astype(jnp.float32),
        lax.psum(grad_conv_weight[:, local_width:].astype(jnp.bfloat16), "tensor").astype(
            jnp.float32
        ),
        lax.psum(grad_conv_bias[local_width:].astype(jnp.bfloat16), "tensor").astype(jnp.float32),
    )
    grad_hidden_norm, grad_norm_gain = norm_pull(grad_normed)
    layer_grads = (
        grad_inner_weight.reshape(grad_inner_weight.shape[0], 2, local_width),
        grad_rate_weight,
        grad_state_weight,
        grad_out_weight,
        grad_norm_gain,
        grad_conv_weight[:, :local_width],
        grad_conv_bias[:local_width],
        grad_conv_state,
        grad_bias_state,
        grad_rate_bias,
        grad_decay_log,
        grad_skip_gain,
        grad_gate_gain,
    )
    return (grad_hidden + grad_hidden_norm, layer_grads)


def stack_layers(layer_sums, position):
    return jnp.stack([grads_here[position] for grads_here in layer_sums])


def span_body(
    tokens,
    cotangent,
    norm_gain,
    inner_weight,
    rate_weight,
    state_weight,
    conv_inner,
    bias_inner,
    conv_state,
    bias_state,
    rate_bias,
    decay_log,
    skip_gain,
    gate_gain,
    out_weight,
):
    small_params = (
        norm_gain,
        conv_inner,
        bias_inner,
        conv_state,
        bias_state,
        rate_bias,
        decay_log,
        skip_gain,
        gate_gain,
    )
    layer_count = norm_gain.shape[0]
    batch_count = tokens.shape[0]
    results = []
    kept_batches = []
    for batch_index in range(batch_count):
        hidden = tokens[batch_index, 0].astype(jnp.float32)
        kept_layers = []
        for layer_index in range(layer_count):
            weights = gather_layer(inner_weight, rate_weight, state_weight, out_weight, layer_index)
            hidden, kept_values = forward_layer(hidden, weights, small_params, layer_index)
            kept_layers.append(kept_values)
        results.append(hidden)
        kept_batches.append(kept_layers)
    layer_sums = [None] * layer_count
    seq_grads = []
    for batch_index in range(batch_count):
        grad_hidden = cotangent[batch_index, 0].astype(jnp.float32)
        for layer_index in reversed(range(layer_count)):
            weights = gather_layer(inner_weight, rate_weight, state_weight, out_weight, layer_index)
            grad_hidden, layer_grads = backward_layer(
                grad_hidden,
                weights,
                small_params,
                kept_batches[batch_index][layer_index],
                layer_index,
            )
            if layer_sums[layer_index] is None:
                layer_sums[layer_index] = layer_grads
            else:
                layer_sums[layer_index] = tuple(
                    (older + newer for older, newer in zip(layer_sums[layer_index], layer_grads))
                )
        seq_grads.append(grad_hidden)
    shard_inner, shard_rate, shard_out = (
        lax.psum_scatter(
            stack_layers(layer_sums, 0), ("dp", "seq"), scatter_dimension=1, tiled=True
        ),
        lax.psum_scatter(
            stack_layers(layer_sums, 1), ("dp", "seq"), scatter_dimension=1, tiled=True
        ),
        lax.psum_scatter(
            stack_layers(layer_sums, 3), ("dp", "seq"), scatter_dimension=2, tiled=True
        ),
    )
    shard_state = lax.psum_scatter(
        stack_layers(layer_sums, 2), ("dp", "seq", "tensor"), scatter_dimension=1, tiled=True
    )
    summed_small = lax.psum(
        (
            stack_layers(layer_sums, 4),
            stack_layers(layer_sums, 5),
            stack_layers(layer_sums, 6),
            stack_layers(layer_sums, 7),
            stack_layers(layer_sums, 8),
            stack_layers(layer_sums, 9),
            stack_layers(layer_sums, 10),
            stack_layers(layer_sums, 11),
            stack_layers(layer_sums, 12),
        ),
        ("dp", "seq"),
    )
    output = jnp.stack(results)[:, None]
    input_grad = jnp.stack(seq_grads)[:, None]
    return (
        output,
        input_grad,
        summed_small[0],
        shard_inner,
        shard_rate,
        shard_state,
        summed_small[1],
        summed_small[2],
        summed_small[3],
        summed_small[4],
        summed_small[5],
        summed_small[6],
        summed_small[7],
        summed_small[8],
        shard_out,
    )


GROUP = ("seq", "tensor")
LANES = 128
ROWS = 8
BF16, F32 = jnp.bfloat16, jnp.float32


def hop(value, first, second):
    pairs = [
        (place * 2 + core, (place ^ (second if core else first)) * 2 + core)
        for place in range(4)
        for core in range(2)
    ]
    return lax.ppermute(value, GROUP, pairs)


def swap(value):
    return lax.ppermute(value, "tensor", [(0, 1), (1, 0)])


def places():
    place, core = lax.axis_index("seq"), lax.axis_index("tensor")
    return place, core, place ^ (1 + core), place ^ (2 - core), place ^ 3


def put(buffer, block, *index):
    spots = index + (0,) * (buffer.ndim - len(index))
    return lax.dynamic_update_slice(buffer, block.reshape((1,) * len(index) + block.shape), spots)


def pick(array, index, axis=0):
    return lax.dynamic_index_in_dim(array, index, axis, False)


def group_gather(block):
    place, core, near, far, across = places()
    from_near, from_far = hop(block, 1, 2), hop(block, 2, 1)
    from_across = hop(from_near, 2, 1)
    out = jnp.zeros((4, 2) + block.shape, block.dtype)
    for piece, own, other in (
        (block, place, place),
        (from_near, near, far),
        (from_far, far, near),
        (from_across, across, across),
    ):
        out = put(out, piece, own, core)
        out = put(out, swap(piece), other, 1 - core)
    return out


def group_scatter(parts):
    place, core, near, far, across = places()
    arrived = swap(pick(parts, 1 - core, 1))
    own = pick(parts, core, 1)

    def both(index):
        return pick(own, index).astype(F32) + pick(arrived, index).astype(F32)

    side = both(near) + hop(both(across).astype(BF16), 2, 1).astype(F32)
    here = both(place) + hop(both(far).astype(BF16), 2, 1).astype(F32)
    return here + hop(side.astype(BF16), 1, 2).astype(F32)


def group_sum(value):
    for first, second in ((1, 2), (2, 1)):
        value = value + hop(value, first, second)
    return value + swap(value)


def line_shift(value, axis, step):
    count = lax.axis_size(axis)
    return lax.ppermute(value, axis, [(i, (i + step) % count) for i in range(count)])


def line_gather(block):
    count, place = lax.axis_size("dp"), lax.axis_index("dp")
    out = put(jnp.zeros((count,) + block.shape, block.dtype), block, place)
    for step in range(1, count):
        out = put(out, line_shift(block, "dp", step), (place - step) % count)
    return out


def line_scatter(parts):
    count, place = lax.axis_size("dp"), lax.axis_index("dp")
    total = pick(parts, place)
    for step in range(1, count):
        sent = pick(parts, (place + step) % count).astype(BF16)
        total = total + line_shift(sent, "dp", step).astype(F32)
    return total


def seq_trade(parts):
    place = lax.axis_index("seq")
    out = put(jnp.zeros_like(parts), pick(parts, place), place)
    for turn in (1, 2, 3):
        got = lax.ppermute(pick(parts, place ^ turn), "seq", [(i, i ^ turn) for i in range(4)])
        out = put(out, got, place ^ turn)
    return out


def mesh_sum(value):
    for turn in (1, 2):
        value = value + lax.ppermute(value, "seq", [(i, i ^ turn) for i in range(4)])
    count = lax.axis_size("dp")
    if count & (count - 1):
        return lax.psum(value, "dp")
    turn = 1
    while turn < count:
        value = value + lax.ppermute(value, "dp", [(i, i ^ turn) for i in range(count)])
        turn *= 2
    return value


def dot(left, right, left_dim=1, right_dim=0):
    return lax.dot_general(
        left, right, (((left_dim,), (right_dim,)), ((), ())), preferred_element_type=F32
    )


def split(value, count):
    pieces = []
    for _ in range(count):
        piece = value.astype(BF16)
        pieces.append(piece)
        value = value - piece.astype(F32)
    return pieces


def exact_left(value, ones, count, right_dim=0):
    rows = value.shape[0]
    stacked = dot(jnp.concatenate(split(value, count), axis=0), ones, 1, right_dim)
    total = stacked[:rows]
    for index in range(1, count):
        total = total + stacked[index * rows : (index + 1) * rows]
    return total


def head_sums(picker, value):
    high, low_part = split(value, 2)
    return dot(picker, high, 1, 1) + dot(picker, low_part, 1, 1)


def front(raw, window, taps, heads, spread, upper, width, state, extra):
    length = raw.shape[0]
    summed = taps[4:5, :] + taps[0:1, :] * window[5 : 5 + length, :]
    for tap in range(1, 4):
        summed = summed + taps[tap : tap + 1, :] * window[5 + tap : 5 + tap + length, :]
    sig = jax.nn.sigmoid(summed)
    activated = summed * sig
    rates = jnp.transpose(raw[:, 2 * width + 2 * state :])[:ROWS] + heads[0:ROWS, :]
    steps = jnp.maximum(rates, 0.0) + jnp.log1p(jnp.exp(-jnp.abs(rates)))
    decays = -jnp.exp(heads[ROWS : 2 * ROWS, :]) * steps
    running = exact_left(decays, upper, 3)
    ending = running[:, length - 1 : length]
    grown = jnp.exp(running)
    tail = jnp.exp(ending - running)
    rows = [steps, running, grown, tail] + extra
    rows.append(jnp.zeros((length - ROWS * len(rows), length), F32))
    columns = jnp.transpose(jnp.concatenate(rows, axis=0))
    high, low_part = split(columns, 2)
    wide = dot(high, spread) + dot(low_part, spread)
    whole_decay = jnp.exp(jnp.broadcast_to(ending, (ROWS, LANES)))
    inputs = activated[:, :width]
    return dict(
        summed=summed,
        sig=sig,
        inputs=inputs,
        keys=activated[:, width : width + state].astype(BF16),
        queries=activated[:, width + state :].astype(BF16),
        rates=rates,
        decays=decays,
        running=running,
        columns=columns,
        steps_wide=wide[:, :width],
        grown_wide=wide[:, width : 2 * width],
        tail_wide=wide[:, 2 * width : 3 * width],
        whole_decay=whole_decay,
    )


def per_row(whole_decay, head_count, head_size):
    return jnp.concatenate(
        [
            jnp.broadcast_to(whole_decay[h : h + 1, :], (head_size, LANES))
            for h in range(head_count)
        ],
        axis=0,
    )


def decay_matrix(parts, h, causal):
    length = causal.shape[0]
    column = parts["columns"][:, ROWS + h : ROWS + h + 1]
    row = parts["running"][h : h + 1, :]
    gap = jnp.broadcast_to(column, (length, length)) - row
    return jnp.exp(jnp.where(causal, gap, -1e30))


def causal_mask(length):
    return lax.broadcasted_iota(jnp.int32, (length, length), 0) >= lax.broadcasted_iota(
        jnp.int32, (length, length), 1
    )


def forward_kernel(
    head_size,
    raw_ref,
    taps_ref,
    chans_ref,
    heads_ref,
    spread_ref,
    upper_ref,
    value_ref,
    square_ref,
    mixed_ref,
    state_ref,
    carry,
    window,
):
    length, width, state = raw_ref.shape[0], chans_ref.shape[1], carry.shape[1]
    conv_width = width + 2 * state
    head_count = width // head_size
    pair = LANES // head_size

    @pl.when(pl.program_id(0) == 0)
    def _():
        carry[...] = jnp.zeros_like(carry)
        window[0:ROWS, :] = jnp.zeros((ROWS, conv_width), F32)

    raw = raw_ref[...]
    window[ROWS : ROWS + length, :] = raw[:, width : width + conv_width].astype(BF16).astype(F32)
    parts = front(
        raw,
        window,
        taps_ref[...],
        heads_ref[...],
        spread_ref[...],
        upper_ref[...],
        width,
        state,
        [],
    )
    window[0:ROWS, :] = window[length : length + ROWS, :]
    inputs, keys, queries = parts["inputs"], parts["keys"], parts["queries"]
    before = carry[...]
    state_ref[...] = before
    stepped = inputs * parts["steps_wide"]
    stepped_low = stepped.astype(BF16)
    scores = dot(queries, keys, 1, 1)
    causal = causal_mask(length)
    lane = lax.broadcasted_iota(jnp.int32, (length, LANES), 1) // head_size
    columns = []
    for block in range(head_count // pair):
        source = stepped_low[:, block * LANES : (block + 1) * LANES]
        joined = None
        for k in range(pair):
            mixing = (scores * decay_matrix(parts, block * pair + k, causal)).astype(BF16)
            got = dot(mixing, source)
            joined = got if joined is None else jnp.where(lane == k, got, joined)
        columns.append(joined)
    carried = dot(queries, before.astype(BF16), 1, 1)
    mixed = (
        jnp.concatenate(columns, axis=1)
        + carried * parts["grown_wide"]
        + chans_ref[0:1, :] * inputs
    )
    update = dot((stepped * parts["tail_wide"]).astype(BF16), keys, 0, 0)
    carry[...] = per_row(parts["whole_decay"], head_count, head_size) * before + update
    gate = raw[:, :width]
    gated = mixed * (gate * jax.nn.sigmoid(gate))
    mixed_ref[...] = mixed
    value_ref[...] = (gated * chans_ref[1:2, :]).astype(BF16)
    squares = jnp.sum(gated * gated, axis=1, keepdims=True)
    square_ref[...] = jnp.transpose(jnp.broadcast_to(squares, (length, length)))[:ROWS]


def backward_kernel(
    head_size,
    inner_count,
    grad_ref,
    raw_ref,
    past_ref,
    mixed_ref,
    state_ref,
    token_ref,
    taps_ref,
    chans_ref,
    heads_ref,
    spread_ref,
    upper_ref,
    picker_ref,
    back_ref,
    normed_ref,
    taps_out,
    chans_out,
    heads_out,
    carry,
    window,
    later,
):
    length, width, state = raw_ref.shape[0], chans_ref.shape[1], carry.shape[1]
    conv_width = width + 2 * state
    head_count = width // head_size
    pair = LANES // head_size
    step, count = pl.program_id(0), pl.num_programs(0)

    @pl.when(step == 0)
    def _():
        carry[...] = jnp.zeros_like(carry)
        later[length : length + ROWS, :] = jnp.zeros((ROWS, conv_width), F32)
        taps_out[...] = jnp.zeros_like(taps_out)
        chans_out[...] = jnp.zeros_like(chans_out)
        heads_out[...] = jnp.zeros_like(heads_out)

    raw = raw_ref[...]
    past = past_ref[:, width : width + conv_width].astype(BF16).astype(F32)
    window[0:ROWS, :] = jnp.where(step == count - 1, 0.0, past)
    window[ROWS : ROWS + length, :] = raw[:, width : width + conv_width].astype(BF16).astype(F32)
    taps, heads, picker = taps_ref[...], heads_ref[...], picker_ref[...]
    parts = front(
        raw, window, taps, heads, spread_ref[...], upper_ref[...], width, state, [token_ref[...]]
    )
    inputs, keys, queries = parts["inputs"], parts["keys"], parts["queries"]
    skip, gain = chans_ref[0:1, :], chans_ref[1:2, :]
    scale = parts["columns"][:, 4 * ROWS : 4 * ROWS + 1]
    inner = parts["columns"][:, 4 * ROWS + 1 : 4 * ROWS + 2]

    gate, mixed = raw[:, :width], mixed_ref[...]
    gate_sig = jax.nn.sigmoid(gate)
    gate_silu = gate * gate_sig
    gated = mixed * gate_silu
    grad = grad_ref[...]
    scaled_gated = gated * scale
    normed_ref[...] = (scaled_gated * gain).astype(BF16)
    gain_term = jnp.sum(grad * scaled_gated, axis=0, keepdims=True)
    grad_gated = scale * (grad * gain) - gated * (scale * scale * scale * inner / inner_count)
    grad_mixed = grad_gated * gate_silu
    back_ref[:, :width] = (
        grad_gated * mixed * (gate_sig + gate_silu * (1.0 - gate_sig))
    ).astype(BF16)
    skip_term = jnp.sum(grad_mixed * inputs, axis=0, keepdims=True)
    chans_out[0:1, :] += skip_term
    chans_out[1:2, :] += gain_term

    stepped = inputs * parts["steps_wide"]
    stepped_low, grad_low = stepped.astype(BF16), grad_mixed.astype(BF16)
    scores = dot(queries, keys, 1, 1)
    causal = causal_mask(length)
    lane = lax.broadcasted_iota(jnp.int32, (length, LANES), 1)
    head_lane = lane // head_size
    grad_scores = jnp.zeros((length, length), F32)
    row_sums = jnp.zeros((length, length), F32)
    column_sums, columns = [], []
    for block in range(head_count // pair):
        cut = slice(block * LANES, (block + 1) * LANES)
        source, target = stepped_low[:, cut], grad_low[:, cut]
        joined = None
        for k in range(pair):
            h = block * pair + k
            spread_h = decay_matrix(parts, h, causal)
            own_target = jnp.where(head_lane == k, target, jnp.zeros_like(target))
            pulled = dot(own_target, source, 1, 1) * spread_h
            grad_scores = grad_scores + pulled
            moved = pulled * scores
            row_sums = jnp.where(lane == h, jnp.sum(moved, axis=1, keepdims=True), row_sums)
            column_sums.append(jnp.sum(moved, axis=0, keepdims=True))
            got = dot((scores * spread_h).astype(BF16), target, 0, 0)
            joined = got if joined is None else jnp.where(head_lane == k, got, joined)
        columns.append(joined)
    before, after = state_ref[...], carry[...]
    before_low, after_low = before.astype(BF16), after.astype(BF16)
    tail_wide, grown_wide = parts["tail_wide"], parts["grown_wide"]
    through = tail_wide * dot(keys, after_low, 1, 1)
    grad_stepped = jnp.concatenate(columns, axis=1) + through
    ended = stepped * through
    carried = dot(queries, before_low, 1, 1) * grown_wide
    whole_rows = per_row(parts["whole_decay"], head_count, head_size)
    kept = whole_rows * after
    held = jnp.sum(kept * before, axis=1, keepdims=True)
    spare = jnp.zeros((ROWS - head_count, 1), F32)
    held_heads = jnp.concatenate(
        [
            jnp.sum(held[h * head_size : (h + 1) * head_size], axis=0, keepdims=True)
            for h in range(head_count)
        ]
        + [spare],
        axis=0,
    )
    ended_heads = head_sums(picker, ended)
    grad_running = (
        jnp.transpose(row_sums)[:ROWS]
        - jnp.concatenate(column_sums + [jnp.zeros((ROWS - head_count, length), F32)], axis=0)
        + head_sums(picker, grad_mixed * carried)
        - ended_heads
    )
    last = jnp.sum(ended_heads, axis=1, keepdims=True) + held_heads
    row_lane = lax.broadcasted_iota(jnp.int32, (ROWS, length), 1)
    grad_running = grad_running + jnp.where(row_lane == length - 1, last, 0.0)
    grad_decays = exact_left(grad_running, upper_ref[...], 3, 1)
    grad_steps = head_sums(picker, inputs * grad_stepped)
    grad_rates = (
        grad_steps - jnp.exp(heads[ROWS : 2 * ROWS, :]) * grad_decays
    ) * jax.nn.sigmoid(parts["rates"])
    row_head = lax.broadcasted_iota(jnp.int32, (ROWS, length), 0)
    grad_rates = jnp.where(row_head < head_count, grad_rates, 0.0)
    heads_out[0:ROWS, :] += grad_rates
    heads_out[ROWS : 2 * ROWS, :] += grad_decays * parts["decays"]
    back_ref[:, 2 * width + 2 * state :] = jnp.transpose(
        jnp.concatenate([grad_rates, jnp.zeros((LANES - ROWS, length), F32)], axis=0)
    ).astype(BF16)

    grad_inputs = parts["steps_wide"] * grad_stepped + skip * grad_mixed
    grown_low = (grown_wide * grad_mixed).astype(BF16)
    scores_low = grad_scores.astype(BF16)
    grad_queries = dot(scores_low, keys) + dot(grown_low, before_low)
    grad_keys = dot(scores_low, queries, 0, 0) + dot(
        (stepped * tail_wide).astype(BF16), after_low
    )
    carry[...] = kept + dot(grown_low, queries, 0, 0)

    sig, summed = parts["sig"], parts["summed"]
    grad_v = jnp.concatenate([grad_inputs, grad_keys, grad_queries], axis=1) * (
        sig + summed * sig * (1.0 - sig)
    )
    later[0:length, :] = grad_v
    grad_conv = taps[3:4, :] * grad_v
    taps_out[4:5, :] += jnp.sum(grad_v, axis=0, keepdims=True)
    for tap in range(4):
        if tap < 3:
            grad_conv = grad_conv + taps[tap : tap + 1, :] * later[3 - tap : 3 - tap + length, :]
        taps_out[tap : tap + 1, :] += jnp.sum(
            grad_v * window[5 + tap : 5 + tap + length, :], axis=0, keepdims=True
        )
    later[length : length + ROWS, :] = grad_v[0:ROWS]
    back_ref[:, width : width + conv_width] = grad_conv.astype(BF16)


def tables(width, head_size):
    channel_head = jnp.arange(width)[None, :] // head_size
    rows = jnp.arange(LANES)[:, None]
    spread = jnp.concatenate(
        [rows == channel_head + ROWS * kind for kind in (0, 2, 3)], axis=1
    ).astype(BF16)
    upper = (rows <= jnp.arange(LANES)[None, :]).astype(BF16)
    picker = (jnp.arange(ROWS)[:, None] == channel_head).astype(BF16)
    return spread, upper, picker


def fixed(shape):
    return pl.BlockSpec(shape, lambda i: (0,) * len(shape))


def mix_forward(raw, small, tabs, head_size, width, state):
    taps, chans, heads = small
    spread, upper, _ = tabs
    tokens, columns = raw.shape
    count = tokens // STRETCH
    return pl.pallas_call(
        lambda *refs: forward_kernel(head_size, *refs),
        grid=(count,),
        in_specs=[
            pl.BlockSpec((STRETCH, columns), lambda i: (i, 0)),
            fixed(taps.shape),
            fixed(chans.shape),
            fixed(heads.shape),
            fixed(spread.shape),
            fixed(upper.shape),
        ],
        out_specs=[
            pl.BlockSpec((STRETCH, width), lambda i: (i, 0)),
            pl.BlockSpec((ROWS, LANES), lambda i: (i, 0)),
            pl.BlockSpec((STRETCH, width), lambda i: (i, 0)),
            pl.BlockSpec((None, width, state), lambda i: (i, 0, 0)),
        ],
        out_shape=[
            jax.ShapeDtypeStruct((tokens, width), BF16),
            jax.ShapeDtypeStruct((count * ROWS, LANES), F32),
            jax.ShapeDtypeStruct((tokens, width), F32),
            jax.ShapeDtypeStruct((count, width, state), F32),
        ],
        scratch_shapes=[
            pltpu.VMEM((width, state), F32),
            pltpu.VMEM((STRETCH + ROWS, width + 2 * state), F32),
        ],
        compiler_params=pltpu.CompilerParams(
            dimension_semantics=("arbitrary",), vmem_limit_bytes=40 * 2**20
        ),
        cost_estimate=pl.CostEstimate(
            flops=15_000_000_000, bytes_accessed=10_000_000, transcendentals=0
        ),
    )(raw, taps, chans, heads, spread, upper)


def mix_backward(grad, raw, mixed, states, token_rows, small, tabs, head_size, inner_count):
    taps, chans, heads = small
    spread, upper, picker = tabs
    tokens, columns = raw.shape
    width, state = states.shape[1:]
    count = tokens // STRETCH
    per = STRETCH // ROWS

    def back(i):
        return (count - 1 - i, 0)

    return pl.pallas_call(
        lambda *refs: backward_kernel(head_size, inner_count, *refs),
        grid=(count,),
        in_specs=[
            pl.BlockSpec((STRETCH, width), back),
            pl.BlockSpec((STRETCH, columns), back),
            pl.BlockSpec((ROWS, columns), lambda i: (jnp.maximum((count - 1 - i) * per - 1, 0), 0)),
            pl.BlockSpec((STRETCH, width), back),
            pl.BlockSpec((None, width, state), lambda i: (count - 1 - i, 0, 0)),
            pl.BlockSpec((ROWS, LANES), back),
            fixed(taps.shape),
            fixed(chans.shape),
            fixed(heads.shape),
            fixed(spread.shape),
            fixed(upper.shape),
            fixed(picker.shape),
        ],
        out_specs=[
            pl.BlockSpec((STRETCH, columns), back),
            pl.BlockSpec((STRETCH, width), back),
            fixed(taps.shape),
            fixed(chans.shape),
            fixed(heads.shape),
        ],
        out_shape=[
            jax.ShapeDtypeStruct((tokens, columns), BF16),
            jax.ShapeDtypeStruct((tokens, width), BF16),
            jax.ShapeDtypeStruct(taps.shape, F32),
            jax.ShapeDtypeStruct(chans.shape, F32),
            jax.ShapeDtypeStruct(heads.shape, F32),
        ],
        scratch_shapes=[
            pltpu.VMEM((width, state), F32),
            pltpu.VMEM((STRETCH + ROWS, width + 2 * state), F32),
            pltpu.VMEM((STRETCH + ROWS, width + 2 * state), F32),
        ],
        compiler_params=pltpu.CompilerParams(
            dimension_semantics=("arbitrary",), vmem_limit_bytes=40 * 2**20
        ),
        cost_estimate=pl.CostEstimate(
            flops=30_000_000_000, bytes_accessed=16_000_000, transcendentals=0
        ),
    )(grad, raw, raw, mixed, states, token_rows, taps, chans, heads, spread, upper, picker)


def norm_scale(hidden):
    return lax.rsqrt(jnp.mean(hidden * hidden, axis=1, keepdims=True) + EPSILON)


def head_body(
    tokens,
    cotangent,
    norm_gain,
    inner_weight,
    rate_weight,
    state_weight,
    conv_inner,
    bias_inner,
    conv_state,
    bias_state,
    rate_bias,
    decay_log,
    skip_gain,
    gate_gain,
    out_weight,
):
    layers, batches = norm_gain.shape[0], tokens.shape[0]
    model = tokens.shape[3]
    place, core = lax.axis_index("seq"), lax.axis_index("tensor")
    line = lax.axis_size("dp")
    share, half_width = inner_weight.shape[1], inner_weight.shape[3]
    inner_count = half_width * 2
    width = half_width // 4
    head_count = rate_bias.shape[1] // 4
    head_size = width // head_count
    state_share, state = state_weight.shape[1], state_weight.shape[2] // 2
    own_rows = tokens.shape[2] // 2
    length = own_rows * 8
    conv_width = width + 2 * state
    columns = 2 * width + 2 * state + LANES
    tabs = tables(width, head_size)

    def out_share(layer):
        turned = out_weight[layer].T.reshape(share, 4, width)
        return turned.transpose(1, 0, 2)

    def inner_share(layer):
        cut = inner_weight[layer].reshape(share, 2, 4, width)
        return cut.transpose(2, 0, 1, 3).reshape(4, share, 2 * width)

    def whole(parts):
        traded = seq_trade(parts)
        return line_gather(traded.reshape(4 * share, -1)).reshape(line * 4 * share, -1)

    heads_here = rate_weight.shape[2]
    rate_flat = rate_weight.reshape(layers, state_share, -1)
    rate_flat = jnp.pad(rate_flat, ((0, 0), (0, 0), (0, LANES - rate_flat.shape[2])))
    small_share = jnp.concatenate([state_weight, rate_flat], axis=2)
    small_line = line_gather(small_share.reshape(layers * state_share, -1))
    small_all = group_gather(small_line.reshape(line * layers * state_share, -1))
    small_all = small_all.reshape(4, 2, line, layers, state_share, -1)
    state_full = small_all[..., : 2 * state].transpose(3, 2, 0, 1, 4, 5).reshape(layers, model, -1)
    rate_half = pick(small_all, core, 1)[..., 2 * state : 2 * state + 2 * heads_here]
    rate_half = rate_half.reshape(4, line, layers, share, heads_here)
    rate_own = lax.dynamic_slice_in_dim(rate_half, place * head_count, head_count, 4)
    rate_own = rate_own.transpose(2, 1, 0, 3, 4).reshape(layers, model, head_count)
    rate_own = jnp.pad(rate_own, ((0, 0), (0, 0), (0, LANES - head_count)))

    in_weights, out_weights = [], []
    for layer in range(layers):
        inner_full = whole(inner_share(layer))
        in_weights.append(
            jnp.concatenate([inner_full, state_full[layer], rate_own[layer]], axis=1)
        )
        out_weights.append(whole(out_share(layer)))

    def quarter(array, count):
        return lax.dynamic_slice_in_dim(array, place * count, count, array.ndim - 1)

    smalls = []
    for layer in range(layers):
        taps = jnp.concatenate([quarter(conv_inner[layer], width), conv_state[layer]], axis=1)
        bias = jnp.concatenate([quarter(bias_inner[layer], width), bias_state[layer]])
        taps = jnp.concatenate([taps, bias[None], jnp.zeros((3, conv_width), F32)], axis=0)
        skip = jnp.repeat(quarter(skip_gain[layer], head_count), head_size)
        chans = jnp.stack([skip, quarter(gate_gain[layer], width)])
        chans = jnp.concatenate([chans, jnp.zeros((ROWS - 2, width), F32)], axis=0)
        heads = jnp.stack([quarter(rate_bias[layer], head_count), quarter(decay_log[layer], head_count)])
        heads = jnp.pad(heads, ((0, 0), (0, ROWS - head_count))).reshape(2 * ROWS, 1)
        smalls.append((taps, chans, jnp.broadcast_to(heads, (2 * ROWS, LANES))))

    def own(array):
        return lax.dynamic_slice_in_dim(array, core * own_rows, own_rows, 0)

    results, kept = [], [[None] * layers for _ in range(batches)]
    hiddens = [own(tokens[batch, 0]).astype(F32) for batch in range(batches)]
    for layer in range(layers):
        for batch in range(batches):
            hidden = hiddens[batch]
            row_scale = norm_scale(hidden)
            normed_own = (hidden * row_scale * norm_gain[layer][None, :]).astype(BF16)
            normed = group_gather(normed_own).reshape(length, model)
            raw = dot(normed, in_weights[layer])
            value, squares, mixed, states = mix_forward(
                raw, smalls[layer], tabs, head_size, width, state
            )
            partial = dot(value, out_weights[layer], 1, 1).astype(BF16)
            summed = group_scatter(partial.reshape(4, 2, own_rows, model))
            squares = group_sum(squares.reshape(-1, ROWS, LANES)[:, 0])
            scales = lax.rsqrt(squares / inner_count + EPSILON)
            own_scale = pick(scales.reshape(8, own_rows), place * 2 + core)[:, None]
            kept[batch][layer] = (hidden, row_scale, normed, raw, mixed, states, summed, scales)
            hiddens[batch] = hidden + own_scale * summed
    results = hiddens

    grads = [own(cotangent[batch, 0]).astype(F32) for batch in range(batches)]
    big, small_sums = [None] * layers, [None] * layers
    for layer in reversed(range(layers)):
        sums = None
        for batch in range(batches):
            hidden, row_scale, normed, raw, mixed, states, summed, scales = kept[batch][layer]
            grad_hidden = grads[batch]
            grad_low = grad_hidden.astype(BF16)
            inner_own = jnp.sum(grad_low.astype(F32) * summed, axis=1)
            inner = jnp.zeros((8, own_rows), F32)
            inner = put(inner, inner_own, place * 2 + core)
            inner = group_sum(inner).reshape(-1, LANES)
            token_rows = jnp.stack([scales, inner], axis=1)
            token_rows = jnp.pad(token_rows, ((0, 0), (0, ROWS - 2), (0, 0)))
            grad_all = group_gather(grad_low).reshape(length, model)
            grad_value = dot(grad_all, out_weights[layer])
            back, normed_out, taps_grad, chans_grad, heads_grad = mix_backward(
                grad_value,
                raw,
                mixed,
                states,
                token_rows.reshape(-1, LANES),
                smalls[layer],
                tabs,
                head_size,
                inner_count,
            )
            partial = dot(back, in_weights[layer], 1, 1).astype(BF16)
            grad_normed = group_scatter(partial.reshape(4, 2, own_rows, model))
            gain_term = jnp.sum(grad_normed * hidden * row_scale, axis=0)
            weighted = grad_normed * norm_gain[layer][None, :]
            mean = jnp.mean(weighted * hidden, axis=1, keepdims=True)
            grads[batch] = (
                grad_hidden
                + row_scale * weighted
                - hidden * (row_scale * row_scale * row_scale) * mean
            )
            out_term = dot(grad_all, normed_out, 0, 0)
            in_term = dot(normed, back, 0, 0)
            new = (in_term, out_term, taps_grad, chans_grad, heads_grad, gain_term)
            sums = new if sums is None else tuple(a + b for a, b in zip(sums, new))
        big[layer] = sums[:2]
        small_sums[layer] = sums[2:]

    def traded(total, cut):
        return seq_trade(total[:, :cut].reshape(4, share, cut).astype(BF16)).astype(F32)

    inner_grads, rate_grads, state_grads, out_grads = [], [], [], []
    for layer in range(layers):
        in_sum, out_sum = big[layer]
        out_total = line_scatter(out_sum.reshape(line, 4 * share, width))
        out_here = traded(out_total, width)
        out_grads.append(out_here.transpose(1, 0, 2).reshape(share, half_width).T)
        states_part = in_sum[:, 2 * width : 2 * width + 2 * state]
        states_part = states_part.reshape(line * 4, 2, state_share, 2 * state)
        sent = swap(pick(states_part, 1 - core, 1).astype(BF16))
        states_part = pick(states_part, core, 1) + sent.astype(F32)
        states_part = states_part.reshape(line, 4 * share, state)
        in_part = in_sum.reshape(line, 4 * share, columns)
        packed = jnp.concatenate(
            [in_part[..., : 2 * width], states_part, in_part[..., 2 * width + 2 * state :]], axis=2
        )
        total = line_scatter(packed)
        here = traded(total, total.shape[1])
        inner_here = here[..., : 2 * width].reshape(4, share, 2, width)
        inner_grads.append(inner_here.transpose(1, 2, 0, 3).reshape(share, 2, half_width))
        state_grads.append(
            jnp.sum(here[..., 2 * width : 2 * width + state], axis=0).reshape(state_share, 2 * state)
        )
        rate_here = here[..., 2 * width + state : 2 * width + state + head_count]
        rate_grads.append(rate_here.transpose(1, 0, 2).reshape(share, heads_here))

    def slot(array, count):
        shape = array.shape[:-1] + (4 * count,)
        spots = (0,) * (array.ndim - 1) + (place * count,)
        return lax.dynamic_update_slice(jnp.zeros(shape, F32), array, spots)

    pieces = []
    for layer in range(layers):
        taps_grad, chans_grad, heads_grad, gain_term = small_sums[layer]
        both = jnp.concatenate([gain_term, taps_grad[:5, width:].reshape(-1)])
        both = both + swap(both)
        head_rows = jnp.stack(
            [
                jnp.sum(heads_grad[:ROWS], axis=1)[:head_count],
                jnp.sum(heads_grad[ROWS:], axis=1)[:head_count],
                jnp.sum(chans_grad[0].reshape(head_count, head_size), axis=1),
            ]
        )
        pieces += [
            both,
            slot(taps_grad[:5, :width], width).reshape(-1),
            slot(chans_grad[1], width),
            slot(head_rows, head_count).reshape(-1),
        ]
    flat = jnp.concatenate(pieces)
    spill = -flat.shape[0] % (ROWS * LANES)
    flat = mesh_sum(jnp.pad(flat, (0, spill)).reshape(-1, LANES)).reshape(-1)
    taken, small_out = 0, []
    for layer in range(layers):
        found = []
        for shape in (
            (model,),
            (5, 2 * state),
            (5, half_width),
            (half_width,),
            (3, 4 * head_count),
        ):
            size = 1
            for extent in shape:
                size *= extent
            found.append(flat[taken : taken + size].reshape(shape))
            taken += size
        small_out.append(found)

    def spread_out(batched):
        both = []
        for value in batched:
            other = swap(value)
            first = jnp.where(core == 0, value, other)
            second = jnp.where(core == 0, other, value)
            both.append(jnp.concatenate([first, second], axis=0))
        return jnp.stack(both)[:, None]

    def stacked(position, cut=lambda value: value):
        return jnp.stack([cut(found[position]) for found in small_out])

    return (
        spread_out(results),
        spread_out(grads),
        stacked(0),
        jnp.stack(inner_grads),
        jnp.stack(rate_grads),
        jnp.stack(state_grads),
        stacked(2, lambda value: value[:4]),
        stacked(2, lambda value: value[4]),
        stacked(1, lambda value: value[:4]),
        stacked(1, lambda value: value[4]),
        stacked(4, lambda value: value[0]),
        stacked(4, lambda value: value[1]),
        stacked(4, lambda value: value[2]),
        stacked(3),
        jnp.stack(out_grads),
    )


def by_heads(mesh, tokens, inner_weight, rate_bias, conv_state, state_weight):
    place_count, core_count, line = mesh.shape["seq"], mesh.shape["tensor"], mesh.shape["dp"]
    if place_count != 4 or core_count != 2:
        return False
    heads, inner = rate_bias.shape[1], inner_weight.shape[3]
    rows = tokens.shape[2] // 8
    return (
        tokens.shape[1] == line
        and tokens.shape[2] % 8 == 0
        and rows == STRETCH
        and heads % 8 == 0
        and heads // 8 <= ROWS
        and (inner // 8) % LANES == 0
        and LANES % (inner // heads) == 0
        and conv_state.shape[1] == 4
        and state_weight.shape[2] == 2 * LANES
        and inner_weight.shape[1] % (line * 4 * 32) == 0
    )


def solution(mesh):
    in_specs = (
        P(None, "dp", "seq", None),
        P(None, "dp", "seq", None),
        P(),
        P(None, ("dp", "seq"), None, "tensor"),
        P(None, ("dp", "seq"), "tensor"),
        P(None, ("dp", "seq", "tensor"), None),
        P(None, None, "tensor"),
        P(None, "tensor"),
        P(),
        P(),
        P(None, "tensor"),
        P(None, "tensor"),
        P(None, "tensor"),
        P(None, "tensor"),
        P(None, "tensor", ("dp", "seq")),
    )
    out_specs = (
        P(None, "dp", "seq", None),
        P(None, "dp", "seq", None),
        P(),
        P(None, ("dp", "seq"), None, "tensor"),
        P(None, ("dp", "seq"), "tensor"),
        P(None, ("dp", "seq", "tensor"), None),
        P(None, None, "tensor"),
        P(None, "tensor"),
        P(),
        P(),
        P(None, "tensor"),
        P(None, "tensor"),
        P(None, "tensor"),
        P(None, "tensor"),
        P(None, "tensor", ("dp", "seq")),
    )
    def run(*arrays):
        by_name = (arrays[0], arrays[3], arrays[10], arrays[8], arrays[5])
        chosen = head_body if by_heads(mesh, *by_name) else span_body
        return jax.shard_map(
            chosen, mesh=mesh, in_specs=in_specs, out_specs=out_specs, check_vma=False
        )(*arrays)

    return run
```

```python
import jax
import jax.numpy as jnp
from jax import lax
from jax.experimental import pallas as pl
from jax.experimental.pallas import tpu as pltpu
from jax.sharding import PartitionSpec as P

DI = 3072
STRETCH = 128


EPSILON = 1e-05
HIGHEST = lax.Precision.HIGHEST


def shifted(value, axis, steps):
    count = lax.axis_size(axis)
    leading, last = (max(0, -steps), min(count, count - steps))
    return lax.ppermute(value, axis, [(source, source + steps) for source in range(leading, last)])


def carried_in(array, axis, combine, identity):
    length, place = (lax.axis_size(axis), lax.axis_index(axis))
    everything = jax.tree.map(
        lambda part, kind: lax.all_gather(part.astype(kind), axis),
        array,
        (jnp.bfloat16, jnp.bfloat16),
    )
    start = jax.tree.map(
        lambda part, zero: jnp.broadcast_to(jnp.asarray(zero, part.dtype), part.shape),
        array,
        identity,
    )

    def turn(k, before):
        reached = k < place
        new = combine(
            before, jax.tree.map(lambda part, own: part[k].astype(own.dtype), everything, array)
        )
        return jax.tree.map(lambda a, b: jnp.where(reached, a, b), new, before)

    return lax.fori_loop(0, length, turn, start)


def carried_in_2(array, axis, join, neutral):
    count = lax.axis_size(axis)
    place = lax.axis_index(axis)
    ahead = count - 1 - place
    gathered = jax.tree.map(
        lambda a, kind: lax.all_gather(a.astype(kind), axis),
        array,
        jax.tree.map(lambda a: jnp.bfloat16 if a.dtype == jnp.float32 else a.dtype, array),
    )
    state = jax.tree.map(lambda a, e: jnp.zeros_like(a) + jnp.asarray(e, a.dtype), array, neutral)

    def one(turn, state):
        source = count - 1 - turn
        return join(
            state,
            jax.tree.map(
                lambda a, own: lax.dynamic_index_in_dim(a, source, 0, False).astype(own.dtype),
                gathered,
                array,
            ),
        )

    return lax.fori_loop(0, ahead, one, state)


def product(left_side, right_side):
    return jnp.dot(left_side, right_side, precision=HIGHEST, preferred_element_type=jnp.float32)


def conv_silu(padded, weight, conv_bias):
    conv_width = weight.shape[0]
    out_rows = padded.shape[0] - conv_width + 1
    summed = conv_bias[None, :] + weight[0][None, :] * padded[0:out_rows]
    for offset in range(1, conv_width):
        summed = summed + weight[offset][None, :] * padded[offset : offset + out_rows]
    return jax.nn.silu(summed)


def block_step(carry_state, pieces):
    inputs, keys_b, queries_c, step_rates, decays = pieces
    running = jnp.cumsum(decays, axis=0)
    block_len = inputs.shape[0]
    causal = jnp.arange(block_len)[:, None] >= jnp.arange(block_len)[None, :]
    spread = running.T[:, :, None] - running.T[:, None, :]
    weights = jnp.exp(jnp.where(causal[None, :, :], spread, -jnp.inf))
    scores = product(queries_c, keys_b.T)
    mixing = scores[None, :, :] * weights * step_rates.T[:, None, :]
    inside = jnp.einsum("hts,shp->thp", mixing, inputs, precision=HIGHEST)
    carried = (
        jnp.einsum("tn,hpn->thp", queries_c, carry_state, precision=HIGHEST)
        * jnp.exp(running)[:, :, None]
    )
    tail_weight = jnp.exp(running[-1][None, :] - running) * step_rates
    update = jnp.einsum("shp,sn->hpn", tail_weight[:, :, None] * inputs, keys_b, precision=HIGHEST)
    return (jnp.exp(running[-1])[:, None, None] * carry_state + update, inside + carried)


def state_step(carry_state, pieces):
    inputs, keys_b, step_rates, decays = pieces
    running = jnp.cumsum(decays, axis=0)
    tail_weight = jnp.exp(running[-1][None, :] - running) * step_rates
    update = jnp.einsum("shp,sn->hpn", tail_weight[:, :, None] * inputs, keys_b, precision=HIGHEST)
    return (jnp.exp(running[-1])[:, None, None] * carry_state + update, None)


def to_blocks(values):
    return values.reshape((values.shape[0] // STRETCH, STRETCH) + values.shape[1:])


def span_summary(inputs, keys_b, step_rates, decays):
    zero_state = jnp.zeros((inputs.shape[1], inputs.shape[2], keys_b.shape[1]), jnp.float32)
    end_state, _ = lax.scan(
        state_step,
        zero_state,
        (to_blocks(inputs), to_blocks(keys_b), to_blocks(step_rates), to_blocks(decays)),
    )
    return (jnp.exp(jnp.sum(decays, axis=0)), end_state)


def span_output(inputs, keys_b, queries_c, step_rates, decays, entry_state, skip_gain):
    _, block_out = lax.scan(
        block_step,
        entry_state,
        (
            to_blocks(inputs),
            to_blocks(keys_b),
            to_blocks(queries_c),
            to_blocks(step_rates),
            to_blocks(decays),
        ),
    )
    mixed_out = block_out.reshape(inputs.shape) + skip_gain[None, :, None] * inputs
    return mixed_out.reshape(inputs.shape[0], -1)


def rate_piece(rate_raw, rate_bias, decay_log):
    step_rates = jax.nn.softplus(rate_raw + rate_bias[None, :])
    return (step_rates, -jnp.exp(decay_log)[None, :] * step_rates)


def norm_piece(hidden, norm_gain):
    row_scale = lax.rsqrt(jnp.mean(hidden * hidden, axis=1, keepdims=True) + EPSILON)
    return hidden * row_scale * norm_gain[None, :]


def chain_combine(earlier, following):
    return (earlier[0] * following[0], following[1] + following[0][:, None, None] * earlier[1])


def gather_layer(inner_weight, rate_weight, state_weight, out_weight, layer_index):
    inner_full, rate_full, out_full = (
        lax.all_gather(inner_weight[layer_index], ("dp", "seq"), axis=0, tiled=True),
        lax.all_gather(rate_weight[layer_index], ("dp", "seq"), axis=0, tiled=True),
        lax.all_gather(out_weight[layer_index], ("dp", "seq"), axis=1, tiled=True),
    )
    state_full = lax.all_gather(
        state_weight[layer_index], ("dp", "seq", "tensor"), axis=0, tiled=True
    )
    return (inner_full.reshape(inner_full.shape[0], -1), rate_full, state_full, out_full)


def forward_layer(hidden, weights, small_params, layer_index):
    inner_full, rate_full, state_full, out_full = weights
    (
        norm_gain,
        conv_inner,
        bias_inner,
        conv_state,
        bias_state,
        rate_bias,
        decay_log,
        skip_gain,
        gate_gain,
    ) = small_params
    seq_rows = hidden.shape[0]
    normed_full, norm_pull = jax.vjp(norm_piece, hidden, norm_gain[layer_index])
    normed = normed_full.astype(jnp.bfloat16)
    gate_inner = jnp.dot(normed, inner_full, preferred_element_type=jnp.float32)
    rate_raw = jnp.dot(normed, rate_full, preferred_element_type=jnp.float32)
    state_raw = jnp.dot(normed, state_full, preferred_element_type=jnp.float32)
    local_width = gate_inner.shape[1] // 2
    gate_part = gate_inner[:, :local_width]
    conv_input = jnp.concatenate([gate_inner[:, local_width:], state_raw], axis=1).astype(
        jnp.bfloat16
    )
    edge_count = conv_inner.shape[1] - 1
    edge_rows = shifted(conv_input[seq_rows - edge_count :], "seq", 1)
    padded = jnp.concatenate([edge_rows, conv_input], axis=0).astype(jnp.float32)
    conv_weight = jnp.concatenate([conv_inner[layer_index], conv_state[layer_index]], axis=1)
    conv_bias = jnp.concatenate([bias_inner[layer_index], bias_state[layer_index]])
    activated, conv_pull = jax.vjp(conv_silu, padded, conv_weight, conv_bias)
    state_size = state_raw.shape[1] // 2
    head_count = rate_bias.shape[1]
    inputs = activated[:, :local_width].reshape(seq_rows, head_count, local_width // head_count)
    keys_b = activated[:, local_width : local_width + state_size]
    queries_c = activated[:, local_width + state_size :]
    (step_rates, decays), rate_pull = jax.vjp(
        rate_piece, rate_raw, rate_bias[layer_index], decay_log[layer_index]
    )
    (span_decay, span_state), summary_pull = jax.vjp(
        span_summary, inputs, keys_b, step_rates, decays
    )
    identity = (jnp.ones_like(span_decay), jnp.zeros_like(span_state))
    entry_state = carried_in((span_decay, span_state), "seq", chain_combine, identity)[1]
    mixed_out, output_pull = jax.vjp(
        span_output,
        inputs,
        keys_b,
        queries_c,
        step_rates,
        decays,
        entry_state,
        skip_gain[layer_index],
    )
    gate_silu, silu_pull = jax.vjp(jax.nn.silu, gate_part)
    gated_out = mixed_out * gate_silu
    square_sum = lax.psum(jnp.sum(gated_out * gated_out, axis=1), "tensor")
    gate_scale = lax.rsqrt(square_sum / DI + EPSILON)[:, None]
    normed_out = (gated_out * gate_scale * gate_gain[layer_index][None, :]).astype(jnp.bfloat16)
    partial_out = jnp.dot(normed_out, out_full, preferred_element_type=jnp.float32)
    new_hidden = hidden + lax.psum(partial_out, "tensor")
    kept_values = (
        norm_pull,
        normed,
        silu_pull,
        gate_silu,
        mixed_out,
        gated_out,
        gate_scale,
        normed_out,
        conv_pull,
        rate_pull,
        summary_pull,
        output_pull,
        span_decay,
        entry_state,
        identity,
        local_width,
        edge_count,
    )
    return (new_hidden, kept_values)


def backward_layer(grad_hidden, weights, small_params, kept_values, layer_index):
    inner_full, rate_full, state_full, out_full = weights
    gate_gain = small_params[8]
    (
        norm_pull,
        normed,
        silu_pull,
        gate_silu,
        mixed_out,
        gated_out,
        gate_scale,
        normed_out,
        conv_pull,
        rate_pull,
        summary_pull,
        output_pull,
        span_decay,
        entry_state,
        identity,
        local_width,
        edge_count,
    ) = kept_values
    seq_rows = normed.shape[0]
    grad_low = grad_hidden.astype(jnp.bfloat16)
    grad_out_weight = jnp.dot(normed_out.T, grad_low, preferred_element_type=jnp.float32)
    grad_normed_out = jnp.dot(grad_low, out_full.T, preferred_element_type=jnp.float32)
    grad_gate_gain = jnp.sum(grad_normed_out * gated_out * gate_scale, axis=0)
    scaled_grad = grad_normed_out * gate_gain[layer_index][None, :]
    inner_sum = lax.psum(jnp.sum(scaled_grad * gated_out, axis=1), "tensor")
    scale_cube = gate_scale * gate_scale * gate_scale
    grad_gated = gate_scale * scaled_grad - gated_out * scale_cube * (inner_sum[:, None] / DI)
    grad_mixed = grad_gated * gate_silu
    grad_gate = silu_pull(grad_gated * mixed_out)[0]
    grad_inputs, grad_keys, grad_queries, grad_rates, grad_decays, grad_entry, grad_skip_gain = (
        output_pull(grad_mixed)
    )
    end_grads = carried_in_2((span_decay, grad_entry), "seq", chain_combine, identity)[1]
    grad_span_decay = jnp.sum(end_grads * entry_state, axis=(1, 2))
    more_inputs, more_keys, more_rates, more_decays = summary_pull((grad_span_decay, end_grads))
    grad_raw, grad_rate_bias, grad_decay_log = rate_pull(
        (grad_rates + more_rates, grad_decays + more_decays)
    )
    grad_activated = jnp.concatenate(
        [(grad_inputs + more_inputs).reshape(seq_rows, -1), grad_keys + more_keys, grad_queries],
        axis=1,
    )
    grad_padded, grad_conv_weight, grad_conv_bias = conv_pull(grad_activated)
    edge_back = shifted(grad_padded[:edge_count], "seq", -1)
    grad_conv_input = grad_padded[edge_count:]
    grad_conv_input = jnp.concatenate(
        [
            grad_conv_input[: seq_rows - edge_count],
            grad_conv_input[seq_rows - edge_count :] + edge_back,
        ],
        axis=0,
    )
    grad_inner_low = jnp.concatenate([grad_gate, grad_conv_input[:, :local_width]], axis=1).astype(
        jnp.bfloat16
    )
    grad_state_raw = grad_conv_input[:, local_width:]
    grad_rate_low = grad_raw.astype(jnp.bfloat16)
    grad_inner_weight = jnp.dot(normed.T, grad_inner_low, preferred_element_type=jnp.float32)
    grad_rate_weight = jnp.dot(normed.T, grad_rate_low, preferred_element_type=jnp.float32)
    grad_state_weight = product(normed.astype(jnp.float32).T, grad_state_raw)
    grad_normed_part = (
        jnp.dot(grad_inner_low, inner_full.T, preferred_element_type=jnp.float32)
        + jnp.dot(grad_rate_low, rate_full.T, preferred_element_type=jnp.float32)
        + product(grad_state_raw, state_full.astype(jnp.float32).T)
    )
    grad_normed, grad_conv_state, grad_bias_state = (
        lax.psum(grad_normed_part.astype(jnp.bfloat16), "tensor").astype(jnp.float32),
        lax.psum(grad_conv_weight[:, local_width:].astype(jnp.bfloat16), "tensor").astype(
            jnp.float32
        ),
        lax.psum(grad_conv_bias[local_width:].astype(jnp.bfloat16), "tensor").astype(jnp.float32),
    )
    grad_hidden_norm, grad_norm_gain = norm_pull(grad_normed)
    layer_grads = (
        grad_inner_weight.reshape(grad_inner_weight.shape[0], 2, local_width),
        grad_rate_weight,
        grad_state_weight,
        grad_out_weight,
        grad_norm_gain,
        grad_conv_weight[:, :local_width],
        grad_conv_bias[:local_width],
        grad_conv_state,
        grad_bias_state,
        grad_rate_bias,
        grad_decay_log,
        grad_skip_gain,
        grad_gate_gain,
    )
    return (grad_hidden + grad_hidden_norm, layer_grads)


def stack_layers(layer_sums, position):
    return jnp.stack([grads_here[position] for grads_here in layer_sums])


def span_body(
    tokens,
    cotangent,
    norm_gain,
    inner_weight,
    rate_weight,
    state_weight,
    conv_inner,
    bias_inner,
    conv_state,
    bias_state,
    rate_bias,
    decay_log,
    skip_gain,
    gate_gain,
    out_weight,
):
    small_params = (
        norm_gain,
        conv_inner,
        bias_inner,
        conv_state,
        bias_state,
        rate_bias,
        decay_log,
        skip_gain,
        gate_gain,
    )
    layer_count = norm_gain.shape[0]
    batch_count = tokens.shape[0]
    results = []
    kept_batches = []
    for batch_index in range(batch_count):
        hidden = tokens[batch_index, 0].astype(jnp.float32)
        kept_layers = []
        for layer_index in range(layer_count):
            weights = gather_layer(inner_weight, rate_weight, state_weight, out_weight, layer_index)
            hidden, kept_values = forward_layer(hidden, weights, small_params, layer_index)
            kept_layers.append(kept_values)
        results.append(hidden)
        kept_batches.append(kept_layers)
    layer_sums = [None] * layer_count
    seq_grads = []
    for batch_index in range(batch_count):
        grad_hidden = cotangent[batch_index, 0].astype(jnp.float32)
        for layer_index in reversed(range(layer_count)):
            weights = gather_layer(inner_weight, rate_weight, state_weight, out_weight, layer_index)
            grad_hidden, layer_grads = backward_layer(
                grad_hidden,
                weights,
                small_params,
                kept_batches[batch_index][layer_index],
                layer_index,
            )
            if layer_sums[layer_index] is None:
                layer_sums[layer_index] = layer_grads
            else:
                layer_sums[layer_index] = tuple(
                    (older + newer for older, newer in zip(layer_sums[layer_index], layer_grads))
                )
        seq_grads.append(grad_hidden)
    shard_inner, shard_rate, shard_out = (
        lax.psum_scatter(
            stack_layers(layer_sums, 0), ("dp", "seq"), scatter_dimension=1, tiled=True
        ),
        lax.psum_scatter(
            stack_layers(layer_sums, 1), ("dp", "seq"), scatter_dimension=1, tiled=True
        ),
        lax.psum_scatter(
            stack_layers(layer_sums, 3), ("dp", "seq"), scatter_dimension=2, tiled=True
        ),
    )
    shard_state = lax.psum_scatter(
        stack_layers(layer_sums, 2), ("dp", "seq", "tensor"), scatter_dimension=1, tiled=True
    )
    summed_small = lax.psum(
        (
            stack_layers(layer_sums, 4),
            stack_layers(layer_sums, 5),
            stack_layers(layer_sums, 6),
            stack_layers(layer_sums, 7),
            stack_layers(layer_sums, 8),
            stack_layers(layer_sums, 9),
            stack_layers(layer_sums, 10),
            stack_layers(layer_sums, 11),
            stack_layers(layer_sums, 12),
        ),
        ("dp", "seq"),
    )
    output = jnp.stack(results)[:, None]
    input_grad = jnp.stack(seq_grads)[:, None]
    return (
        output,
        input_grad,
        summed_small[0],
        shard_inner,
        shard_rate,
        shard_state,
        summed_small[1],
        summed_small[2],
        summed_small[3],
        summed_small[4],
        summed_small[5],
        summed_small[6],
        summed_small[7],
        summed_small[8],
        shard_out,
    )


GROUP = ("seq", "tensor")
LANES = 128
ROWS = 8
BF16, F32 = jnp.bfloat16, jnp.float32


def hop(value, first, second):
    pairs = [
        (place * 2 + core, (place ^ (second if core else first)) * 2 + core)
        for place in range(4)
        for core in range(2)
    ]
    return lax.ppermute(value, GROUP, pairs)


def swap(value):
    return lax.ppermute(value, "tensor", [(0, 1), (1, 0)])


def places():
    place, core = lax.axis_index("seq"), lax.axis_index("tensor")
    return place, core, place ^ (1 + core), place ^ (2 - core), place ^ 3


def put(buffer, block, *index):
    spots = index + (0,) * (buffer.ndim - len(index))
    return lax.dynamic_update_slice(buffer, block.reshape((1,) * len(index) + block.shape), spots)


def pick(array, index, axis=0):
    return lax.dynamic_index_in_dim(array, index, axis, False)


def line_shift(value, axis, step):
    count = lax.axis_size(axis)
    return lax.ppermute(value, axis, [(i, (i + step) % count) for i in range(count)])


def line_place(blocks, columns):
    count, place, rows = lax.axis_size("dp"), lax.axis_index("dp"), blocks[0].shape[0]
    out = jnp.zeros((count * rows, columns), blocks[0].dtype)
    for step, block in enumerate(blocks):
        out = lax.dynamic_update_slice(out, block, ((place - step) % count * rows, 0))
    return out


def line_near(block):
    count = lax.axis_size("dp")
    return jnp.stack([block] + [line_shift(block, "dp", step) for step in range(1, count)])


def line_sum_steps(part):
    count, place = lax.axis_size("dp"), lax.axis_index("dp")
    sent = [part((place + step) % count).astype(BF16) for step in range(1, count)]
    got = [line_shift(value, "dp", step + 1) for step, value in enumerate(sent)]
    token = yield sent
    total = part(place)
    for value in gate(got, token):
        total = total + value.astype(F32)
    return total


def seq_trade(parts):
    place = lax.axis_index("seq")
    out = put(jnp.zeros_like(parts), pick(parts, place), place)
    for turn in (1, 2, 3):
        got = lax.ppermute(pick(parts, place ^ turn), "seq", [(i, i ^ turn) for i in range(4)])
        out = put(out, got, place ^ turn)
    return out


def mesh_sum_steps(value):
    count = lax.axis_size("dp")
    turns = [("seq", 4, 1), ("seq", 4, 2)]
    turns += [("dp", count, 1 << bit) for bit in range(count.bit_length() - 1)]
    for axis, size, turn in turns:
        moved = lax.ppermute(value, axis, [(i, i ^ turn) for i in range(size)])
        token = yield value
        value = value + gate(moved, token)
    return value


def trade_steps(parts):
    place = lax.axis_index("seq")
    sent = [pick(parts, place ^ turn) for turn in (1, 2, 3)]
    got = [
        lax.ppermute(value, "seq", [(i, i ^ turn) for i in range(4)])
        for turn, value in zip((1, 2, 3), sent)
    ]
    token = yield sent
    out = put(jnp.zeros_like(parts), pick(parts, place), place)
    for turn, value in zip((1, 2, 3), gate(got, token)):
        out = put(out, value, place ^ turn)
    return out


def dot(left, right, left_dim=1, right_dim=0):
    return lax.dot_general(
        left, right, (((left_dim,), (right_dim,)), ((), ())), preferred_element_type=F32
    )


def split(value, count):
    pieces = []
    for _ in range(count):
        piece = value.astype(BF16)
        pieces.append(piece)
        value = value - piece.astype(F32)
    return pieces


def exact_left(value, ones, count, right_dim=0):
    rows = value.shape[0]
    stacked = dot(jnp.concatenate(split(value, count), axis=0), ones, 1, right_dim)
    total = stacked[:rows]
    for index in range(1, count):
        total = total + stacked[index * rows : (index + 1) * rows]
    return total


def head_sums(picker, value):
    high, low_part = split(value, 2)
    return dot(picker, high, 1, 1) + dot(picker, low_part, 1, 1)


def front(raw, window, taps, heads, spread, upper, width, state, extra):
    length = raw.shape[0]
    summed = taps[4:5, :] + taps[0:1, :] * window[5 : 5 + length, :]
    for tap in range(1, 4):
        summed = summed + taps[tap : tap + 1, :] * window[5 + tap : 5 + tap + length, :]
    sig = jax.nn.sigmoid(summed)
    activated = summed * sig
    rates = jnp.transpose(raw[:, 2 * width + 2 * state :])[:ROWS] + heads[0:ROWS, :]
    steps = jnp.maximum(rates, 0.0) + jnp.log1p(jnp.exp(-jnp.abs(rates)))
    decays = -jnp.exp(heads[ROWS : 2 * ROWS, :]) * steps
    running = exact_left(decays, upper, 3)
    ending = running[:, length - 1 : length]
    grown = jnp.exp(running)
    tail = jnp.exp(ending - running)
    rows = [steps, running, grown, tail] + extra
    rows.append(jnp.zeros((length - ROWS * len(rows), length), F32))
    columns = jnp.transpose(jnp.concatenate(rows, axis=0))
    high, low_part = split(columns, 2)
    wide = dot(high, spread) + dot(low_part, spread)
    whole_decay = jnp.exp(jnp.broadcast_to(ending, (ROWS, LANES)))
    inputs = activated[:, :width]
    return dict(
        summed=summed,
        sig=sig,
        inputs=inputs,
        keys=activated[:, width : width + state].astype(BF16),
        queries=activated[:, width + state :].astype(BF16),
        rates=rates,
        decays=decays,
        running=running,
        columns=columns,
        steps_wide=wide[:, :width],
        grown_wide=wide[:, width : 2 * width],
        tail_wide=wide[:, 2 * width : 3 * width],
        whole_decay=whole_decay,
    )


def per_row(whole_decay, head_count, head_size):
    return jnp.concatenate(
        [
            jnp.broadcast_to(whole_decay[h : h + 1, :], (head_size, LANES))
            for h in range(head_count)
        ],
        axis=0,
    )


def decay_matrix(parts, h, causal):
    length = causal.shape[0]
    column = parts["columns"][:, ROWS + h : ROWS + h + 1]
    row = parts["running"][h : h + 1, :]
    gap = jnp.broadcast_to(column, (length, length)) - row
    return jnp.exp(jnp.where(causal, gap, -1e30))


def causal_mask(length):
    return lax.broadcasted_iota(jnp.int32, (length, length), 0) >= lax.broadcasted_iota(
        jnp.int32, (length, length), 1
    )


def forward_kernel(
    head_size,
    order_ref,
    raw_ref,
    taps_ref,
    chans_ref,
    heads_ref,
    spread_ref,
    upper_ref,
    value_ref,
    square_ref,
    mixed_ref,
    state_ref,
    carry,
    window,
):
    length, width, state = raw_ref.shape[0], chans_ref.shape[1], carry.shape[1]
    conv_width = width + 2 * state
    head_count = width // head_size
    pair = LANES // head_size

    @pl.when(pl.program_id(0) == 0)
    def _():
        carry[...] = jnp.zeros_like(carry)
        window[0:ROWS, :] = jnp.zeros((ROWS, conv_width), F32)

    raw = raw_ref[...]
    window[ROWS : ROWS + length, :] = raw[:, width : width + conv_width].astype(BF16).astype(F32)
    parts = front(
        raw,
        window,
        taps_ref[...],
        heads_ref[...],
        spread_ref[...],
        upper_ref[...],
        width,
        state,
        [],
    )
    window[0:ROWS, :] = window[length : length + ROWS, :]
    inputs, keys, queries = parts["inputs"], parts["keys"], parts["queries"]
    before = carry[...]
    state_ref[...] = before
    stepped = inputs * parts["steps_wide"]
    stepped_low = stepped.astype(BF16)
    scores = dot(queries, keys, 1, 1)
    causal = causal_mask(length)
    lane = lax.broadcasted_iota(jnp.int32, (length, LANES), 1) // head_size
    columns = []
    for block in range(head_count // pair):
        source = stepped_low[:, block * LANES : (block + 1) * LANES]
        joined = None
        for k in range(pair):
            mixing = (scores * decay_matrix(parts, block * pair + k, causal)).astype(BF16)
            got = dot(mixing, source)
            joined = got if joined is None else jnp.where(lane == k, got, joined)
        columns.append(joined)
    carried = dot(queries, before.astype(BF16), 1, 1)
    mixed = (
        jnp.concatenate(columns, axis=1)
        + carried * parts["grown_wide"]
        + chans_ref[0:1, :] * inputs
    )
    update = dot((stepped * parts["tail_wide"]).astype(BF16), keys, 0, 0)
    carry[...] = per_row(parts["whole_decay"], head_count, head_size) * before + update
    gate = raw[:, :width]
    gated = mixed * (gate * jax.nn.sigmoid(gate))
    mixed_ref[...] = mixed
    value_ref[...] = (gated * chans_ref[1:2, :]).astype(BF16)
    squares = jnp.sum(gated * gated, axis=1, keepdims=True)
    square_ref[...] = jnp.transpose(jnp.broadcast_to(squares, (length, length)))[:ROWS]


def backward_kernel(
    head_size,
    inner_count,
    order_ref,
    grad_ref,
    raw_ref,
    past_ref,
    mixed_ref,
    state_ref,
    token_ref,
    taps_ref,
    chans_ref,
    heads_ref,
    spread_ref,
    upper_ref,
    picker_ref,
    back_ref,
    taps_out,
    chans_out,
    heads_out,
    carry,
    window,
    later,
):
    length, width, state = raw_ref.shape[0], chans_ref.shape[1], carry.shape[1]
    conv_width = width + 2 * state
    head_count = width // head_size
    pair = LANES // head_size
    step, count = pl.program_id(0), pl.num_programs(0)

    @pl.when(step == 0)
    def _():
        carry[...] = jnp.zeros_like(carry)
        later[length : length + ROWS, :] = jnp.zeros((ROWS, conv_width), F32)
        taps_out[...] = jnp.zeros_like(taps_out)
        chans_out[...] = jnp.zeros_like(chans_out)
        heads_out[...] = jnp.zeros_like(heads_out)

    raw = raw_ref[...]
    past = past_ref[:, width : width + conv_width].astype(BF16).astype(F32)
    window[0:ROWS, :] = jnp.where(step == count - 1, 0.0, past)
    window[ROWS : ROWS + length, :] = raw[:, width : width + conv_width].astype(BF16).astype(F32)
    taps, heads, picker = taps_ref[...], heads_ref[...], picker_ref[...]
    parts = front(
        raw, window, taps, heads, spread_ref[...], upper_ref[...], width, state, [token_ref[...]]
    )
    inputs, keys, queries = parts["inputs"], parts["keys"], parts["queries"]
    skip, gain = chans_ref[0:1, :], chans_ref[1:2, :]
    scale = parts["columns"][:, 4 * ROWS : 4 * ROWS + 1]
    inner = parts["columns"][:, 4 * ROWS + 1 : 4 * ROWS + 2]

    gate, mixed = raw[:, :width], mixed_ref[...]
    gate_sig = jax.nn.sigmoid(gate)
    gate_silu = gate * gate_sig
    gated = mixed * gate_silu
    grad = grad_ref[...]
    scaled_gated = gated * scale
    gain_term = jnp.sum(grad * scaled_gated, axis=0, keepdims=True)
    grad_gated = scale * (grad * gain) - gated * (scale * scale * scale * inner / inner_count)
    grad_mixed = grad_gated * gate_silu
    back_ref[:, :width] = (
        grad_gated * mixed * (gate_sig + gate_silu * (1.0 - gate_sig))
    ).astype(BF16)
    skip_term = jnp.sum(grad_mixed * inputs, axis=0, keepdims=True)
    chans_out[0:1, :] += skip_term
    chans_out[1:2, :] += gain_term

    stepped = inputs * parts["steps_wide"]
    stepped_low, grad_low = stepped.astype(BF16), grad_mixed.astype(BF16)
    scores = dot(queries, keys, 1, 1)
    causal = causal_mask(length)
    lane = lax.broadcasted_iota(jnp.int32, (length, LANES), 1)
    head_lane = lane // head_size
    grad_scores = jnp.zeros((length, length), F32)
    row_sums = jnp.zeros((length, length), F32)
    column_sums, columns = [], []
    for block in range(head_count // pair):
        cut = slice(block * LANES, (block + 1) * LANES)
        source, target = stepped_low[:, cut], grad_low[:, cut]
        joined = None
        for k in range(pair):
            h = block * pair + k
            spread_h = decay_matrix(parts, h, causal)
            own_target = jnp.where(head_lane == k, target, jnp.zeros_like(target))
            pulled = dot(own_target, source, 1, 1) * spread_h
            grad_scores = grad_scores + pulled
            moved = pulled * scores
            row_sums = jnp.where(lane == h, jnp.sum(moved, axis=1, keepdims=True), row_sums)
            column_sums.append(jnp.sum(moved, axis=0, keepdims=True))
            got = dot((scores * spread_h).astype(BF16), target, 0, 0)
            joined = got if joined is None else jnp.where(head_lane == k, got, joined)
        columns.append(joined)
    before, after = state_ref[...], carry[...]
    before_low, after_low = before.astype(BF16), after.astype(BF16)
    tail_wide, grown_wide = parts["tail_wide"], parts["grown_wide"]
    through = tail_wide * dot(keys, after_low, 1, 1)
    grad_stepped = jnp.concatenate(columns, axis=1) + through
    ended = stepped * through
    carried = dot(queries, before_low, 1, 1) * grown_wide
    whole_rows = per_row(parts["whole_decay"], head_count, head_size)
    kept = whole_rows * after
    held = jnp.sum(kept * before, axis=1, keepdims=True)
    spare = jnp.zeros((ROWS - head_count, 1), F32)
    held_heads = jnp.concatenate(
        [
            jnp.sum(held[h * head_size : (h + 1) * head_size], axis=0, keepdims=True)
            for h in range(head_count)
        ]
        + [spare],
        axis=0,
    )
    ended_heads = head_sums(picker, ended)
    grad_running = (
        jnp.transpose(row_sums)[:ROWS]
        - jnp.concatenate(column_sums + [jnp.zeros((ROWS - head_count, length), F32)], axis=0)
        + head_sums(picker, grad_mixed * carried)
        - ended_heads
    )
    last = jnp.sum(ended_heads, axis=1, keepdims=True) + held_heads
    row_lane = lax.broadcasted_iota(jnp.int32, (ROWS, length), 1)
    grad_running = grad_running + jnp.where(row_lane == length - 1, last, 0.0)
    grad_decays = exact_left(grad_running, upper_ref[...], 3, 1)
    grad_steps = head_sums(picker, inputs * grad_stepped)
    grad_rates = (
        grad_steps - jnp.exp(heads[ROWS : 2 * ROWS, :]) * grad_decays
    ) * jax.nn.sigmoid(parts["rates"])
    row_head = lax.broadcasted_iota(jnp.int32, (ROWS, length), 0)
    grad_rates = jnp.where(row_head < head_count, grad_rates, 0.0)
    heads_out[0:ROWS, :] += grad_rates
    heads_out[ROWS : 2 * ROWS, :] += grad_decays * parts["decays"]
    back_ref[:, 2 * width + 2 * state :] = jnp.transpose(
        jnp.concatenate([grad_rates, jnp.zeros((LANES - ROWS, length), F32)], axis=0)
    ).astype(BF16)

    grad_inputs = parts["steps_wide"] * grad_stepped + skip * grad_mixed
    grown_low = (grown_wide * grad_mixed).astype(BF16)
    scores_low = grad_scores.astype(BF16)
    grad_queries = dot(scores_low, keys) + dot(grown_low, before_low)
    grad_keys = dot(scores_low, queries, 0, 0) + dot(
        (stepped * tail_wide).astype(BF16), after_low
    )
    carry[...] = kept + dot(grown_low, queries, 0, 0)

    sig, summed = parts["sig"], parts["summed"]
    grad_v = jnp.concatenate([grad_inputs, grad_keys, grad_queries], axis=1) * (
        sig + summed * sig * (1.0 - sig)
    )
    later[0:length, :] = grad_v
    grad_conv = taps[3:4, :] * grad_v
    taps_out[4:5, :] += jnp.sum(grad_v, axis=0, keepdims=True)
    for tap in range(4):
        if tap < 3:
            grad_conv = grad_conv + taps[tap : tap + 1, :] * later[3 - tap : 3 - tap + length, :]
        taps_out[tap : tap + 1, :] += jnp.sum(
            grad_v * window[5 + tap : 5 + tap + length, :], axis=0, keepdims=True
        )
    later[length : length + ROWS, :] = grad_v[0:ROWS]
    back_ref[:, width : width + conv_width] = grad_conv.astype(BF16)


def tables(width, head_size):
    channel_head = jnp.arange(width)[None, :] // head_size
    rows = jnp.arange(LANES)[:, None]
    spread = jnp.concatenate(
        [rows == channel_head + ROWS * kind for kind in (0, 2, 3)], axis=1
    ).astype(BF16)
    upper = (rows <= jnp.arange(LANES)[None, :]).astype(BF16)
    picker = (jnp.arange(ROWS)[:, None] == channel_head).astype(BF16)
    return spread, upper, picker


def fixed(shape):
    return pl.BlockSpec(shape, lambda i, order: (0,) * len(shape))


def mix_forward(raw, order, small, tabs, head_size, width, state):
    taps, chans, heads = small
    spread, upper, _ = tabs
    tokens, columns = raw.shape
    count = tokens // STRETCH
    return pl.pallas_call(
        lambda *refs: forward_kernel(head_size, *refs),
        grid_spec=pltpu.PrefetchScalarGridSpec(
            num_scalar_prefetch=1,
            grid=(count,),
            in_specs=[
                pl.BlockSpec((STRETCH, columns), lambda i, order: (order[i], 0)),
                fixed(taps.shape),
                fixed(chans.shape),
                fixed(heads.shape),
                fixed(spread.shape),
                fixed(upper.shape),
            ],
            out_specs=[
                pl.BlockSpec((STRETCH, width), lambda i, order: (order[i], 0)),
                pl.BlockSpec((ROWS, LANES), lambda i, order: (i, 0)),
                pl.BlockSpec((STRETCH, width), lambda i, order: (i, 0)),
                pl.BlockSpec((None, width, state), lambda i, order: (i, 0, 0)),
            ],
            scratch_shapes=[
                pltpu.VMEM((width, state), F32),
                pltpu.VMEM((STRETCH + ROWS, width + 2 * state), F32),
            ],
        ),
        out_shape=[
            jax.ShapeDtypeStruct((tokens, width), BF16),
            jax.ShapeDtypeStruct((count * ROWS, LANES), F32),
            jax.ShapeDtypeStruct((tokens, width), F32),
            jax.ShapeDtypeStruct((count, width, state), F32),
        ],
        compiler_params=pltpu.CompilerParams(
            dimension_semantics=("arbitrary",), vmem_limit_bytes=40 * 2**20
        ),
        cost_estimate=pl.CostEstimate(
            flops=11_000_000_000, bytes_accessed=10_000_000, transcendentals=0
        ),
    )(order, raw, taps, chans, heads, spread, upper)


def mix_backward(grad, raw, mixed, states, token_rows, order, small, tabs, head_size, inner_count):
    taps, chans, heads = small
    spread, upper, picker = tabs
    tokens, columns = raw.shape
    width, state = states.shape[1:]
    count = tokens // STRETCH
    per = STRETCH // ROWS

    def moved(i, order):
        return (order[count - 1 - i], 0)

    def back(i, order):
        return (count - 1 - i, 0)

    def past(i, order):
        return (order[jnp.maximum(count - 2 - i, 0)] * per + per - 1, 0)

    return pl.pallas_call(
        lambda *refs: backward_kernel(head_size, inner_count, *refs),
        grid_spec=pltpu.PrefetchScalarGridSpec(
            num_scalar_prefetch=1,
            grid=(count,),
            in_specs=[
                pl.BlockSpec((STRETCH, width), moved),
                pl.BlockSpec((STRETCH, columns), moved),
                pl.BlockSpec((ROWS, columns), past),
                pl.BlockSpec((STRETCH, width), back),
                pl.BlockSpec((None, width, state), lambda i, order: (count - 1 - i, 0, 0)),
                pl.BlockSpec((ROWS, LANES), back),
                fixed(taps.shape),
                fixed(chans.shape),
                fixed(heads.shape),
                fixed(spread.shape),
                fixed(upper.shape),
                fixed(picker.shape),
            ],
            out_specs=[
                pl.BlockSpec((STRETCH, columns), moved),
                fixed(taps.shape),
                fixed(chans.shape),
                fixed(heads.shape),
            ],
            scratch_shapes=[
                pltpu.VMEM((width, state), F32),
                pltpu.VMEM((STRETCH + ROWS, width + 2 * state), F32),
                pltpu.VMEM((STRETCH + ROWS, width + 2 * state), F32),
            ],
        ),
        out_shape=[
            jax.ShapeDtypeStruct((tokens, columns), BF16),
            jax.ShapeDtypeStruct(taps.shape, F32),
            jax.ShapeDtypeStruct(chans.shape, F32),
            jax.ShapeDtypeStruct(heads.shape, F32),
        ],
        compiler_params=pltpu.CompilerParams(
            dimension_semantics=("arbitrary",), vmem_limit_bytes=40 * 2**20
        ),
        cost_estimate=pl.CostEstimate(
            flops=23_000_000_000, bytes_accessed=16_000_000, transcendentals=0
        ),
    )(order, grad, raw, raw, mixed, states, token_rows, taps, chans, heads, spread, upper, picker)


def small_kernel(layers, heads_here, head_count, state, spot_ref, place_ref, arrived_ref, out_ref):
    share = arrived_ref.shape[1]
    rows = share // layers
    row = lax.broadcasted_iota(jnp.int32, (LANES, LANES), 0)
    lane = lax.broadcasted_iota(jnp.int32, (LANES, LANES), 1)
    chosen = []
    for layer in range(layers):
        source = lane + layer * heads_here + place_ref[0] * head_count
        chosen.append(((row == source) & (lane < head_count)).astype(BF16))
    for index in range(out_ref.shape[1] // share):
        pair = [arrived_ref[spot_ref[2 * index + which]] for which in range(2)]
        own = jnp.where(place_ref[1] == 0, pair[0][:, 2 * state :], pair[1][:, 2 * state :])
        turned = jnp.concatenate([own.astype(F32), jnp.zeros((LANES - share, LANES), F32)], axis=0)
        turned = jnp.transpose(turned)[:share].astype(BF16)
        spot = index * share
        for layer in range(layers):
            cut = slice(layer * rows, (layer + 1) * rows)
            out_ref[layer, spot : spot + rows, : 2 * state] = pair[0][cut, : 2 * state]
            out_ref[layer, spot + rows : spot + share, : 2 * state] = pair[1][cut, : 2 * state]
            out_ref[layer, spot : spot + share, 2 * state :] = dot(turned, chosen[layer]).astype(BF16)


def small_unpack(arrived, order, layers, heads_here, head_count, state):
    line, share, columns = arrived.shape[0] // 8, arrived.shape[1], arrived.shape[2]
    place, core = lax.axis_index("seq"), lax.axis_index("tensor")
    back = (lax.axis_index("dp") - jnp.arange(line)) % line
    spots = (order[None, :] * line + back[:, None]).reshape(-1).astype(jnp.int32)
    scalars = pl.BlockSpec(memory_space=pltpu.SMEM)
    return pl.pallas_call(
        lambda *refs: small_kernel(layers, heads_here, head_count, state, *refs),
        in_specs=[scalars, scalars, pl.BlockSpec(memory_space=pltpu.VMEM)],
        out_shape=jax.ShapeDtypeStruct((layers, line * 4 * share, columns), BF16),
        compiler_params=pltpu.CompilerParams(vmem_limit_bytes=40 * 2**20),
    )(spots, jnp.stack([place, core]).astype(jnp.int32), arrived)


def finish_kernel(
    head_count, state, first_ref, second_ref, first_out, second_out, inner_ref, out_ref, state_ref, rate_ref
):
    width = out_ref.shape[2] // 4
    share = out_ref.shape[1]
    for layer, (ref, more) in enumerate(((first_ref, first_out), (second_ref, second_out))):
        states = jnp.zeros((share, 2 * state), F32)
        rates = []
        for index in range(4):
            value = ref[index].astype(F32)
            spot = slice(index * width, (index + 1) * width)
            inner_ref[layer, 0, :, spot] = value[:, :width]
            inner_ref[layer, 1, :, spot] = value[:, width : 2 * width]
            states = states + value[:, 2 * width : 2 * width + 2 * state]
            rate = jnp.concatenate(
                [value[:, 2 * width + 2 * state :], jnp.zeros((LANES - share, LANES), F32)], axis=0
            )
            rates.append(jnp.transpose(rate)[:head_count, :share])
            out_ref[layer, :, spot] = more[index].astype(F32)
        rate_ref[layer] = jnp.concatenate(rates, axis=0)
        state_ref[layer] = states


def finish(first, second, first_out, second_out, head_count, state, width):
    share = first.shape[1]
    return pl.pallas_call(
        lambda *refs: finish_kernel(head_count, state, *refs),
        out_shape=[
            jax.ShapeDtypeStruct((2, 2, share, 4 * width), F32),
            jax.ShapeDtypeStruct((2, share, 4 * width), F32),
            jax.ShapeDtypeStruct((2, share, 2 * state), F32),
            jax.ShapeDtypeStruct((2, 4 * head_count, share), F32),
        ],
        compiler_params=pltpu.CompilerParams(vmem_limit_bytes=40 * 2**20),
    )(first, second, first_out, second_out)


def norm_scale(hidden):
    return lax.rsqrt(jnp.mean(hidden * hidden, axis=1, keepdims=True) + EPSILON)


PLAN = (
    "v a l ga",
    "gb a v a",
    "b ga gb a",
    "b a b ga",
    "gb a b a",
    "b a b l",
    "a b a b",
    "a b a b",
    "a b a b",
    "a b a b",
    "a b a b",
    "a b oa1 a",
    "b xo a b",
    "a ob1 b a",
    "q ia1 b xo",
    "a b ib1 r",
    "a b oa0 a",
    "b a a b",
    "ob0 y ia0 b",
    "ib0 u a b",
    "a m b y",
    "q m b q",
    "m y b xg",
    "m r m r",
    "xg m u u",
)


def gate(value, token):
    return value if token is None else lax.optimization_barrier((value, token))[0]


def gather_steps(block):
    from_near, from_far = hop(block, 1, 2), hop(block, 2, 1)
    token = yield block
    from_near = gate(from_near, token)
    from_across = hop(from_near, 2, 1)
    token = yield from_near
    four = jnp.stack([block, from_near, gate(from_far, token), gate(from_across, token)])
    twin = swap(four)
    token = yield four
    return jnp.concatenate([four, gate(twin, token)])


def scatter_steps(own, other, tiny=None):
    got = swap(other)
    moved = None if tiny is None else hop(tiny, 1, 2)
    token = yield other
    got = gate(got, token)
    to_far = (own[2:].astype(F32) + got[2:].astype(F32)).astype(BF16)
    from_far = hop(to_far, 2, 1)
    if tiny is not None:
        tiny = tiny + gate(moved, token)
        moved = hop(tiny, 2, 1)
    token = yield to_far
    from_far = gate(from_far, token)
    both = own[:2].astype(F32) + got[:2].astype(F32) + from_far.astype(F32)
    side = both[1].astype(BF16)
    from_near = hop(side, 1, 2)
    if tiny is not None:
        tiny = tiny + gate(moved, token)
        moved = swap(tiny)
    token = yield (side, both[0])
    total = both[0] + gate(from_near, token).astype(F32)
    if tiny is not None:
        tiny = tiny + gate(moved, token)
    return total, tiny


def arrival_order():
    place, core = lax.axis_index("seq"), lax.axis_index("tensor")
    block = jnp.arange(8)
    turn, their = block // 2 ^ place, block % 2
    first = jnp.where(their == 0, turn, jnp.where(turn == 1, 2, jnp.where(turn == 2, 1, turn)))
    return (first + jnp.where(their == core, 0, 4)).astype(jnp.int32)


class Track:
    def __init__(self):
        self.token = None
        self.chains = {}

    def begin(self, name, chain):
        next(chain)
        self.chains[name] = chain

    def run(self, *plan):
        for name in " ".join(plan).split():
            name, _, count = name.partition("*")
            for _ in range(int(count or 1)):
                try:
                    self.token = self.chains[name].send(self.token)
                except StopIteration:
                    pass


def late_gather(store, key, block):
    token = yield None
    store[key] = yield from gather_steps(gate(block, token))


def kept_result(store, key, chain):
    yield None
    store[key] = yield from chain


def together(main, side):
    token = yield (next(main), next(side))
    result, running = None, [True, True]
    while any(running):
        values = []
        for index, chain in enumerate((main, side)):
            if running[index]:
                try:
                    values.append(chain.send(token))
                except StopIteration as stop:
                    running[index] = False
                    result = stop.value if index == 0 else result
        if any(running):
            token = yield tuple(values)
    return result


def sum_steps(value, store, key):
    moved = hop(value, 1, 2)
    token = yield value
    value = value + gate(moved, token)
    moved = hop(value, 2, 1)
    token = yield value
    value = value + gate(moved, token)
    moved = swap(value)
    token = yield value
    store[key] = value + gate(moved, token)


def head_body(
    tokens,
    cotangent,
    norm_gain,
    inner_weight,
    rate_weight,
    state_weight,
    conv_inner,
    bias_inner,
    conv_state,
    bias_state,
    rate_bias,
    decay_log,
    skip_gain,
    gate_gain,
    out_weight,
):
    layers, batches = norm_gain.shape[0], tokens.shape[0]
    model = tokens.shape[3]
    place, core = lax.axis_index("seq"), lax.axis_index("tensor")
    line = lax.axis_size("dp")
    share, half_width = inner_weight.shape[1], inner_weight.shape[3]
    inner_count = half_width * 2
    width = half_width // 4
    head_count = rate_bias.shape[1] // 4
    head_size = width // head_count
    state_share, state = state_weight.shape[1], state_weight.shape[2] // 2
    own_rows = tokens.shape[2] // 2
    length = own_rows * 8
    conv_width = width + 2 * state
    columns = 2 * width + 2 * state + LANES
    heads_here = rate_weight.shape[2]
    tabs = tables(width, head_size)

    def own(array):
        return lax.dynamic_slice_in_dim(array, core * own_rows, own_rows, 0)

    def quarter(array, count):
        return lax.dynamic_slice_in_dim(array, place * count, count, array.ndim - 1)

    def out_share(layer):
        turned = out_weight[layer].T.reshape(share, 4, width)
        return turned.transpose(1, 0, 2)

    def inner_share(layer):
        cut = inner_weight[layer].reshape(share, 2, 4, width)
        return cut.transpose(2, 0, 1, 3).reshape(4, share, 2 * width)

    def first_for(taker):
        cut = lax.dynamic_slice(inner_weight[0], (0, 0, taker * width), (share, 2, width))
        return jnp.concatenate([cut[:, 0], cut[:, 1]], axis=1)

    out_weights, in_weights = {}, {}

    def first_out():
        token = yield None
        traded = yield from trade_steps(gate(out_share(0), token))
        traded = traded.reshape(4 * share, width)
        got = [line_shift(traded, "dp", step) for step in range(1, line)]
        token = yield traded
        out_weights[0] = line_place([traded] + gate(got, token), width)

    def later(layer):
        token = yield None
        mixed_share = jnp.concatenate([inner_share(layer), out_share(layer)], axis=2)
        traded = yield from trade_steps(gate(mixed_share, token))
        full = lax.all_gather(traded.reshape(4 * share, -1), "dp").reshape(model, -1)
        token = yield traded
        full = gate(full, token)
        out_weights[layer] = full[:, 2 * width :]
        in_weights[layer] = jnp.concatenate([full[:, : 2 * width], small_full[layer]], axis=1)
        yield in_weights[layer]

    first = put(jnp.zeros((4, share, 2 * width), BF16), first_for(place), place)
    first_sent = [first_for(place ^ turn) for turn in (1, 2, 3)]
    for turn, value in zip((1, 2, 3), first_sent):
        pairs = [(i, i ^ turn) for i in range(4)]
        first = put(first, lax.ppermute(value, "seq", pairs), place ^ turn)
    first = first.reshape(4 * share, 2 * width)
    rate_rows = rate_weight.transpose(0, 2, 1).reshape(layers * heads_here, share)
    rate_rows = jnp.pad(rate_rows, ((0, share - layers * heads_here), (0, LANES - share)))
    small_share = jnp.concatenate([state_weight.reshape(share, 2 * state), rate_rows], axis=1)
    small_near = line_near(small_share)

    smalls = []

    def prepare():
        token = yield None
        given = (conv_inner, conv_state, bias_inner, bias_state, skip_gain, gate_gain, rate_bias, decay_log)
        (
            conv_inner_,
            conv_state_,
            bias_inner_,
            bias_state_,
            skip_gain_,
            gate_gain_,
            rate_bias_,
            decay_log_,
        ) = gate(given, token)
        for layer in range(layers):
            taps = jnp.concatenate([quarter(conv_inner_[layer], width), conv_state_[layer]], axis=1)
            bias = jnp.concatenate([quarter(bias_inner_[layer], width), bias_state_[layer]])
            taps = jnp.concatenate([taps, bias[None], jnp.zeros((3, conv_width), F32)], axis=0)
            skip = jnp.repeat(quarter(skip_gain_[layer], head_count), head_size)
            chans = jnp.stack([skip, quarter(gate_gain_[layer], width)])
            chans = jnp.concatenate([chans, jnp.zeros((ROWS - 2, width), F32)], axis=0)
            heads = jnp.stack(
                [quarter(rate_bias_[layer], head_count), quarter(decay_log_[layer], head_count)]
            )
            heads = jnp.pad(heads, ((0, 0), (0, ROWS - head_count))).reshape(2 * ROWS, 1)
            smalls.append((taps, chans, jnp.broadcast_to(heads, (2 * ROWS, LANES))))
        yield smalls

    order = arrival_order()
    track = Track()
    track.token = (first_sent, small_share)
    hiddens = [own(tokens[batch, 0]).astype(F32) for batch in range(batches)]
    row_scales, normed_all, whole = [], {}, {}
    for batch in range(batches):
        row_scales.append(norm_scale(hiddens[batch]))
        normed = (hiddens[batch] * row_scales[batch] * norm_gain[0][None, :]).astype(BF16)
        normed = gate(normed, track.token)
        track.begin(str(batch), kept_result(normed_all, (0, batch), gather_steps(normed)))
    track.begin("s", kept_result(whole, "small", gather_steps(gate(small_near, first))))
    track.begin("p", prepare())
    grads, grad_all = [], {}
    for batch, name in enumerate(("ga", "gb")):
        low_part = own(gate(cotangent[batch, 0], first_sent))
        grads.append(low_part.astype(F32))
        track.begin(name, late_gather(grad_all, (layers - 1, batch), low_part))
    track.run("0 1")
    first_got = [line_shift(first, "dp", step) for step in range(1, line)]
    track.token = first
    track.run("s")
    track.token = first_got[0]
    track.run("0 1 s p", "0 1 s ga", "gb 0 1 s")
    track.begin("v", first_out())
    track.begin("l", later(1))
    track.run("v l")
    first_full = line_place(gate([first] + first_got, track.token), columns)
    small_full = small_unpack(
        whole["small"].reshape(-1, share, small_share.shape[1]),
        order,
        layers,
        heads_here,
        head_count,
        state,
    )
    in_weights[0] = lax.dynamic_update_slice(first_full, small_full[0], (0, 2 * width))
    track.token = first_full
    gradients, inners, terms, outputs = {}, {}, {}, {}

    def inner_products(grad_low, summed):
        inner = jnp.sum(grad_low.astype(F32) * summed, axis=1)
        return put(jnp.zeros((8, own_rows), F32), inner, place * 2 + core)

    moves = order[None, :] == jnp.arange(8)[:, None]

    def halves_of(value, weight):
        half = length // 2
        other = dot(value[half:], weight, 1, 1).astype(BF16)
        return (
            dot(value[:half], weight, 1, 1).astype(BF16).reshape(4, own_rows, model),
            other.reshape(4, own_rows, model),
        )

    def batch_chain(batch):
        token = yield None
        hidden, row_scale = hiddens[batch], row_scales[batch]
        normed = normed_all[0, batch]
        kept = {}
        for layer in range(layers):
            normed = normed.reshape(length, model)
            raw = dot(gate(normed, token), in_weights[layer])
            token = yield raw
            value, squares, mixed, states = mix_forward(
                gate(raw, token), order, smalls[layer], tabs, head_size, width, state
            )
            token = yield value
            halves = halves_of(gate(value, token), out_weights[layer])
            summed, squares = yield from scatter_steps(
                *halves, squares.reshape(-1, ROWS, LANES)[:, 0]
            )
            scales = lax.rsqrt(squares / inner_count + EPSILON)
            flat_scales = scales.reshape(8, own_rows)
            own_scale = pick(flat_scales, place * 2 + core)[:, None]
            arrived = jnp.sum(jnp.where(moves[:, :, None], flat_scales[None], 0.0), axis=1)
            normed_out = (value.astype(F32) * arrived.reshape(length, 1)).astype(BF16)
            kept[layer] = (hidden, row_scale, normed, raw, mixed, states, summed, scales, normed_out)
            hidden = hidden + own_scale * summed
            if layer + 1 < layers:
                row_scale = norm_scale(hidden)
                normed = (hidden * row_scale * norm_gain[layer + 1][None, :]).astype(BF16)
                normed = yield from gather_steps(normed)
                token = None
        outputs[batch] = hidden
        grad_hidden = grads[batch]
        top_inner = inner_products(grad_hidden.astype(BF16), kept[layers - 1][6])
        yield from sum_steps(top_inner, inners, (layers - 1, batch))
        token = None
        for layer in reversed(range(layers)):
            hidden, row_scale, normed, raw, mixed, states, summed, scales, normed_out = kept[layer]
            whole_grad = grad_all[layer, batch].reshape(length, model)
            terms[layer, batch] = [whole_grad, normed_out, normed, None]
            grad_value = dot(gate(whole_grad, token), out_weights[layer])
            token = yield grad_value
            token_rows = jnp.stack([scales, inners[layer, batch].reshape(-1, LANES)], axis=1)
            token_rows = jnp.pad(token_rows, ((0, 0), (0, ROWS - 2), (0, 0)))
            back, taps_grad, chans_grad, heads_grad = mix_backward(
                gate(grad_value, token),
                raw,
                mixed,
                states,
                token_rows.reshape(-1, LANES),
                order,
                smalls[layer],
                tabs,
                head_size,
                inner_count,
            )
            terms[layer, batch][3] = back
            token = yield back
            halves = halves_of(gate(back, token), in_weights[layer])
            gain_term = sum(
                jnp.sum(part.reshape(-1, model).astype(F32) * cut.astype(F32), axis=0)
                for part, cut in zip(halves, (normed[: length // 2], normed[length // 2 :]))
            )
            gradients[layer, batch] = (
                taps_grad,
                chans_grad,
                heads_grad,
                gain_term / norm_gain[layer],
            )
            grad_normed, _ = yield from scatter_steps(*halves)
            weighted = grad_normed * norm_gain[layer][None, :]
            mean = jnp.mean(weighted * hidden, axis=1, keepdims=True)
            grad_hidden = (
                grad_hidden
                + row_scale * weighted
                - hidden * (row_scale * row_scale * row_scale) * mean
            )
            if layer > 0:
                grad_low = grad_hidden.astype(BF16)
                inner = inner_products(grad_low, kept[layer - 1][6])
                grad_all[layer - 1, batch] = yield from together(
                    gather_steps(grad_low), sum_steps(inner, inners, (layer - 1, batch))
                )
                token = None
        grads[batch] = grad_hidden
        yield grad_hidden

    totals = {}

    def term(key, layer, batch, left, right):
        value = dot(left, right, 0, 0)
        if batch > 0:
            value = value + totals[key, layer, batch - 1]
        totals[key, layer, batch] = value.astype(BF16) if batch == batches - 1 else value
        return totals[key, layer, batch]

    def out_term(layer, batch):
        token = yield None
        whole_grad, normed_out, _, _ = terms[layer, batch]
        yield term("out", layer, batch, gate(whole_grad, token), normed_out)

    def in_term(layer, batch):
        token = yield None
        _, _, normed, back = terms[layer, batch]
        yield term("in", layer, batch, gate(normed, token), back)

    rows = 4 * share

    def line_cut(array, index):
        return lax.dynamic_slice_in_dim(array, index * rows, rows, 0)

    def out_part(layer):
        total = totals["out", layer, batches - 1]
        return lambda index: line_cut(total, index).astype(F32)

    shares = {}

    def line_sum(total):
        return lax.psum_scatter(total, "dp", scatter_dimension=0, tiled=True)

    def first_sums(key):
        yield None
        if key == "out":
            total = yield from line_sum_steps(out_part(0))
            total = total.astype(BF16)
        else:
            packed = totals["in", 0, batches - 1]
            total = line_sum(packed)
            token = yield packed
            total = gate(total, token)
        shares[key, 0] = yield from trade_steps(total.reshape(4, share, -1))

    def later_sums(key, layer):
        token = yield None
        packed = totals[key, layer, batches - 1]
        total = line_sum(gate(packed, token))
        token = yield packed
        shares[key, layer] = yield from trade_steps(gate(total, token).reshape(4, share, -1))
        yield shares[key, layer]

    def both_cores(values, store, key):
        yield None
        others = [swap(value) for value in values()]
        token = yield values()
        both = []
        for value, other in zip(values(), gate(others, token)):
            first = jnp.where(core == 0, value, other)
            second = jnp.where(core == 0, other, value)
            both.append(jnp.concatenate([first, second], axis=0))
        store[key] = jnp.stack(both)[:, None]
        yield store[key]

    def small_sums():
        yield None
        flats = []
        for layer in range(layers):
            taps_grad, chans_grad, heads_grad, gain_term = (
                sum(values) for values in zip(*(gradients[layer, batch] for batch in range(batches)))
            )
            both = jnp.concatenate([gain_term, taps_grad[:5, width:].reshape(-1)])
            head_rows = jnp.stack(
                [
                    jnp.sum(heads_grad[:ROWS], axis=1)[:head_count],
                    jnp.sum(heads_grad[ROWS:], axis=1)[:head_count],
                    jnp.sum(chans_grad[0].reshape(head_count, head_size), axis=1),
                ]
            )
            flat = jnp.concatenate(
                [
                    both,
                    slot(taps_grad[:5, :width], width).reshape(-1),
                    slot(chans_grad[1], width),
                    slot(head_rows, head_count).reshape(-1),
                ]
            )
            flats.append(jnp.pad(flat, (0, -flat.shape[0] % LANES)))
        flat = jnp.stack(flats)
        shared = model + 10 * state
        moved = swap(flat[:, :shared])
        token = yield flat
        flat = lax.dynamic_update_slice(flat, flat[:, :shared] + gate(moved, token), (0, 0))
        finished["flat"] = yield from mesh_sum_steps(flat)

    def slot(array, count):
        shape = array.shape[:-1] + (4 * count,)
        spots = (0,) * (array.ndim - 1) + (place * count,)
        return lax.dynamic_update_slice(jnp.zeros(shape, F32), array, spots)

    finished = {}
    for batch, name in enumerate("ab"):
        track.begin(name, batch_chain(batch))
        for layer in range(layers):
            track.begin(f"o{name}{layer}", out_term(layer, batch))
            track.begin(f"i{name}{layer}", in_term(layer, batch))
    track.begin("y", first_sums("out"))
    track.begin("u", first_sums("in"))
    track.begin("r", later_sums("in", 1))
    track.begin("q", later_sums("out", 1))
    track.begin("xo", both_cores(lambda: [outputs[0], outputs[1]], finished, "output"))
    track.begin("xg", both_cores(lambda: [grads[0], grads[1]], finished, "input_grad"))
    track.begin("m", small_sums())
    track.run(*PLAN)

    inner_grad, out_grad, state_terms, rate_grad = finish(
        shares["in", 0],
        shares["in", 1],
        shares["out", 0],
        shares["out", 1],
        head_count,
        state,
        width,
    )
    state_terms = state_terms.reshape(layers, 2, state_share, 2 * state)
    state_grad = pick(state_terms, core, 1) + swap(pick(state_terms, 1 - core, 1))
    flat = finished["flat"]
    taken, small_out = 0, []
    for shape in ((model,), (5, 2 * state), (5, half_width), (half_width,), (3, 4 * head_count)):
        size = 1
        for extent in shape:
            size *= extent
        small_out.append(flat[:, taken : taken + size].reshape((layers,) + shape))
        taken += size

    return (
        finished["output"],
        finished["input_grad"],
        small_out[0],
        inner_grad.transpose(0, 2, 1, 3),
        rate_grad.transpose(0, 2, 1),
        state_grad,
        small_out[2][:, :4],
        small_out[2][:, 4],
        small_out[1][:, :4],
        small_out[1][:, 4],
        small_out[4][:, 0],
        small_out[4][:, 1],
        small_out[4][:, 2],
        small_out[3],
        out_grad.transpose(0, 2, 1),
    )


def by_heads(mesh, tokens, inner_weight, rate_bias, conv_state, state_weight):
    place_count, core_count, line = mesh.shape["seq"], mesh.shape["tensor"], mesh.shape["dp"]
    if place_count != 4 or core_count != 2:
        return False
    heads, inner = rate_bias.shape[1], inner_weight.shape[3]
    rows = tokens.shape[2] // 8
    return (
        tokens.shape[1] == line
        and tokens.shape[2] % 8 == 0
        and rows == STRETCH
        and tokens.shape[0] == 2
        and line >= 2
        and inner_weight.shape[0] == 2
        and heads % 8 == 0
        and heads // 8 <= ROWS
        and (inner // 8) % LANES == 0
        and LANES % (inner // heads) == 0
        and conv_state.shape[1] == 4
        and state_weight.shape[2] == 2 * LANES
        and inner_weight.shape[1] % (line * 4 * 32) == 0
    )


def solution(mesh):
    in_specs = (
        P(None, "dp", "seq", None),
        P(None, "dp", "seq", None),
        P(),
        P(None, ("dp", "seq"), None, "tensor"),
        P(None, ("dp", "seq"), "tensor"),
        P(None, ("dp", "seq", "tensor"), None),
        P(None, None, "tensor"),
        P(None, "tensor"),
        P(),
        P(),
        P(None, "tensor"),
        P(None, "tensor"),
        P(None, "tensor"),
        P(None, "tensor"),
        P(None, "tensor", ("dp", "seq")),
    )
    out_specs = (
        P(None, "dp", "seq", None),
        P(None, "dp", "seq", None),
        P(),
        P(None, ("dp", "seq"), None, "tensor"),
        P(None, ("dp", "seq"), "tensor"),
        P(None, ("dp", "seq", "tensor"), None),
        P(None, None, "tensor"),
        P(None, "tensor"),
        P(),
        P(),
        P(None, "tensor"),
        P(None, "tensor"),
        P(None, "tensor"),
        P(None, "tensor"),
        P(None, "tensor", ("dp", "seq")),
    )
    def run(*arrays):
        by_name = (arrays[0], arrays[3], arrays[10], arrays[8], arrays[5])
        chosen = head_body if by_heads(mesh, *by_name) else span_body
        return jax.shard_map(
            chosen, mesh=mesh, in_specs=in_specs, out_specs=out_specs, check_vma=False
        )(*arrays)

    return run
```

```python
import jax
import jax.numpy as jnp
from jax import lax
from jax.experimental import pallas as pl
from jax.experimental.pallas import tpu as pltpu
from jax.sharding import PartitionSpec as P

DI = 3072
STRETCH = 128


EPSILON = 1e-05
HIGHEST = lax.Precision.HIGHEST


def shifted(value, axis, steps):
    count = lax.axis_size(axis)
    leading, last = (max(0, -steps), min(count, count - steps))
    return lax.ppermute(value, axis, [(source, source + steps) for source in range(leading, last)])


def carried_in(array, axis, combine, identity):
    length, place = (lax.axis_size(axis), lax.axis_index(axis))
    everything = jax.tree.map(
        lambda part, kind: lax.all_gather(part.astype(kind), axis),
        array,
        (jnp.bfloat16, jnp.bfloat16),
    )
    start = jax.tree.map(
        lambda part, zero: jnp.broadcast_to(jnp.asarray(zero, part.dtype), part.shape),
        array,
        identity,
    )

    def turn(k, before):
        reached = k < place
        new = combine(
            before, jax.tree.map(lambda part, own: part[k].astype(own.dtype), everything, array)
        )
        return jax.tree.map(lambda a, b: jnp.where(reached, a, b), new, before)

    return lax.fori_loop(0, length, turn, start)


def carried_in_2(array, axis, join, neutral):
    count = lax.axis_size(axis)
    place = lax.axis_index(axis)
    ahead = count - 1 - place
    gathered = jax.tree.map(
        lambda a, kind: lax.all_gather(a.astype(kind), axis),
        array,
        jax.tree.map(lambda a: jnp.bfloat16 if a.dtype == jnp.float32 else a.dtype, array),
    )
    state = jax.tree.map(lambda a, e: jnp.zeros_like(a) + jnp.asarray(e, a.dtype), array, neutral)

    def one(turn, state):
        source = count - 1 - turn
        return join(
            state,
            jax.tree.map(
                lambda a, own: lax.dynamic_index_in_dim(a, source, 0, False).astype(own.dtype),
                gathered,
                array,
            ),
        )

    return lax.fori_loop(0, ahead, one, state)


def product(left_side, right_side):
    return jnp.dot(left_side, right_side, precision=HIGHEST, preferred_element_type=jnp.float32)


def conv_silu(padded, weight, conv_bias):
    conv_width = weight.shape[0]
    out_rows = padded.shape[0] - conv_width + 1
    summed = conv_bias[None, :] + weight[0][None, :] * padded[0:out_rows]
    for offset in range(1, conv_width):
        summed = summed + weight[offset][None, :] * padded[offset : offset + out_rows]
    return jax.nn.silu(summed)


def block_step(carry_state, pieces):
    inputs, keys_b, queries_c, step_rates, decays = pieces
    running = jnp.cumsum(decays, axis=0)
    block_len = inputs.shape[0]
    causal = jnp.arange(block_len)[:, None] >= jnp.arange(block_len)[None, :]
    spread = running.T[:, :, None] - running.T[:, None, :]
    weights = jnp.exp(jnp.where(causal[None, :, :], spread, -jnp.inf))
    scores = product(queries_c, keys_b.T)
    mixing = scores[None, :, :] * weights * step_rates.T[:, None, :]
    inside = jnp.einsum("hts,shp->thp", mixing, inputs, precision=HIGHEST)
    carried = (
        jnp.einsum("tn,hpn->thp", queries_c, carry_state, precision=HIGHEST)
        * jnp.exp(running)[:, :, None]
    )
    tail_weight = jnp.exp(running[-1][None, :] - running) * step_rates
    update = jnp.einsum("shp,sn->hpn", tail_weight[:, :, None] * inputs, keys_b, precision=HIGHEST)
    return (jnp.exp(running[-1])[:, None, None] * carry_state + update, inside + carried)


def state_step(carry_state, pieces):
    inputs, keys_b, step_rates, decays = pieces
    running = jnp.cumsum(decays, axis=0)
    tail_weight = jnp.exp(running[-1][None, :] - running) * step_rates
    update = jnp.einsum("shp,sn->hpn", tail_weight[:, :, None] * inputs, keys_b, precision=HIGHEST)
    return (jnp.exp(running[-1])[:, None, None] * carry_state + update, None)


def to_blocks(values):
    return values.reshape((values.shape[0] // STRETCH, STRETCH) + values.shape[1:])


def span_summary(inputs, keys_b, step_rates, decays):
    zero_state = jnp.zeros((inputs.shape[1], inputs.shape[2], keys_b.shape[1]), jnp.float32)
    end_state, _ = lax.scan(
        state_step,
        zero_state,
        (to_blocks(inputs), to_blocks(keys_b), to_blocks(step_rates), to_blocks(decays)),
    )
    return (jnp.exp(jnp.sum(decays, axis=0)), end_state)


def span_output(inputs, keys_b, queries_c, step_rates, decays, entry_state, skip_gain):
    _, block_out = lax.scan(
        block_step,
        entry_state,
        (
            to_blocks(inputs),
            to_blocks(keys_b),
            to_blocks(queries_c),
            to_blocks(step_rates),
            to_blocks(decays),
        ),
    )
    mixed_out = block_out.reshape(inputs.shape) + skip_gain[None, :, None] * inputs
    return mixed_out.reshape(inputs.shape[0], -1)


def rate_piece(rate_raw, rate_bias, decay_log):
    step_rates = jax.nn.softplus(rate_raw + rate_bias[None, :])
    return (step_rates, -jnp.exp(decay_log)[None, :] * step_rates)


def norm_piece(hidden, norm_gain):
    row_scale = lax.rsqrt(jnp.mean(hidden * hidden, axis=1, keepdims=True) + EPSILON)
    return hidden * row_scale * norm_gain[None, :]


def chain_combine(earlier, following):
    return (earlier[0] * following[0], following[1] + following[0][:, None, None] * earlier[1])


def gather_layer(inner_weight, rate_weight, state_weight, out_weight, layer_index):
    inner_full, rate_full, out_full = (
        lax.all_gather(inner_weight[layer_index], ("dp", "seq"), axis=0, tiled=True),
        lax.all_gather(rate_weight[layer_index], ("dp", "seq"), axis=0, tiled=True),
        lax.all_gather(out_weight[layer_index], ("dp", "seq"), axis=1, tiled=True),
    )
    state_full = lax.all_gather(
        state_weight[layer_index], ("dp", "seq", "tensor"), axis=0, tiled=True
    )
    return (inner_full.reshape(inner_full.shape[0], -1), rate_full, state_full, out_full)


def forward_layer(hidden, weights, small_params, layer_index):
    inner_full, rate_full, state_full, out_full = weights
    (
        norm_gain,
        conv_inner,
        bias_inner,
        conv_state,
        bias_state,
        rate_bias,
        decay_log,
        skip_gain,
        gate_gain,
    ) = small_params
    seq_rows = hidden.shape[0]
    normed_full, norm_pull = jax.vjp(norm_piece, hidden, norm_gain[layer_index])
    normed = normed_full.astype(jnp.bfloat16)
    gate_inner = jnp.dot(normed, inner_full, preferred_element_type=jnp.float32)
    rate_raw = jnp.dot(normed, rate_full, preferred_element_type=jnp.float32)
    state_raw = jnp.dot(normed, state_full, preferred_element_type=jnp.float32)
    local_width = gate_inner.shape[1] // 2
    gate_part = gate_inner[:, :local_width]
    conv_input = jnp.concatenate([gate_inner[:, local_width:], state_raw], axis=1).astype(
        jnp.bfloat16
    )
    edge_count = conv_inner.shape[1] - 1
    edge_rows = shifted(conv_input[seq_rows - edge_count :], "seq", 1)
    padded = jnp.concatenate([edge_rows, conv_input], axis=0).astype(jnp.float32)
    conv_weight = jnp.concatenate([conv_inner[layer_index], conv_state[layer_index]], axis=1)
    conv_bias = jnp.concatenate([bias_inner[layer_index], bias_state[layer_index]])
    activated, conv_pull = jax.vjp(conv_silu, padded, conv_weight, conv_bias)
    state_size = state_raw.shape[1] // 2
    head_count = rate_bias.shape[1]
    inputs = activated[:, :local_width].reshape(seq_rows, head_count, local_width // head_count)
    keys_b = activated[:, local_width : local_width + state_size]
    queries_c = activated[:, local_width + state_size :]
    (step_rates, decays), rate_pull = jax.vjp(
        rate_piece, rate_raw, rate_bias[layer_index], decay_log[layer_index]
    )
    (span_decay, span_state), summary_pull = jax.vjp(
        span_summary, inputs, keys_b, step_rates, decays
    )
    identity = (jnp.ones_like(span_decay), jnp.zeros_like(span_state))
    entry_state = carried_in((span_decay, span_state), "seq", chain_combine, identity)[1]
    mixed_out, output_pull = jax.vjp(
        span_output,
        inputs,
        keys_b,
        queries_c,
        step_rates,
        decays,
        entry_state,
        skip_gain[layer_index],
    )
    gate_silu, silu_pull = jax.vjp(jax.nn.silu, gate_part)
    gated_out = mixed_out * gate_silu
    square_sum = lax.psum(jnp.sum(gated_out * gated_out, axis=1), "tensor")
    gate_scale = lax.rsqrt(square_sum / DI + EPSILON)[:, None]
    normed_out = (gated_out * gate_scale * gate_gain[layer_index][None, :]).astype(jnp.bfloat16)
    partial_out = jnp.dot(normed_out, out_full, preferred_element_type=jnp.float32)
    new_hidden = hidden + lax.psum(partial_out, "tensor")
    kept_values = (
        norm_pull,
        normed,
        silu_pull,
        gate_silu,
        mixed_out,
        gated_out,
        gate_scale,
        normed_out,
        conv_pull,
        rate_pull,
        summary_pull,
        output_pull,
        span_decay,
        entry_state,
        identity,
        local_width,
        edge_count,
    )
    return (new_hidden, kept_values)


def backward_layer(grad_hidden, weights, small_params, kept_values, layer_index):
    inner_full, rate_full, state_full, out_full = weights
    gate_gain = small_params[8]
    (
        norm_pull,
        normed,
        silu_pull,
        gate_silu,
        mixed_out,
        gated_out,
        gate_scale,
        normed_out,
        conv_pull,
        rate_pull,
        summary_pull,
        output_pull,
        span_decay,
        entry_state,
        identity,
        local_width,
        edge_count,
    ) = kept_values
    seq_rows = normed.shape[0]
    grad_low = grad_hidden.astype(jnp.bfloat16)
    grad_out_weight = jnp.dot(normed_out.T, grad_low, preferred_element_type=jnp.float32)
    grad_normed_out = jnp.dot(grad_low, out_full.T, preferred_element_type=jnp.float32)
    grad_gate_gain = jnp.sum(grad_normed_out * gated_out * gate_scale, axis=0)
    scaled_grad = grad_normed_out * gate_gain[layer_index][None, :]
    inner_sum = lax.psum(jnp.sum(scaled_grad * gated_out, axis=1), "tensor")
    scale_cube = gate_scale * gate_scale * gate_scale
    grad_gated = gate_scale * scaled_grad - gated_out * scale_cube * (inner_sum[:, None] / DI)
    grad_mixed = grad_gated * gate_silu
    grad_gate = silu_pull(grad_gated * mixed_out)[0]
    grad_inputs, grad_keys, grad_queries, grad_rates, grad_decays, grad_entry, grad_skip_gain = (
        output_pull(grad_mixed)
    )
    end_grads = carried_in_2((span_decay, grad_entry), "seq", chain_combine, identity)[1]
    grad_span_decay = jnp.sum(end_grads * entry_state, axis=(1, 2))
    more_inputs, more_keys, more_rates, more_decays = summary_pull((grad_span_decay, end_grads))
    grad_raw, grad_rate_bias, grad_decay_log = rate_pull(
        (grad_rates + more_rates, grad_decays + more_decays)
    )
    grad_activated = jnp.concatenate(
        [(grad_inputs + more_inputs).reshape(seq_rows, -1), grad_keys + more_keys, grad_queries],
        axis=1,
    )
    grad_padded, grad_conv_weight, grad_conv_bias = conv_pull(grad_activated)
    edge_back = shifted(grad_padded[:edge_count], "seq", -1)
    grad_conv_input = grad_padded[edge_count:]
    grad_conv_input = jnp.concatenate(
        [
            grad_conv_input[: seq_rows - edge_count],
            grad_conv_input[seq_rows - edge_count :] + edge_back,
        ],
        axis=0,
    )
    grad_inner_low = jnp.concatenate([grad_gate, grad_conv_input[:, :local_width]], axis=1).astype(
        jnp.bfloat16
    )
    grad_state_raw = grad_conv_input[:, local_width:]
    grad_rate_low = grad_raw.astype(jnp.bfloat16)
    grad_inner_weight = jnp.dot(normed.T, grad_inner_low, preferred_element_type=jnp.float32)
    grad_rate_weight = jnp.dot(normed.T, grad_rate_low, preferred_element_type=jnp.float32)
    grad_state_weight = product(normed.astype(jnp.float32).T, grad_state_raw)
    grad_normed_part = (
        jnp.dot(grad_inner_low, inner_full.T, preferred_element_type=jnp.float32)
        + jnp.dot(grad_rate_low, rate_full.T, preferred_element_type=jnp.float32)
        + product(grad_state_raw, state_full.astype(jnp.float32).T)
    )
    grad_normed, grad_conv_state, grad_bias_state = (
        lax.psum(grad_normed_part.astype(jnp.bfloat16), "tensor").astype(jnp.float32),
        lax.psum(grad_conv_weight[:, local_width:].astype(jnp.bfloat16), "tensor").astype(
            jnp.float32
        ),
        lax.psum(grad_conv_bias[local_width:].astype(jnp.bfloat16), "tensor").astype(jnp.float32),
    )
    grad_hidden_norm, grad_norm_gain = norm_pull(grad_normed)
    layer_grads = (
        grad_inner_weight.reshape(grad_inner_weight.shape[0], 2, local_width),
        grad_rate_weight,
        grad_state_weight,
        grad_out_weight,
        grad_norm_gain,
        grad_conv_weight[:, :local_width],
        grad_conv_bias[:local_width],
        grad_conv_state,
        grad_bias_state,
        grad_rate_bias,
        grad_decay_log,
        grad_skip_gain,
        grad_gate_gain,
    )
    return (grad_hidden + grad_hidden_norm, layer_grads)


def stack_layers(layer_sums, position):
    return jnp.stack([grads_here[position] for grads_here in layer_sums])


def span_body(
    tokens,
    cotangent,
    norm_gain,
    inner_weight,
    rate_weight,
    state_weight,
    conv_inner,
    bias_inner,
    conv_state,
    bias_state,
    rate_bias,
    decay_log,
    skip_gain,
    gate_gain,
    out_weight,
):
    small_params = (
        norm_gain,
        conv_inner,
        bias_inner,
        conv_state,
        bias_state,
        rate_bias,
        decay_log,
        skip_gain,
        gate_gain,
    )
    layer_count = norm_gain.shape[0]
    batch_count = tokens.shape[0]
    results = []
    kept_batches = []
    for batch_index in range(batch_count):
        hidden = tokens[batch_index, 0].astype(jnp.float32)
        kept_layers = []
        for layer_index in range(layer_count):
            weights = gather_layer(inner_weight, rate_weight, state_weight, out_weight, layer_index)
            hidden, kept_values = forward_layer(hidden, weights, small_params, layer_index)
            kept_layers.append(kept_values)
        results.append(hidden)
        kept_batches.append(kept_layers)
    layer_sums = [None] * layer_count
    seq_grads = []
    for batch_index in range(batch_count):
        grad_hidden = cotangent[batch_index, 0].astype(jnp.float32)
        for layer_index in reversed(range(layer_count)):
            weights = gather_layer(inner_weight, rate_weight, state_weight, out_weight, layer_index)
            grad_hidden, layer_grads = backward_layer(
                grad_hidden,
                weights,
                small_params,
                kept_batches[batch_index][layer_index],
                layer_index,
            )
            if layer_sums[layer_index] is None:
                layer_sums[layer_index] = layer_grads
            else:
                layer_sums[layer_index] = tuple(
                    (older + newer for older, newer in zip(layer_sums[layer_index], layer_grads))
                )
        seq_grads.append(grad_hidden)
    shard_inner, shard_rate, shard_out = (
        lax.psum_scatter(
            stack_layers(layer_sums, 0), ("dp", "seq"), scatter_dimension=1, tiled=True
        ),
        lax.psum_scatter(
            stack_layers(layer_sums, 1), ("dp", "seq"), scatter_dimension=1, tiled=True
        ),
        lax.psum_scatter(
            stack_layers(layer_sums, 3), ("dp", "seq"), scatter_dimension=2, tiled=True
        ),
    )
    shard_state = lax.psum_scatter(
        stack_layers(layer_sums, 2), ("dp", "seq", "tensor"), scatter_dimension=1, tiled=True
    )
    summed_small = lax.psum(
        (
            stack_layers(layer_sums, 4),
            stack_layers(layer_sums, 5),
            stack_layers(layer_sums, 6),
            stack_layers(layer_sums, 7),
            stack_layers(layer_sums, 8),
            stack_layers(layer_sums, 9),
            stack_layers(layer_sums, 10),
            stack_layers(layer_sums, 11),
            stack_layers(layer_sums, 12),
        ),
        ("dp", "seq"),
    )
    output = jnp.stack(results)[:, None]
    input_grad = jnp.stack(seq_grads)[:, None]
    return (
        output,
        input_grad,
        summed_small[0],
        shard_inner,
        shard_rate,
        shard_state,
        summed_small[1],
        summed_small[2],
        summed_small[3],
        summed_small[4],
        summed_small[5],
        summed_small[6],
        summed_small[7],
        summed_small[8],
        shard_out,
    )


GROUP = ("seq", "tensor")
LANES = 128
ROWS = 8
BF16, F32 = jnp.bfloat16, jnp.float32


def hop(value, first, second):
    pairs = [
        (place * 2 + core, (place ^ (second if core else first)) * 2 + core)
        for place in range(4)
        for core in range(2)
    ]
    return lax.ppermute(value, GROUP, pairs)


def swap(value):
    return lax.ppermute(value, "tensor", [(0, 1), (1, 0)])


def places():
    place, core = lax.axis_index("seq"), lax.axis_index("tensor")
    return place, core, place ^ (1 + core), place ^ (2 - core), place ^ 3


def put(buffer, block, *index):
    spots = index + (0,) * (buffer.ndim - len(index))
    return lax.dynamic_update_slice(buffer, block.reshape((1,) * len(index) + block.shape), spots)


def pick(array, index, axis=0):
    return lax.dynamic_index_in_dim(array, index, axis, False)


def line_shift(value, axis, step):
    count = lax.axis_size(axis)
    return lax.ppermute(value, axis, [(i, (i + step) % count) for i in range(count)])


def line_place(blocks, columns):
    count, place, rows = lax.axis_size("dp"), lax.axis_index("dp"), blocks[0].shape[0]
    out = jnp.zeros((count * rows, columns), blocks[0].dtype)
    for step, block in enumerate(blocks):
        out = lax.dynamic_update_slice(out, block, ((place - step) % count * rows, 0))
    return out


def line_near(block):
    count = lax.axis_size("dp")
    return jnp.stack([block] + [line_shift(block, "dp", step) for step in range(1, count)])


def line_sum_steps(part):
    count, place = lax.axis_size("dp"), lax.axis_index("dp")
    sent = [part((place + step) % count).astype(BF16) for step in range(1, count)]
    got = [line_shift(value, "dp", step + 1) for step, value in enumerate(sent)]
    token = yield sent
    total = part(place)
    for value in gate(got, token):
        total = total + value.astype(F32)
    return total


def seq_trade(parts):
    place = lax.axis_index("seq")
    out = put(jnp.zeros_like(parts), pick(parts, place), place)
    for turn in (1, 2, 3):
        got = lax.ppermute(pick(parts, place ^ turn), "seq", [(i, i ^ turn) for i in range(4)])
        out = put(out, got, place ^ turn)
    return out


def mesh_sum_steps(value):
    count = lax.axis_size("dp")
    turns = [("seq", 4, 1), ("seq", 4, 2)]
    turns += [("dp", count, 1 << bit) for bit in range(count.bit_length() - 1)]
    for axis, size, turn in turns:
        moved = lax.ppermute(value, axis, [(i, i ^ turn) for i in range(size)])
        token = yield value
        value = value + gate(moved, token)
    return value


def trade_steps(parts):
    place = lax.axis_index("seq")
    sent = [pick(parts, place ^ turn) for turn in (1, 2, 3)]
    got = [
        lax.ppermute(value, "seq", [(i, i ^ turn) for i in range(4)])
        for turn, value in zip((1, 2, 3), sent)
    ]
    token = yield sent
    out = put(jnp.zeros_like(parts), pick(parts, place), place)
    for turn, value in zip((1, 2, 3), gate(got, token)):
        out = put(out, value, place ^ turn)
    return out


def dot(left, right, left_dim=1, right_dim=0):
    return lax.dot_general(
        left, right, (((left_dim,), (right_dim,)), ((), ())), preferred_element_type=F32
    )


def split(value, count):
    pieces = []
    for _ in range(count):
        piece = value.astype(BF16)
        pieces.append(piece)
        value = value - piece.astype(F32)
    return pieces


def exact_left(value, ones, count, right_dim=0):
    rows = value.shape[0]
    stacked = dot(jnp.concatenate(split(value, count), axis=0), ones, 1, right_dim)
    total = stacked[:rows]
    for index in range(1, count):
        total = total + stacked[index * rows : (index + 1) * rows]
    return total


def head_sums(picker, value):
    high, low_part = split(value, 2)
    return dot(picker, high, 1, 1) + dot(picker, low_part, 1, 1)


def front(raw, window, taps, heads, spread, upper, width, state, extra):
    length = raw.shape[0]
    summed = taps[4:5, :] + taps[0:1, :] * window[5 : 5 + length, :]
    for tap in range(1, 4):
        summed = summed + taps[tap : tap + 1, :] * window[5 + tap : 5 + tap + length, :]
    sig = jax.nn.sigmoid(summed)
    activated = summed * sig
    rates = jnp.transpose(raw[:, 2 * width + 2 * state :])[:ROWS] + heads[0:ROWS, :]
    steps = jnp.maximum(rates, 0.0) + jnp.log1p(jnp.exp(-jnp.abs(rates)))
    decays = -jnp.exp(heads[ROWS : 2 * ROWS, :]) * steps
    running = exact_left(decays, upper, 3)
    ending = running[:, length - 1 : length]
    grown = jnp.exp(running)
    tail = jnp.exp(ending - running)
    rows = [steps, running, grown, tail] + extra
    rows.append(jnp.zeros((LANES // 2 - ROWS * len(rows), length), F32))
    rows = jnp.concatenate(rows, axis=0)
    high = rows.astype(BF16).astype(F32)
    halves = jnp.transpose(jnp.concatenate([high, rows - high], axis=0))
    columns = halves[:, : LANES // 2] + halves[:, LANES // 2 :]
    wide = dot(halves.astype(BF16), spread)
    whole_decay = jnp.exp(jnp.broadcast_to(ending, (ROWS, LANES)))
    inputs = activated[:, :width]
    return dict(
        summed=summed,
        sig=sig,
        inputs=inputs,
        keys=activated[:, width : width + state].astype(BF16),
        queries=activated[:, width + state :].astype(BF16),
        rates=rates,
        decays=decays,
        running=running,
        columns=columns,
        steps_wide=wide[:, :width],
        grown_wide=wide[:, width : 2 * width],
        tail_wide=wide[:, 2 * width : 3 * width],
        whole_decay=whole_decay,
    )


def per_row(whole_decay, head_count, head_size):
    return jnp.concatenate(
        [
            jnp.broadcast_to(whole_decay[h : h + 1, :], (head_size, LANES))
            for h in range(head_count)
        ],
        axis=0,
    )


def decay_matrix(parts, h, causal):
    length = causal.shape[0]
    column = parts["columns"][:, ROWS + h : ROWS + h + 1]
    row = parts["running"][h : h + 1, :]
    gap = jnp.broadcast_to(column, (length, length)) - row
    return jnp.exp(jnp.where(causal, gap, -1e30))


def causal_mask(length):
    return lax.broadcasted_iota(jnp.int32, (length, length), 0) >= lax.broadcasted_iota(
        jnp.int32, (length, length), 1
    )


def forward_kernel(
    head_size,
    order_ref,
    raw_first,
    raw_second,
    taps_ref,
    chans_ref,
    heads_ref,
    spread_ref,
    upper_ref,
    value_ref,
    square_ref,
    mixed_ref,
    state_ref,
    carry,
    window_first,
    window_second,
):
    length, width, state = raw_first.shape[0], chans_ref.shape[1], carry.shape[1]
    conv_width = width + 2 * state
    head_count = width // head_size
    pair = LANES // head_size
    step = pl.program_id(0)

    @pl.when(step == 0)
    def _():
        carry[...] = jnp.zeros_like(carry)
        window_first[0:ROWS, :] = jnp.zeros((ROWS, conv_width), F32)

    raws = [raw_first[...], raw_second[...]]
    windows = [window_first, window_second]
    for raw, window in zip(raws, windows):
        window[ROWS : ROWS + length, :] = raw[:, width : width + conv_width].astype(BF16).astype(F32)
    window_second[0:ROWS, :] = window_first[length : length + ROWS, :]
    taps, heads = taps_ref[...], heads_ref[...]
    fronts = [
        front(raw, window, taps, heads, spread_ref[...], upper_ref[...], width, state, [])
        for raw, window in zip(raws, windows)
    ]
    window_first[0:ROWS, :] = window_second[length : length + ROWS, :]
    causal = causal_mask(length)
    lane = lax.broadcasted_iota(jnp.int32, (length, LANES), 1) // head_size
    insides, steppeds = [], []
    for parts in fronts:
        stepped = parts["inputs"] * parts["steps_wide"]
        stepped_low = stepped.astype(BF16)
        scores = dot(parts["queries"], parts["keys"], 1, 1)
        columns = []
        for block in range(head_count // pair):
            source = stepped_low[:, block * LANES : (block + 1) * LANES]
            joined = None
            for k in range(pair):
                mixing = (scores * decay_matrix(parts, block * pair + k, causal)).astype(BF16)
                got = dot(mixing, source)
                joined = got if joined is None else jnp.where(lane == k, got, joined)
            columns.append(joined)
        insides.append(jnp.concatenate(columns, axis=1))
        steppeds.append(stepped)
    updates = [
        dot((stepped * parts["tail_wide"]).astype(BF16), parts["keys"], 0, 0)
        for stepped, parts in zip(steppeds, fronts)
    ]
    before = carry[...]
    for sub, (raw, parts, inside, update) in enumerate(zip(raws, fronts, insides, updates)):
        inputs = parts["inputs"]
        state_ref[sub] = before
        carried = dot(parts["queries"], before.astype(BF16), 1, 1)
        mixed = inside + carried * parts["grown_wide"] + chans_ref[0:1, :] * inputs
        before = per_row(parts["whole_decay"], head_count, head_size) * before + update
        gate_part = raw[:, :width]
        gated = mixed * (gate_part * jax.nn.sigmoid(gate_part))
        rows = pl.ds(pl.multiple_of(order_ref[2 * step + sub] * length, length), length)
        mixed_ref[rows, :] = mixed
        value_ref[rows, :] = (gated * chans_ref[1:2, :]).astype(BF16)
        squares = jnp.sum(gated * gated, axis=1, keepdims=True)
        square_ref[sub * ROWS : (sub + 1) * ROWS, :] = jnp.transpose(
            jnp.broadcast_to(squares, (length, length))
        )[:ROWS]
    carry[...] = before


def backward_kernel(
    head_size,
    inner_count,
    order_ref,
    grad_first,
    grad_second,
    raw_first,
    raw_second,
    past_ref,
    mixed_first,
    mixed_second,
    state_ref,
    token_ref,
    taps_ref,
    chans_ref,
    heads_ref,
    spread_ref,
    upper_ref,
    picker_ref,
    back_ref,
    taps_out,
    chans_out,
    heads_out,
    carry,
    window_first,
    window_second,
    later_first,
    later_second,
):
    length, width, state = raw_first.shape[0], chans_ref.shape[1], carry.shape[1]
    conv_width = width + 2 * state
    head_count = width // head_size
    pair = LANES // head_size
    step, count = pl.program_id(0), pl.num_programs(0)

    @pl.when(step == 0)
    def _():
        carry[...] = jnp.zeros_like(carry)
        later_first[length : length + ROWS, :] = jnp.zeros((ROWS, conv_width), F32)
        taps_out[...] = jnp.zeros_like(taps_out)
        chans_out[...] = jnp.zeros_like(chans_out)
        heads_out[...] = jnp.zeros_like(heads_out)

    raws = [raw_first[...], raw_second[...]]
    windows, laters = [window_first, window_second], [later_first, later_second]
    conv = slice(width, width + conv_width)
    for raw, window in zip(raws, windows):
        window[ROWS : ROWS + length, :] = raw[:, conv].astype(BF16).astype(F32)
    window_first[0:ROWS, :] = window_second[length : length + ROWS, :]
    past = past_ref[:, conv].astype(BF16).astype(F32)
    window_second[0:ROWS, :] = jnp.where(step == count - 1, 0.0, past)
    taps, heads, picker = taps_ref[...], heads_ref[...], picker_ref[...]
    skip, gain = chans_ref[0:1, :], chans_ref[1:2, :]
    causal = causal_mask(length)
    lane = lax.broadcasted_iota(jnp.int32, (length, LANES), 1)
    head_lane = lane // head_size
    places_of = [
        pl.ds(pl.multiple_of(order_ref[2 * count - 1 - 2 * step - sub] * length, length), length)
        for sub in range(2)
    ]

    fronts, held = [], []
    for sub, (raw, window, grad_ref, mixed_ref) in enumerate(
        zip(raws, windows, (grad_first, grad_second), (mixed_first, mixed_second))
    ):
        token = token_ref[(1 - sub) * ROWS : (2 - sub) * ROWS, :]
        parts = front(
            raw, window, taps, heads, spread_ref[...], upper_ref[...], width, state, [token]
        )
        fronts.append(parts)
        inputs = parts["inputs"]
        scale = parts["columns"][:, 4 * ROWS : 4 * ROWS + 1]
        inner = parts["columns"][:, 4 * ROWS + 1 : 4 * ROWS + 2]
        gate_part, mixed = raw[:, :width], mixed_ref[...]
        gate_sig = jax.nn.sigmoid(gate_part)
        gate_silu = gate_part * gate_sig
        gated = mixed * gate_silu
        grad = grad_ref[...]
        gain_term = jnp.sum(grad * (gated * scale), axis=0, keepdims=True)
        grad_gated = scale * (grad * gain) - gated * (scale * scale * scale * inner / inner_count)
        grad_mixed = grad_gated * gate_silu
        back_ref[places_of[sub], :width] = (
            grad_gated * mixed * (gate_sig + gate_silu * (1.0 - gate_sig))
        ).astype(BF16)
        chans_out[0:1, :] += jnp.sum(grad_mixed * inputs, axis=0, keepdims=True)
        chans_out[1:2, :] += gain_term
        held.append(grad_mixed)

    works = []
    for parts, grad_mixed in zip(fronts, held):
        stepped = parts["inputs"] * parts["steps_wide"]
        stepped_low, grad_low = stepped.astype(BF16), grad_mixed.astype(BF16)
        scores = dot(parts["queries"], parts["keys"], 1, 1)
        grad_scores = jnp.zeros((length, length), F32)
        row_sums = jnp.zeros((length, length), F32)
        column_sums, columns = [], []
        for block in range(head_count // pair):
            cut = slice(block * LANES, (block + 1) * LANES)
            source, target = stepped_low[:, cut], grad_low[:, cut]
            joined = None
            for k in range(pair):
                h = block * pair + k
                spread_h = decay_matrix(parts, h, causal)
                own_target = jnp.where(head_lane == k, target, jnp.zeros_like(target))
                pulled = dot(own_target, source, 1, 1) * spread_h
                grad_scores = grad_scores + pulled
                moved = pulled * scores
                row_sums = jnp.where(lane == h, jnp.sum(moved, axis=1, keepdims=True), row_sums)
                column_sums.append(jnp.sum(moved, axis=0, keepdims=True))
                got = dot((scores * spread_h).astype(BF16), target, 0, 0)
                joined = got if joined is None else jnp.where(head_lane == k, got, joined)
            columns.append(joined)
        column_sums.append(jnp.zeros((ROWS - head_count, length), F32))
        differences = jnp.transpose(row_sums)[:ROWS] - jnp.concatenate(column_sums, axis=0)
        works.append((stepped, grad_scores, jnp.concatenate(columns, axis=1), differences))

    after = carry[...]
    row_lane = lax.broadcasted_iota(jnp.int32, (ROWS, length), 1)
    row_head = lax.broadcasted_iota(jnp.int32, (ROWS, length), 0)
    for sub, (parts, grad_mixed, work) in enumerate(zip(fronts, held, works)):
        inputs, keys, queries = parts["inputs"], parts["keys"], parts["queries"]
        stepped, grad_scores, inside, differences = work
        window, later = windows[sub], laters[sub]
        before = state_ref[1 - sub]
        before_low, after_low = before.astype(BF16), after.astype(BF16)
        tail_wide, grown_wide = parts["tail_wide"], parts["grown_wide"]
        through = tail_wide * dot(keys, after_low, 1, 1)
        grad_stepped = inside + through
        ended = stepped * through
        carried = dot(queries, before_low, 1, 1) * grown_wide
        kept = per_row(parts["whole_decay"], head_count, head_size) * after
        kept_sum = jnp.sum(kept * before, axis=1, keepdims=True)
        kept_heads = jnp.concatenate(
            [
                jnp.sum(kept_sum[h * head_size : (h + 1) * head_size], axis=0, keepdims=True)
                for h in range(head_count)
            ]
            + [jnp.zeros((ROWS - head_count, 1), F32)],
            axis=0,
        )
        ended_heads = head_sums(picker, ended)
        grad_running = differences + head_sums(picker, grad_mixed * carried) - ended_heads
        last = jnp.sum(ended_heads, axis=1, keepdims=True) + kept_heads
        grad_running = grad_running + jnp.where(row_lane == length - 1, last, 0.0)
        grad_decays = exact_left(grad_running, upper_ref[...], 3, 1)
        grad_steps = head_sums(picker, inputs * grad_stepped)
        grad_rates = (
            grad_steps - jnp.exp(heads[ROWS : 2 * ROWS, :]) * grad_decays
        ) * jax.nn.sigmoid(parts["rates"])
        grad_rates = jnp.where(row_head < head_count, grad_rates, 0.0)
        heads_out[0:ROWS, :] += grad_rates
        heads_out[ROWS : 2 * ROWS, :] += grad_decays * parts["decays"]
        back_ref[places_of[sub], 2 * width + 2 * state :] = jnp.transpose(
            jnp.concatenate([grad_rates, jnp.zeros((LANES - ROWS, length), F32)], axis=0)
        ).astype(BF16)

        grad_inputs = parts["steps_wide"] * grad_stepped + skip * grad_mixed
        grown_low = (grown_wide * grad_mixed).astype(BF16)
        scores_low = grad_scores.astype(BF16)
        grad_queries = dot(scores_low, keys) + dot(grown_low, before_low)
        grad_keys = dot(scores_low, queries, 0, 0) + dot(
            (stepped * tail_wide).astype(BF16), after_low
        )
        after = kept + dot(grown_low, queries, 0, 0)

        sig, summed = parts["sig"], parts["summed"]
        grad_v = jnp.concatenate([grad_inputs, grad_keys, grad_queries], axis=1) * (
            sig + summed * sig * (1.0 - sig)
        )
        later[0:length, :] = grad_v
        grad_conv = taps[3:4, :] * grad_v
        taps_out[4:5, :] += jnp.sum(grad_v, axis=0, keepdims=True)
        for tap in range(4):
            if tap < 3:
                moved = later[3 - tap : 3 - tap + length, :]
                grad_conv = grad_conv + taps[tap : tap + 1, :] * moved
            taps_out[tap : tap + 1, :] += jnp.sum(
                grad_v * window[5 + tap : 5 + tap + length, :], axis=0, keepdims=True
            )
        laters[1 - sub][length : length + ROWS, :] = grad_v[0:ROWS]
        back_ref[places_of[sub], conv] = grad_conv.astype(BF16)
    carry[...] = after


def tables(width, head_size):
    channel_head = jnp.arange(width)[None, :] // head_size
    rows = jnp.arange(LANES)[:, None]
    spread = jnp.concatenate(
        [rows % (LANES // 2) == channel_head + ROWS * kind for kind in (0, 2, 3)], axis=1
    ).astype(BF16)
    upper = (rows <= jnp.arange(LANES)[None, :]).astype(BF16)
    picker = (jnp.arange(ROWS)[:, None] == channel_head).astype(BF16)
    return spread, upper, picker


def fixed(shape):
    return pl.BlockSpec(shape, lambda i, order: (0,) * len(shape))


def mix_forward(raw, order, small, tabs, head_size, width, state):
    taps, chans, heads = small
    spread, upper, _ = tabs
    tokens, columns = raw.shape
    count = tokens // STRETCH

    def moved(sub):
        return pl.BlockSpec((STRETCH, columns), lambda i, order: (order[2 * i + sub], 0))

    return pl.pallas_call(
        lambda *refs: forward_kernel(head_size, *refs),
        grid_spec=pltpu.PrefetchScalarGridSpec(
            num_scalar_prefetch=1,
            grid=(count // 2,),
            in_specs=[
                moved(0),
                moved(1),
                fixed(taps.shape),
                fixed(chans.shape),
                fixed(heads.shape),
                fixed(spread.shape),
                fixed(upper.shape),
            ],
            out_specs=[
                fixed((tokens, width)),
                pl.BlockSpec((2 * ROWS, LANES), lambda i, order: (i, 0)),
                fixed((tokens, width)),
                pl.BlockSpec((2, width, state), lambda i, order: (i, 0, 0)),
            ],
            scratch_shapes=[
                pltpu.VMEM((width, state), F32),
                pltpu.VMEM((STRETCH + ROWS, width + 2 * state), F32),
                pltpu.VMEM((STRETCH + ROWS, width + 2 * state), F32),
            ],
        ),
        out_shape=[
            jax.ShapeDtypeStruct((tokens, width), BF16),
            jax.ShapeDtypeStruct((count * ROWS, LANES), F32),
            jax.ShapeDtypeStruct((tokens, width), F32),
            jax.ShapeDtypeStruct((count, width, state), F32),
        ],
        compiler_params=pltpu.CompilerParams(
            dimension_semantics=("arbitrary",), vmem_limit_bytes=20 * 2**20
        ),
        cost_estimate=pl.CostEstimate(
            flops=11_000_000_000, bytes_accessed=10_000_000, transcendentals=0
        ),
    )(order, raw, raw, taps, chans, heads, spread, upper)


def mix_backward(grad, raw, mixed, states, token_rows, order, small, tabs, head_size, inner_count):
    taps, chans, heads = small
    spread, upper, picker = tabs
    tokens, columns = raw.shape
    width, state = states.shape[1:]
    count = tokens // STRETCH
    per = STRETCH // ROWS

    steps = count // 2

    def moved(sub, extent):
        return pl.BlockSpec(
            (STRETCH, extent), lambda i, order: (order[count - 1 - 2 * i - sub], 0)
        )

    def past(i, order):
        return (order[jnp.maximum(count - 3 - 2 * i, 0)] * per + per - 1, 0)

    return pl.pallas_call(
        lambda *refs: backward_kernel(head_size, inner_count, *refs),
        grid_spec=pltpu.PrefetchScalarGridSpec(
            num_scalar_prefetch=1,
            grid=(steps,),
            in_specs=[
                moved(0, width),
                moved(1, width),
                moved(0, columns),
                moved(1, columns),
                pl.BlockSpec((ROWS, columns), past),
                moved(0, width),
                moved(1, width),
                pl.BlockSpec((2, width, state), lambda i, order: (steps - 1 - i, 0, 0)),
                pl.BlockSpec((2 * ROWS, LANES), lambda i, order: (steps - 1 - i, 0)),
                fixed(taps.shape),
                fixed(chans.shape),
                fixed(heads.shape),
                fixed(spread.shape),
                fixed(upper.shape),
                fixed(picker.shape),
            ],
            out_specs=[
                fixed((tokens, columns)),
                fixed(taps.shape),
                fixed(chans.shape),
                fixed(heads.shape),
            ],
            scratch_shapes=[pltpu.VMEM((width, state), F32)]
            + [pltpu.VMEM((STRETCH + ROWS, width + 2 * state), F32) for _ in range(4)],
        ),
        out_shape=[
            jax.ShapeDtypeStruct((tokens, columns), BF16),
            jax.ShapeDtypeStruct(taps.shape, F32),
            jax.ShapeDtypeStruct(chans.shape, F32),
            jax.ShapeDtypeStruct(heads.shape, F32),
        ],
        compiler_params=pltpu.CompilerParams(
            dimension_semantics=("arbitrary",), vmem_limit_bytes=24 * 2**20
        ),
        cost_estimate=pl.CostEstimate(
            flops=23_000_000_000, bytes_accessed=16_000_000, transcendentals=0
        ),
    )(
        order,
        grad,
        grad,
        raw,
        raw,
        raw,
        mixed,
        mixed,
        states,
        token_rows,
        taps,
        chans,
        heads,
        spread,
        upper,
        picker,
    )


def small_kernel(layers, heads_here, head_count, state, spot_ref, place_ref, arrived_ref, out_ref):
    share = arrived_ref.shape[1]
    rows = share // layers
    row = lax.broadcasted_iota(jnp.int32, (LANES, LANES), 0)
    lane = lax.broadcasted_iota(jnp.int32, (LANES, LANES), 1)
    chosen = []
    for layer in range(layers):
        source = lane + layer * heads_here + place_ref[0] * head_count
        chosen.append(((row == source) & (lane < head_count)).astype(BF16))
    for index in range(out_ref.shape[1] // share):
        pair = [arrived_ref[spot_ref[2 * index + which]] for which in range(2)]
        own = jnp.where(place_ref[1] == 0, pair[0][:, 2 * state :], pair[1][:, 2 * state :])
        turned = jnp.concatenate([own.astype(F32), jnp.zeros((LANES - share, LANES), F32)], axis=0)
        turned = jnp.transpose(turned)[:share].astype(BF16)
        spot = index * share
        for layer in range(layers):
            cut = slice(layer * rows, (layer + 1) * rows)
            out_ref[layer, spot : spot + rows, : 2 * state] = pair[0][cut, : 2 * state]
            out_ref[layer, spot + rows : spot + share, : 2 * state] = pair[1][cut, : 2 * state]
            out_ref[layer, spot : spot + share, 2 * state :] = dot(turned, chosen[layer]).astype(BF16)


def small_unpack(arrived, order, layers, heads_here, head_count, state):
    line, share, columns = arrived.shape[0] // 8, arrived.shape[1], arrived.shape[2]
    place, core = lax.axis_index("seq"), lax.axis_index("tensor")
    back = (lax.axis_index("dp") - jnp.arange(line)) % line
    spots = (order[None, :] * line + back[:, None]).reshape(-1).astype(jnp.int32)
    scalars = pl.BlockSpec(memory_space=pltpu.SMEM)
    return pl.pallas_call(
        lambda *refs: small_kernel(layers, heads_here, head_count, state, *refs),
        in_specs=[scalars, scalars, pl.BlockSpec(memory_space=pltpu.VMEM)],
        out_shape=jax.ShapeDtypeStruct((layers, line * 4 * share, columns), BF16),
        compiler_params=pltpu.CompilerParams(vmem_limit_bytes=14 * 2**20),
    )(spots, jnp.stack([place, core]).astype(jnp.int32), arrived)


def finish_kernel(
    head_count, state, first_ref, second_ref, first_out, second_out, inner_ref, out_ref, state_ref, rate_ref
):
    width = out_ref.shape[2] // 4
    share = out_ref.shape[1]
    for layer, (ref, more) in enumerate(((first_ref, first_out), (second_ref, second_out))):
        states = jnp.zeros((share, 2 * state), F32)
        rates = []
        for index in range(4):
            value = ref[index].astype(F32)
            spot = slice(index * width, (index + 1) * width)
            inner_ref[layer, 0, :, spot] = value[:, :width]
            inner_ref[layer, 1, :, spot] = value[:, width : 2 * width]
            states = states + value[:, 2 * width : 2 * width + 2 * state]
            rate = jnp.concatenate(
                [value[:, 2 * width + 2 * state :], jnp.zeros((LANES - share, LANES), F32)], axis=0
            )
            rates.append(jnp.transpose(rate)[:head_count, :share])
            out_ref[layer, :, spot] = more[index].astype(F32)
        rate_ref[layer] = jnp.concatenate(rates, axis=0)
        state_ref[layer] = states


def finish(first, second, first_out, second_out, head_count, state, width):
    share = first.shape[1]
    return pl.pallas_call(
        lambda *refs: finish_kernel(head_count, state, *refs),
        out_shape=[
            jax.ShapeDtypeStruct((2, 2, share, 4 * width), F32),
            jax.ShapeDtypeStruct((2, share, 4 * width), F32),
            jax.ShapeDtypeStruct((2, share, 2 * state), F32),
            jax.ShapeDtypeStruct((2, 4 * head_count, share), F32),
        ],
        compiler_params=pltpu.CompilerParams(vmem_limit_bytes=14 * 2**20),
    )(first, second, first_out, second_out)


def norm_scale(hidden):
    return lax.rsqrt(jnp.mean(hidden * hidden, axis=1, keepdims=True) + EPSILON)


PLAN = (
    "v a l ga",
    "gb a v a",
    "b ga gb a",
    "b a b ga",
    "gb a b a",
    "b a b l",
    "a b a b",
    "a b a b",
    "a b a b",
    "a b a b",
    "a b a b",
    "a b oa1 a",
    "b xo a b",
    "a ob1 b a",
    "q ia1 b xo",
    "a b ib1 r",
    "a b oa0 a",
    "b a a b",
    "ob0 y ia0 b",
    "ib0 u a b",
    "a m b y",
    "q m b q",
    "m y b xg",
    "m r m r",
    "xg m u u",
)


def gate(value, token):
    return value if token is None else lax.optimization_barrier((value, token))[0]


def gather_steps(block):
    from_near, from_far = hop(block, 1, 2), hop(block, 2, 1)
    token = yield block
    from_near = gate(from_near, token)
    from_across = hop(from_near, 2, 1)
    token = yield from_near
    four = jnp.stack([block, from_near, gate(from_far, token), gate(from_across, token)])
    twin = swap(four)
    token = yield four
    return jnp.concatenate([four, gate(twin, token)])


def scatter_steps(own, other, tiny=None):
    got = swap(other)
    moved = None if tiny is None else hop(tiny, 1, 2)
    token = yield other
    got = gate(got, token)
    to_far = (own[2:].astype(F32) + got[2:].astype(F32)).astype(BF16)
    from_far = hop(to_far, 2, 1)
    if tiny is not None:
        tiny = tiny + gate(moved, token)
        moved = hop(tiny, 2, 1)
    token = yield to_far
    from_far = gate(from_far, token)
    both = own[:2].astype(F32) + got[:2].astype(F32) + from_far.astype(F32)
    side = both[1].astype(BF16)
    from_near = hop(side, 1, 2)
    if tiny is not None:
        tiny = tiny + gate(moved, token)
        moved = swap(tiny)
    token = yield (side, both[0])
    total = both[0] + gate(from_near, token).astype(F32)
    if tiny is not None:
        tiny = tiny + gate(moved, token)
    return total, tiny


def arrival_order():
    place, core = lax.axis_index("seq"), lax.axis_index("tensor")
    block = jnp.arange(8)
    turn, their = block // 2 ^ place, block % 2
    first = jnp.where(their == 0, turn, jnp.where(turn == 1, 2, jnp.where(turn == 2, 1, turn)))
    return (first + jnp.where(their == core, 0, 4)).astype(jnp.int32)


class Track:
    def __init__(self):
        self.token = None
        self.chains = {}

    def begin(self, name, chain):
        next(chain)
        self.chains[name] = chain

    def run(self, *plan):
        for name in " ".join(plan).split():
            name, _, count = name.partition("*")
            for _ in range(int(count or 1)):
                try:
                    self.token = self.chains[name].send(self.token)
                except StopIteration:
                    pass


def late_gather(store, key, block):
    token = yield None
    store[key] = yield from gather_steps(gate(block, token))


def kept_result(store, key, chain):
    yield None
    store[key] = yield from chain


def together(main, side):
    token = yield (next(main), next(side))
    result, running = None, [True, True]
    while any(running):
        values = []
        for index, chain in enumerate((main, side)):
            if running[index]:
                try:
                    values.append(chain.send(token))
                except StopIteration as stop:
                    running[index] = False
                    result = stop.value if index == 0 else result
        if any(running):
            token = yield tuple(values)
    return result


def sum_steps(value, store, key):
    moved = hop(value, 1, 2)
    token = yield value
    value = value + gate(moved, token)
    moved = hop(value, 2, 1)
    token = yield value
    value = value + gate(moved, token)
    moved = swap(value)
    token = yield value
    store[key] = value + gate(moved, token)


def head_body(
    tokens,
    cotangent,
    norm_gain,
    inner_weight,
    rate_weight,
    state_weight,
    conv_inner,
    bias_inner,
    conv_state,
    bias_state,
    rate_bias,
    decay_log,
    skip_gain,
    gate_gain,
    out_weight,
):
    layers, batches = norm_gain.shape[0], tokens.shape[0]
    model = tokens.shape[3]
    place, core = lax.axis_index("seq"), lax.axis_index("tensor")
    line = lax.axis_size("dp")
    share, half_width = inner_weight.shape[1], inner_weight.shape[3]
    inner_count = half_width * 2
    width = half_width // 4
    head_count = rate_bias.shape[1] // 4
    head_size = width // head_count
    state_share, state = state_weight.shape[1], state_weight.shape[2] // 2
    own_rows = tokens.shape[2] // 2
    length = own_rows * 8
    conv_width = width + 2 * state
    columns = 2 * width + 2 * state + LANES
    heads_here = rate_weight.shape[2]
    tabs = tables(width, head_size)

    def own(array):
        return lax.dynamic_slice_in_dim(array, core * own_rows, own_rows, 0)

    def quarter(array, count):
        return lax.dynamic_slice_in_dim(array, place * count, count, array.ndim - 1)

    def out_share(layer):
        turned = out_weight[layer].T.reshape(share, 4, width)
        return turned.transpose(1, 0, 2)

    def inner_share(layer):
        cut = inner_weight[layer].reshape(share, 2, 4, width)
        return cut.transpose(2, 0, 1, 3).reshape(4, share, 2 * width)

    def first_for(taker):
        cut = lax.dynamic_slice(inner_weight[0], (0, 0, taker * width), (share, 2, width))
        return jnp.concatenate([cut[:, 0], cut[:, 1]], axis=1)

    out_weights, in_weights = {}, {}

    def first_out():
        token = yield None
        traded = yield from trade_steps(gate(out_share(0), token))
        traded = traded.reshape(4 * share, width)
        got = [line_shift(traded, "dp", step) for step in range(1, line)]
        token = yield traded
        out_weights[0] = line_place([traded] + gate(got, token), width)

    def later(layer):
        token = yield None
        mixed_share = jnp.concatenate([inner_share(layer), out_share(layer)], axis=2)
        traded = yield from trade_steps(gate(mixed_share, token))
        full = lax.all_gather(traded.reshape(4 * share, -1), "dp").reshape(model, -1)
        token = yield traded
        full = gate(full, token)
        out_weights[layer] = full[:, 2 * width :]
        in_weights[layer] = jnp.concatenate([full[:, : 2 * width], small_full[layer]], axis=1)
        yield in_weights[layer]

    first = put(jnp.zeros((4, share, 2 * width), BF16), first_for(place), place)
    first_sent = [first_for(place ^ turn) for turn in (1, 2, 3)]
    for turn, value in zip((1, 2, 3), first_sent):
        pairs = [(i, i ^ turn) for i in range(4)]
        first = put(first, lax.ppermute(value, "seq", pairs), place ^ turn)
    first = first.reshape(4 * share, 2 * width)
    rate_rows = rate_weight.transpose(0, 2, 1).reshape(layers * heads_here, share)
    rate_rows = jnp.pad(rate_rows, ((0, share - layers * heads_here), (0, LANES - share)))
    small_share = jnp.concatenate([state_weight.reshape(share, 2 * state), rate_rows], axis=1)
    small_near = line_near(small_share)

    smalls = []

    def prepare():
        token = yield None
        given = (conv_inner, conv_state, bias_inner, bias_state, skip_gain, gate_gain, rate_bias, decay_log)
        (
            conv_inner_,
            conv_state_,
            bias_inner_,
            bias_state_,
            skip_gain_,
            gate_gain_,
            rate_bias_,
            decay_log_,
        ) = gate(given, token)
        for layer in range(layers):
            taps = jnp.concatenate([quarter(conv_inner_[layer], width), conv_state_[layer]], axis=1)
            bias = jnp.concatenate([quarter(bias_inner_[layer], width), bias_state_[layer]])
            taps = jnp.concatenate([taps, bias[None], jnp.zeros((3, conv_width), F32)], axis=0)
            skip = jnp.repeat(quarter(skip_gain_[layer], head_count), head_size)
            chans = jnp.stack([skip, quarter(gate_gain_[layer], width)])
            chans = jnp.concatenate([chans, jnp.zeros((ROWS - 2, width), F32)], axis=0)
            heads = jnp.stack(
                [quarter(rate_bias_[layer], head_count), quarter(decay_log_[layer], head_count)]
            )
            heads = jnp.pad(heads, ((0, 0), (0, ROWS - head_count))).reshape(2 * ROWS, 1)
            smalls.append((taps, chans, jnp.broadcast_to(heads, (2 * ROWS, LANES))))
        yield smalls

    order = arrival_order()
    track = Track()
    track.token = (first_sent, small_share)
    hiddens = [own(tokens[batch, 0]).astype(F32) for batch in range(batches)]
    row_scales, normed_all, whole = [], {}, {}
    for batch in range(batches):
        row_scales.append(norm_scale(hiddens[batch]))
        normed = (hiddens[batch] * row_scales[batch] * norm_gain[0][None, :]).astype(BF16)
        normed = gate(normed, track.token)
        track.begin(str(batch), kept_result(normed_all, (0, batch), gather_steps(normed)))
    track.begin("s", kept_result(whole, "small", gather_steps(gate(small_near, first))))
    track.begin("p", prepare())
    grads, grad_all = [], {}
    for batch, name in enumerate(("ga", "gb")):
        low_part = own(gate(cotangent[batch, 0], first_sent))
        grads.append(low_part.astype(F32))
        track.begin(name, late_gather(grad_all, (layers - 1, batch), low_part))
    track.run("0 1")
    first_got = [line_shift(first, "dp", step) for step in range(1, line)]
    track.token = first
    track.run("s")
    track.token = first_got[0]
    track.run("0 1 s p", "0 1 s ga", "gb 0 1 s")
    track.begin("v", first_out())
    track.begin("l", later(1))
    track.run("v l")
    first_full = line_place(gate([first] + first_got, track.token), columns)
    small_full = small_unpack(
        whole["small"].reshape(-1, share, small_share.shape[1]),
        order,
        layers,
        heads_here,
        head_count,
        state,
    )
    in_weights[0] = lax.dynamic_update_slice(first_full, small_full[0], (0, 2 * width))
    track.token = first_full
    gradients, inners, terms, outputs = {}, {}, {}, {}

    def inner_products(grad_low, summed):
        inner = jnp.sum(grad_low.astype(F32) * summed, axis=1)
        return put(jnp.zeros((8, own_rows), F32), inner, place * 2 + core)

    moves = order[None, :] == jnp.arange(8)[:, None]

    def halves_of(value, weight):
        half = length // 2
        other = dot(value[half:], weight, 1, 1).astype(BF16)
        return (
            dot(value[:half], weight, 1, 1).astype(BF16).reshape(4, own_rows, model),
            other.reshape(4, own_rows, model),
        )

    def batch_chain(batch):
        token = yield None
        hidden, row_scale = hiddens[batch], row_scales[batch]
        normed = normed_all[0, batch]
        kept = {}
        for layer in range(layers):
            normed = normed.reshape(length, model)
            raw = dot(gate(normed, token), in_weights[layer])
            token = yield raw
            value, squares, mixed, states = mix_forward(
                gate(raw, token), order, smalls[layer], tabs, head_size, width, state
            )
            token = yield value
            halves = halves_of(gate(value, token), out_weights[layer])
            summed, squares = yield from scatter_steps(
                *halves, squares.reshape(-1, ROWS, LANES)[:, 0]
            )
            scales = lax.rsqrt(squares / inner_count + EPSILON)
            flat_scales = scales.reshape(8, own_rows)
            own_scale = pick(flat_scales, place * 2 + core)[:, None]
            arrived = jnp.sum(jnp.where(moves[:, :, None], flat_scales[None], 0.0), axis=1)
            normed_out = (value.astype(F32) * arrived.reshape(length, 1)).astype(BF16)
            kept[layer] = (hidden, row_scale, normed, raw, mixed, states, summed, scales, normed_out)
            hidden = hidden + own_scale * summed
            if layer + 1 < layers:
                row_scale = norm_scale(hidden)
                normed = (hidden * row_scale * norm_gain[layer + 1][None, :]).astype(BF16)
                normed = yield from gather_steps(normed)
                token = None
        outputs[batch] = hidden
        grad_hidden = grads[batch]
        top_inner = inner_products(grad_hidden.astype(BF16), kept[layers - 1][6])
        yield from sum_steps(top_inner, inners, (layers - 1, batch))
        token = None
        for layer in reversed(range(layers)):
            hidden, row_scale, normed, raw, mixed, states, summed, scales, normed_out = kept[layer]
            whole_grad = grad_all[layer, batch].reshape(length, model)
            terms[layer, batch] = [whole_grad, normed_out, normed, None]
            grad_value = dot(gate(whole_grad, token), out_weights[layer])
            token = yield grad_value
            token_rows = jnp.stack([scales, inners[layer, batch].reshape(-1, LANES)], axis=1)
            token_rows = jnp.pad(token_rows, ((0, 0), (0, ROWS - 2), (0, 0)))
            back, taps_grad, chans_grad, heads_grad = mix_backward(
                gate(grad_value, token),
                raw,
                mixed,
                states,
                token_rows.reshape(-1, LANES),
                order,
                smalls[layer],
                tabs,
                head_size,
                inner_count,
            )
            terms[layer, batch][3] = back
            token = yield back
            halves = halves_of(gate(back, token), in_weights[layer])
            gain_term = sum(
                jnp.sum(part.reshape(-1, model).astype(F32) * cut.astype(F32), axis=0)
                for part, cut in zip(halves, (normed[: length // 2], normed[length // 2 :]))
            )
            gradients[layer, batch] = (
                taps_grad,
                chans_grad,
                heads_grad,
                gain_term / norm_gain[layer],
            )
            grad_normed, _ = yield from scatter_steps(*halves)
            weighted = grad_normed * norm_gain[layer][None, :]
            mean = jnp.mean(weighted * hidden, axis=1, keepdims=True)
            grad_hidden = (
                grad_hidden
                + row_scale * weighted
                - hidden * (row_scale * row_scale * row_scale) * mean
            )
            if layer > 0:
                grad_low = grad_hidden.astype(BF16)
                inner = inner_products(grad_low, kept[layer - 1][6])
                grad_all[layer - 1, batch] = yield from together(
                    gather_steps(grad_low), sum_steps(inner, inners, (layer - 1, batch))
                )
                token = None
        grads[batch] = grad_hidden
        yield grad_hidden

    totals = {}

    def term(key, layer, batch, left, right):
        value = dot(left, right, 0, 0)
        if batch > 0:
            value = value + totals[key, layer, batch - 1]
        totals[key, layer, batch] = value.astype(BF16) if batch == batches - 1 else value
        return totals[key, layer, batch]

    def out_term(layer, batch):
        token = yield None
        whole_grad, normed_out, _, _ = terms[layer, batch]
        yield term("out", layer, batch, gate(whole_grad, token), normed_out)

    def in_term(layer, batch):
        token = yield None
        _, _, normed, back = terms[layer, batch]
        yield term("in", layer, batch, gate(normed, token), back)

    rows = 4 * share

    def line_cut(array, index):
        return lax.dynamic_slice_in_dim(array, index * rows, rows, 0)

    def out_part(layer):
        total = totals["out", layer, batches - 1]
        return lambda index: line_cut(total, index).astype(F32)

    shares = {}

    def line_sum(total):
        return lax.psum_scatter(total, "dp", scatter_dimension=0, tiled=True)

    def first_sums(key):
        yield None
        if key == "out":
            total = yield from line_sum_steps(out_part(0))
            total = total.astype(BF16)
        else:
            packed = totals["in", 0, batches - 1]
            total = line_sum(packed)
            token = yield packed
            total = gate(total, token)
        shares[key, 0] = yield from trade_steps(total.reshape(4, share, -1))

    def later_sums(key, layer):
        token = yield None
        packed = totals[key, layer, batches - 1]
        total = line_sum(gate(packed, token))
        token = yield packed
        shares[key, layer] = yield from trade_steps(gate(total, token).reshape(4, share, -1))
        yield shares[key, layer]

    def both_cores(values, store, key):
        yield None
        others = [swap(value) for value in values()]
        token = yield values()
        both = []
        for value, other in zip(values(), gate(others, token)):
            first = jnp.where(core == 0, value, other)
            second = jnp.where(core == 0, other, value)
            both.append(jnp.concatenate([first, second], axis=0))
        store[key] = jnp.stack(both)[:, None]
        yield store[key]

    def small_sums():
        yield None
        flats = []
        for layer in range(layers):
            taps_grad, chans_grad, heads_grad, gain_term = (
                sum(values) for values in zip(*(gradients[layer, batch] for batch in range(batches)))
            )
            both = jnp.concatenate([gain_term, taps_grad[:5, width:].reshape(-1)])
            head_rows = jnp.stack(
                [
                    jnp.sum(heads_grad[:ROWS], axis=1)[:head_count],
                    jnp.sum(heads_grad[ROWS:], axis=1)[:head_count],
                    jnp.sum(chans_grad[0].reshape(head_count, head_size), axis=1),
                ]
            )
            flat = jnp.concatenate(
                [
                    both,
                    slot(taps_grad[:5, :width], width).reshape(-1),
                    slot(chans_grad[1], width),
                    slot(head_rows, head_count).reshape(-1),
                ]
            )
            flats.append(jnp.pad(flat, (0, -flat.shape[0] % LANES)))
        flat = jnp.stack(flats)
        shared = model + 10 * state
        moved = swap(flat[:, :shared])
        token = yield flat
        flat = lax.dynamic_update_slice(flat, flat[:, :shared] + gate(moved, token), (0, 0))
        finished["flat"] = yield from mesh_sum_steps(flat)

    def slot(array, count):
        shape = array.shape[:-1] + (4 * count,)
        spots = (0,) * (array.ndim - 1) + (place * count,)
        return lax.dynamic_update_slice(jnp.zeros(shape, F32), array, spots)

    finished = {}
    for batch, name in enumerate("ab"):
        track.begin(name, batch_chain(batch))
        for layer in range(layers):
            track.begin(f"o{name}{layer}", out_term(layer, batch))
            track.begin(f"i{name}{layer}", in_term(layer, batch))
    track.begin("y", first_sums("out"))
    track.begin("u", first_sums("in"))
    track.begin("r", later_sums("in", 1))
    track.begin("q", later_sums("out", 1))
    track.begin("xo", both_cores(lambda: [outputs[0], outputs[1]], finished, "output"))
    track.begin("xg", both_cores(lambda: [grads[0], grads[1]], finished, "input_grad"))
    track.begin("m", small_sums())
    track.run(*PLAN)

    inner_grad, out_grad, state_terms, rate_grad = finish(
        shares["in", 0],
        shares["in", 1],
        shares["out", 0],
        shares["out", 1],
        head_count,
        state,
        width,
    )
    state_terms = state_terms.reshape(layers, 2, state_share, 2 * state)
    state_grad = pick(state_terms, core, 1) + swap(pick(state_terms, 1 - core, 1))
    flat = finished["flat"]
    taken, small_out = 0, []
    for shape in ((model,), (5, 2 * state), (5, half_width), (half_width,), (3, 4 * head_count)):
        size = 1
        for extent in shape:
            size *= extent
        small_out.append(flat[:, taken : taken + size].reshape((layers,) + shape))
        taken += size

    return (
        finished["output"],
        finished["input_grad"],
        small_out[0],
        inner_grad.transpose(0, 2, 1, 3),
        rate_grad.transpose(0, 2, 1),
        state_grad,
        small_out[2][:, :4],
        small_out[2][:, 4],
        small_out[1][:, :4],
        small_out[1][:, 4],
        small_out[4][:, 0],
        small_out[4][:, 1],
        small_out[4][:, 2],
        small_out[3],
        out_grad.transpose(0, 2, 1),
    )


def by_heads(mesh, tokens, inner_weight, rate_bias, conv_state, state_weight):
    place_count, core_count, line = mesh.shape["seq"], mesh.shape["tensor"], mesh.shape["dp"]
    if place_count != 4 or core_count != 2:
        return False
    heads, inner = rate_bias.shape[1], inner_weight.shape[3]
    rows = tokens.shape[2] // 8
    return (
        tokens.shape[1] == line
        and tokens.shape[2] % 8 == 0
        and rows == STRETCH
        and tokens.shape[0] == 2
        and line >= 2
        and inner_weight.shape[0] == 2
        and heads % 8 == 0
        and heads // 8 <= ROWS
        and (inner // 8) % LANES == 0
        and LANES % (inner // heads) == 0
        and conv_state.shape[1] == 4
        and state_weight.shape[2] == 2 * LANES
        and inner_weight.shape[1] % (line * 4 * 32) == 0
    )


def solution(mesh):
    in_specs = (
        P(None, "dp", "seq", None),
        P(None, "dp", "seq", None),
        P(),
        P(None, ("dp", "seq"), None, "tensor"),
        P(None, ("dp", "seq"), "tensor"),
        P(None, ("dp", "seq", "tensor"), None),
        P(None, None, "tensor"),
        P(None, "tensor"),
        P(),
        P(),
        P(None, "tensor"),
        P(None, "tensor"),
        P(None, "tensor"),
        P(None, "tensor"),
        P(None, "tensor", ("dp", "seq")),
    )
    out_specs = (
        P(None, "dp", "seq", None),
        P(None, "dp", "seq", None),
        P(),
        P(None, ("dp", "seq"), None, "tensor"),
        P(None, ("dp", "seq"), "tensor"),
        P(None, ("dp", "seq", "tensor"), None),
        P(None, None, "tensor"),
        P(None, "tensor"),
        P(),
        P(),
        P(None, "tensor"),
        P(None, "tensor"),
        P(None, "tensor"),
        P(None, "tensor"),
        P(None, "tensor", ("dp", "seq")),
    )
    def run(*arrays):
        by_name = (arrays[0], arrays[3], arrays[10], arrays[8], arrays[5])
        chosen = head_body if by_heads(mesh, *by_name) else span_body
        return jax.shard_map(
            chosen, mesh=mesh, in_specs=in_specs, out_specs=out_specs, check_vma=False
        )(*arrays)

    return run
```

```python
import jax
import jax.numpy as jnp
from jax import lax
from jax.experimental import pallas as pl
from jax.experimental.pallas import tpu as pltpu
from jax.sharding import PartitionSpec as P

DI = 3072
STRETCH = 128


EPSILON = 1e-05
HIGHEST = lax.Precision.HIGHEST


def shifted(value, axis, steps):
    count = lax.axis_size(axis)
    leading, last = (max(0, -steps), min(count, count - steps))
    return lax.ppermute(value, axis, [(source, source + steps) for source in range(leading, last)])


def carried_in(array, axis, combine, identity):
    length, place = (lax.axis_size(axis), lax.axis_index(axis))
    everything = jax.tree.map(
        lambda part, kind: lax.all_gather(part.astype(kind), axis),
        array,
        (jnp.bfloat16, jnp.bfloat16),
    )
    start = jax.tree.map(
        lambda part, zero: jnp.broadcast_to(jnp.asarray(zero, part.dtype), part.shape),
        array,
        identity,
    )

    def turn(k, before):
        reached = k < place
        new = combine(
            before, jax.tree.map(lambda part, own: part[k].astype(own.dtype), everything, array)
        )
        return jax.tree.map(lambda a, b: jnp.where(reached, a, b), new, before)

    return lax.fori_loop(0, length, turn, start)


def carried_in_2(array, axis, join, neutral):
    count = lax.axis_size(axis)
    place = lax.axis_index(axis)
    ahead = count - 1 - place
    gathered = jax.tree.map(
        lambda a, kind: lax.all_gather(a.astype(kind), axis),
        array,
        jax.tree.map(lambda a: jnp.bfloat16 if a.dtype == jnp.float32 else a.dtype, array),
    )
    state = jax.tree.map(lambda a, e: jnp.zeros_like(a) + jnp.asarray(e, a.dtype), array, neutral)

    def one(turn, state):
        source = count - 1 - turn
        return join(
            state,
            jax.tree.map(
                lambda a, own: lax.dynamic_index_in_dim(a, source, 0, False).astype(own.dtype),
                gathered,
                array,
            ),
        )

    return lax.fori_loop(0, ahead, one, state)


def product(left_side, right_side):
    return jnp.dot(left_side, right_side, precision=HIGHEST, preferred_element_type=jnp.float32)


def conv_silu(padded, weight, conv_bias):
    conv_width = weight.shape[0]
    out_rows = padded.shape[0] - conv_width + 1
    summed = conv_bias[None, :] + weight[0][None, :] * padded[0:out_rows]
    for offset in range(1, conv_width):
        summed = summed + weight[offset][None, :] * padded[offset : offset + out_rows]
    return jax.nn.silu(summed)


def block_step(carry_state, pieces):
    inputs, keys_b, queries_c, step_rates, decays = pieces
    running = jnp.cumsum(decays, axis=0)
    block_len = inputs.shape[0]
    causal = jnp.arange(block_len)[:, None] >= jnp.arange(block_len)[None, :]
    spread = running.T[:, :, None] - running.T[:, None, :]
    weights = jnp.exp(jnp.where(causal[None, :, :], spread, -jnp.inf))
    scores = product(queries_c, keys_b.T)
    mixing = scores[None, :, :] * weights * step_rates.T[:, None, :]
    inside = jnp.einsum("hts,shp->thp", mixing, inputs, precision=HIGHEST)
    carried = (
        jnp.einsum("tn,hpn->thp", queries_c, carry_state, precision=HIGHEST)
        * jnp.exp(running)[:, :, None]
    )
    tail_weight = jnp.exp(running[-1][None, :] - running) * step_rates
    update = jnp.einsum("shp,sn->hpn", tail_weight[:, :, None] * inputs, keys_b, precision=HIGHEST)
    return (jnp.exp(running[-1])[:, None, None] * carry_state + update, inside + carried)


def state_step(carry_state, pieces):
    inputs, keys_b, step_rates, decays = pieces
    running = jnp.cumsum(decays, axis=0)
    tail_weight = jnp.exp(running[-1][None, :] - running) * step_rates
    update = jnp.einsum("shp,sn->hpn", tail_weight[:, :, None] * inputs, keys_b, precision=HIGHEST)
    return (jnp.exp(running[-1])[:, None, None] * carry_state + update, None)


def to_blocks(values):
    return values.reshape((values.shape[0] // STRETCH, STRETCH) + values.shape[1:])


def span_summary(inputs, keys_b, step_rates, decays):
    zero_state = jnp.zeros((inputs.shape[1], inputs.shape[2], keys_b.shape[1]), jnp.float32)
    end_state, _ = lax.scan(
        state_step,
        zero_state,
        (to_blocks(inputs), to_blocks(keys_b), to_blocks(step_rates), to_blocks(decays)),
    )
    return (jnp.exp(jnp.sum(decays, axis=0)), end_state)


def span_output(inputs, keys_b, queries_c, step_rates, decays, entry_state, skip_gain):
    _, block_out = lax.scan(
        block_step,
        entry_state,
        (
            to_blocks(inputs),
            to_blocks(keys_b),
            to_blocks(queries_c),
            to_blocks(step_rates),
            to_blocks(decays),
        ),
    )
    mixed_out = block_out.reshape(inputs.shape) + skip_gain[None, :, None] * inputs
    return mixed_out.reshape(inputs.shape[0], -1)


def rate_piece(rate_raw, rate_bias, decay_log):
    step_rates = jax.nn.softplus(rate_raw + rate_bias[None, :])
    return (step_rates, -jnp.exp(decay_log)[None, :] * step_rates)


def norm_piece(hidden, norm_gain):
    row_scale = lax.rsqrt(jnp.mean(hidden * hidden, axis=1, keepdims=True) + EPSILON)
    return hidden * row_scale * norm_gain[None, :]


def chain_combine(earlier, following):
    return (earlier[0] * following[0], following[1] + following[0][:, None, None] * earlier[1])


def gather_layer(inner_weight, rate_weight, state_weight, out_weight, layer_index):
    inner_full, rate_full, out_full = (
        lax.all_gather(inner_weight[layer_index], ("dp", "seq"), axis=0, tiled=True),
        lax.all_gather(rate_weight[layer_index], ("dp", "seq"), axis=0, tiled=True),
        lax.all_gather(out_weight[layer_index], ("dp", "seq"), axis=1, tiled=True),
    )
    state_full = lax.all_gather(
        state_weight[layer_index], ("dp", "seq", "tensor"), axis=0, tiled=True
    )
    return (inner_full.reshape(inner_full.shape[0], -1), rate_full, state_full, out_full)


def forward_layer(hidden, weights, small_params, layer_index):
    inner_full, rate_full, state_full, out_full = weights
    (
        norm_gain,
        conv_inner,
        bias_inner,
        conv_state,
        bias_state,
        rate_bias,
        decay_log,
        skip_gain,
        gate_gain,
    ) = small_params
    seq_rows = hidden.shape[0]
    normed_full, norm_pull = jax.vjp(norm_piece, hidden, norm_gain[layer_index])
    normed = normed_full.astype(jnp.bfloat16)
    gate_inner = jnp.dot(normed, inner_full, preferred_element_type=jnp.float32)
    rate_raw = jnp.dot(normed, rate_full, preferred_element_type=jnp.float32)
    state_raw = jnp.dot(normed, state_full, preferred_element_type=jnp.float32)
    local_width = gate_inner.shape[1] // 2
    gate_part = gate_inner[:, :local_width]
    conv_input = jnp.concatenate([gate_inner[:, local_width:], state_raw], axis=1).astype(
        jnp.bfloat16
    )
    edge_count = conv_inner.shape[1] - 1
    edge_rows = shifted(conv_input[seq_rows - edge_count :], "seq", 1)
    padded = jnp.concatenate([edge_rows, conv_input], axis=0).astype(jnp.float32)
    conv_weight = jnp.concatenate([conv_inner[layer_index], conv_state[layer_index]], axis=1)
    conv_bias = jnp.concatenate([bias_inner[layer_index], bias_state[layer_index]])
    activated, conv_pull = jax.vjp(conv_silu, padded, conv_weight, conv_bias)
    state_size = state_raw.shape[1] // 2
    head_count = rate_bias.shape[1]
    inputs = activated[:, :local_width].reshape(seq_rows, head_count, local_width // head_count)
    keys_b = activated[:, local_width : local_width + state_size]
    queries_c = activated[:, local_width + state_size :]
    (step_rates, decays), rate_pull = jax.vjp(
        rate_piece, rate_raw, rate_bias[layer_index], decay_log[layer_index]
    )
    (span_decay, span_state), summary_pull = jax.vjp(
        span_summary, inputs, keys_b, step_rates, decays
    )
    identity = (jnp.ones_like(span_decay), jnp.zeros_like(span_state))
    entry_state = carried_in((span_decay, span_state), "seq", chain_combine, identity)[1]
    mixed_out, output_pull = jax.vjp(
        span_output,
        inputs,
        keys_b,
        queries_c,
        step_rates,
        decays,
        entry_state,
        skip_gain[layer_index],
    )
    gate_silu, silu_pull = jax.vjp(jax.nn.silu, gate_part)
    gated_out = mixed_out * gate_silu
    square_sum = lax.psum(jnp.sum(gated_out * gated_out, axis=1), "tensor")
    gate_scale = lax.rsqrt(square_sum / DI + EPSILON)[:, None]
    normed_out = (gated_out * gate_scale * gate_gain[layer_index][None, :]).astype(jnp.bfloat16)
    partial_out = jnp.dot(normed_out, out_full, preferred_element_type=jnp.float32)
    new_hidden = hidden + lax.psum(partial_out, "tensor")
    kept_values = (
        norm_pull,
        normed,
        silu_pull,
        gate_silu,
        mixed_out,
        gated_out,
        gate_scale,
        normed_out,
        conv_pull,
        rate_pull,
        summary_pull,
        output_pull,
        span_decay,
        entry_state,
        identity,
        local_width,
        edge_count,
    )
    return (new_hidden, kept_values)


def backward_layer(grad_hidden, weights, small_params, kept_values, layer_index):
    inner_full, rate_full, state_full, out_full = weights
    gate_gain = small_params[8]
    (
        norm_pull,
        normed,
        silu_pull,
        gate_silu,
        mixed_out,
        gated_out,
        gate_scale,
        normed_out,
        conv_pull,
        rate_pull,
        summary_pull,
        output_pull,
        span_decay,
        entry_state,
        identity,
        local_width,
        edge_count,
    ) = kept_values
    seq_rows = normed.shape[0]
    grad_low = grad_hidden.astype(jnp.bfloat16)
    grad_out_weight = jnp.dot(normed_out.T, grad_low, preferred_element_type=jnp.float32)
    grad_normed_out = jnp.dot(grad_low, out_full.T, preferred_element_type=jnp.float32)
    grad_gate_gain = jnp.sum(grad_normed_out * gated_out * gate_scale, axis=0)
    scaled_grad = grad_normed_out * gate_gain[layer_index][None, :]
    inner_sum = lax.psum(jnp.sum(scaled_grad * gated_out, axis=1), "tensor")
    scale_cube = gate_scale * gate_scale * gate_scale
    grad_gated = gate_scale * scaled_grad - gated_out * scale_cube * (inner_sum[:, None] / DI)
    grad_mixed = grad_gated * gate_silu
    grad_gate = silu_pull(grad_gated * mixed_out)[0]
    grad_inputs, grad_keys, grad_queries, grad_rates, grad_decays, grad_entry, grad_skip_gain = (
        output_pull(grad_mixed)
    )
    end_grads = carried_in_2((span_decay, grad_entry), "seq", chain_combine, identity)[1]
    grad_span_decay = jnp.sum(end_grads * entry_state, axis=(1, 2))
    more_inputs, more_keys, more_rates, more_decays = summary_pull((grad_span_decay, end_grads))
    grad_raw, grad_rate_bias, grad_decay_log = rate_pull(
        (grad_rates + more_rates, grad_decays + more_decays)
    )
    grad_activated = jnp.concatenate(
        [(grad_inputs + more_inputs).reshape(seq_rows, -1), grad_keys + more_keys, grad_queries],
        axis=1,
    )
    grad_padded, grad_conv_weight, grad_conv_bias = conv_pull(grad_activated)
    edge_back = shifted(grad_padded[:edge_count], "seq", -1)
    grad_conv_input = grad_padded[edge_count:]
    grad_conv_input = jnp.concatenate(
        [
            grad_conv_input[: seq_rows - edge_count],
            grad_conv_input[seq_rows - edge_count :] + edge_back,
        ],
        axis=0,
    )
    grad_inner_low = jnp.concatenate([grad_gate, grad_conv_input[:, :local_width]], axis=1).astype(
        jnp.bfloat16
    )
    grad_state_raw = grad_conv_input[:, local_width:]
    grad_rate_low = grad_raw.astype(jnp.bfloat16)
    grad_inner_weight = jnp.dot(normed.T, grad_inner_low, preferred_element_type=jnp.float32)
    grad_rate_weight = jnp.dot(normed.T, grad_rate_low, preferred_element_type=jnp.float32)
    grad_state_weight = product(normed.astype(jnp.float32).T, grad_state_raw)
    grad_normed_part = (
        jnp.dot(grad_inner_low, inner_full.T, preferred_element_type=jnp.float32)
        + jnp.dot(grad_rate_low, rate_full.T, preferred_element_type=jnp.float32)
        + product(grad_state_raw, state_full.astype(jnp.float32).T)
    )
    grad_normed, grad_conv_state, grad_bias_state = (
        lax.psum(grad_normed_part.astype(jnp.bfloat16), "tensor").astype(jnp.float32),
        lax.psum(grad_conv_weight[:, local_width:].astype(jnp.bfloat16), "tensor").astype(
            jnp.float32
        ),
        lax.psum(grad_conv_bias[local_width:].astype(jnp.bfloat16), "tensor").astype(jnp.float32),
    )
    grad_hidden_norm, grad_norm_gain = norm_pull(grad_normed)
    layer_grads = (
        grad_inner_weight.reshape(grad_inner_weight.shape[0], 2, local_width),
        grad_rate_weight,
        grad_state_weight,
        grad_out_weight,
        grad_norm_gain,
        grad_conv_weight[:, :local_width],
        grad_conv_bias[:local_width],
        grad_conv_state,
        grad_bias_state,
        grad_rate_bias,
        grad_decay_log,
        grad_skip_gain,
        grad_gate_gain,
    )
    return (grad_hidden + grad_hidden_norm, layer_grads)


def stack_layers(layer_sums, position):
    return jnp.stack([grads_here[position] for grads_here in layer_sums])


def span_body(
    tokens,
    cotangent,
    norm_gain,
    inner_weight,
    rate_weight,
    state_weight,
    conv_inner,
    bias_inner,
    conv_state,
    bias_state,
    rate_bias,
    decay_log,
    skip_gain,
    gate_gain,
    out_weight,
):
    small_params = (
        norm_gain,
        conv_inner,
        bias_inner,
        conv_state,
        bias_state,
        rate_bias,
        decay_log,
        skip_gain,
        gate_gain,
    )
    layer_count = norm_gain.shape[0]
    batch_count = tokens.shape[0]
    results = []
    kept_batches = []
    for batch_index in range(batch_count):
        hidden = tokens[batch_index, 0].astype(jnp.float32)
        kept_layers = []
        for layer_index in range(layer_count):
            weights = gather_layer(inner_weight, rate_weight, state_weight, out_weight, layer_index)
            hidden, kept_values = forward_layer(hidden, weights, small_params, layer_index)
            kept_layers.append(kept_values)
        results.append(hidden)
        kept_batches.append(kept_layers)
    layer_sums = [None] * layer_count
    seq_grads = []
    for batch_index in range(batch_count):
        grad_hidden = cotangent[batch_index, 0].astype(jnp.float32)
        for layer_index in reversed(range(layer_count)):
            weights = gather_layer(inner_weight, rate_weight, state_weight, out_weight, layer_index)
            grad_hidden, layer_grads = backward_layer(
                grad_hidden,
                weights,
                small_params,
                kept_batches[batch_index][layer_index],
                layer_index,
            )
            if layer_sums[layer_index] is None:
                layer_sums[layer_index] = layer_grads
            else:
                layer_sums[layer_index] = tuple(
                    (older + newer for older, newer in zip(layer_sums[layer_index], layer_grads))
                )
        seq_grads.append(grad_hidden)
    shard_inner, shard_rate, shard_out = (
        lax.psum_scatter(
            stack_layers(layer_sums, 0), ("dp", "seq"), scatter_dimension=1, tiled=True
        ),
        lax.psum_scatter(
            stack_layers(layer_sums, 1), ("dp", "seq"), scatter_dimension=1, tiled=True
        ),
        lax.psum_scatter(
            stack_layers(layer_sums, 3), ("dp", "seq"), scatter_dimension=2, tiled=True
        ),
    )
    shard_state = lax.psum_scatter(
        stack_layers(layer_sums, 2), ("dp", "seq", "tensor"), scatter_dimension=1, tiled=True
    )
    summed_small = lax.psum(
        (
            stack_layers(layer_sums, 4),
            stack_layers(layer_sums, 5),
            stack_layers(layer_sums, 6),
            stack_layers(layer_sums, 7),
            stack_layers(layer_sums, 8),
            stack_layers(layer_sums, 9),
            stack_layers(layer_sums, 10),
            stack_layers(layer_sums, 11),
            stack_layers(layer_sums, 12),
        ),
        ("dp", "seq"),
    )
    output = jnp.stack(results)[:, None]
    input_grad = jnp.stack(seq_grads)[:, None]
    return (
        output,
        input_grad,
        summed_small[0],
        shard_inner,
        shard_rate,
        shard_state,
        summed_small[1],
        summed_small[2],
        summed_small[3],
        summed_small[4],
        summed_small[5],
        summed_small[6],
        summed_small[7],
        summed_small[8],
        shard_out,
    )


GROUP = ("seq", "tensor")
LANES = 128
ROWS = 8
BF16, F32 = jnp.bfloat16, jnp.float32


def hop(value, first, second):
    pairs = [
        (place * 2 + core, (place ^ (second if core else first)) * 2 + core)
        for place in range(4)
        for core in range(2)
    ]
    return lax.ppermute(value, GROUP, pairs)


def swap(value):
    return lax.ppermute(value, "tensor", [(0, 1), (1, 0)])


def places():
    place, core = lax.axis_index("seq"), lax.axis_index("tensor")
    return place, core, place ^ (1 + core), place ^ (2 - core), place ^ 3


def put(buffer, block, *index):
    spots = index + (0,) * (buffer.ndim - len(index))
    return lax.dynamic_update_slice(buffer, block.reshape((1,) * len(index) + block.shape), spots)


def pick(array, index, axis=0):
    return lax.dynamic_index_in_dim(array, index, axis, False)


def line_shift(value, axis, step):
    count = lax.axis_size(axis)
    return lax.ppermute(value, axis, [(i, (i + step) % count) for i in range(count)])


def line_place(blocks, columns):
    count, place, rows = lax.axis_size("dp"), lax.axis_index("dp"), blocks[0].shape[0]
    out = jnp.zeros((count * rows, columns), blocks[0].dtype)
    for step, block in enumerate(blocks):
        out = lax.dynamic_update_slice(out, block, ((place - step) % count * rows, 0))
    return out


def line_near(block):
    count = lax.axis_size("dp")
    return jnp.stack([block] + [line_shift(block, "dp", step) for step in range(1, count)])


def line_sum_steps(part):
    count, place = lax.axis_size("dp"), lax.axis_index("dp")
    sent = [part((place + step) % count).astype(BF16) for step in range(1, count)]
    got = [line_shift(value, "dp", step + 1) for step, value in enumerate(sent)]
    token = yield sent
    total = part(place)
    for value in gate(got, token):
        total = total + value.astype(F32)
    return total


def seq_trade(parts):
    place = lax.axis_index("seq")
    out = put(jnp.zeros_like(parts), pick(parts, place), place)
    for turn in (1, 2, 3):
        got = lax.ppermute(pick(parts, place ^ turn), "seq", [(i, i ^ turn) for i in range(4)])
        out = put(out, got, place ^ turn)
    return out


def mesh_sum_steps(value):
    count = lax.axis_size("dp")
    turns = [("seq", 4, 1), ("seq", 4, 2)]
    turns += [("dp", count, 1 << bit) for bit in range(count.bit_length() - 1)]
    for axis, size, turn in turns:
        moved = lax.ppermute(value, axis, [(i, i ^ turn) for i in range(size)])
        token = yield value
        value = value + gate(moved, token)
    return value


def trade_steps(parts):
    place = lax.axis_index("seq")
    sent = [pick(parts, place ^ turn) for turn in (1, 2, 3)]
    got = [
        lax.ppermute(value, "seq", [(i, i ^ turn) for i in range(4)])
        for turn, value in zip((1, 2, 3), sent)
    ]
    token = yield sent
    out = put(jnp.zeros_like(parts), pick(parts, place), place)
    for turn, value in zip((1, 2, 3), gate(got, token)):
        out = put(out, value, place ^ turn)
    return out


def dot(left, right, left_dim=1, right_dim=0):
    return lax.dot_general(
        left, right, (((left_dim,), (right_dim,)), ((), ())), preferred_element_type=F32
    )


def split(value, count):
    pieces = []
    for _ in range(count):
        piece = value.astype(BF16)
        pieces.append(piece)
        value = value - piece.astype(F32)
    return pieces


def exact_left(value, ones, count, right_dim=0):
    rows = value.shape[0]
    stacked = dot(jnp.concatenate(split(value, count), axis=0), ones, 1, right_dim)
    total = stacked[:rows]
    for index in range(1, count):
        total = total + stacked[index * rows : (index + 1) * rows]
    return total


def head_sums(picker, value):
    high, low_part = split(value, 2)
    return dot(picker, high, 1, 1) + dot(picker, low_part, 1, 1)


def front(raw, window, taps, heads, spread, upper, width, state, extra):
    length = raw.shape[0]
    summed = taps[4:5, :] + taps[0:1, :] * window[5 : 5 + length, :]
    for tap in range(1, 4):
        summed = summed + taps[tap : tap + 1, :] * window[5 + tap : 5 + tap + length, :]
    sig = jax.nn.sigmoid(summed)
    activated = summed * sig
    rates = jnp.transpose(raw[:, 2 * width + 2 * state :])[:ROWS] + heads[0:ROWS, :]
    steps = jnp.maximum(rates, 0.0) + jnp.log1p(jnp.exp(-jnp.abs(rates)))
    decays = -jnp.exp(heads[ROWS : 2 * ROWS, :]) * steps
    running = exact_left(decays, upper, 3)
    ending = running[:, length - 1 : length]
    grown = jnp.exp(running)
    tail = jnp.exp(ending - running)
    rows = [steps, running, grown, tail] + extra
    rows.append(jnp.zeros((LANES // 2 - ROWS * len(rows), length), F32))
    rows = jnp.concatenate(rows, axis=0)
    high = rows.astype(BF16).astype(F32)
    halves = jnp.transpose(jnp.concatenate([high, rows - high], axis=0))
    columns = halves[:, : LANES // 2] + halves[:, LANES // 2 :]
    wide = dot(halves.astype(BF16), spread)
    whole_decay = jnp.exp(jnp.broadcast_to(ending, (ROWS, LANES)))
    inputs = activated[:, :width]
    return dict(
        summed=summed,
        sig=sig,
        inputs=inputs,
        keys=activated[:, width : width + state].astype(BF16),
        queries=activated[:, width + state :].astype(BF16),
        rates=rates,
        decays=decays,
        running=running,
        columns=columns,
        steps_wide=wide[:, :width],
        grown_wide=wide[:, width : 2 * width],
        tail_wide=wide[:, 2 * width : 3 * width],
        whole_decay=whole_decay,
    )


def per_row(whole_decay, head_count, head_size):
    return jnp.concatenate(
        [
            jnp.broadcast_to(whole_decay[h : h + 1, :], (head_size, LANES))
            for h in range(head_count)
        ],
        axis=0,
    )


def decay_matrix(parts, h, causal):
    length = causal.shape[0]
    column = parts["columns"][:, ROWS + h : ROWS + h + 1]
    row = parts["running"][h : h + 1, :]
    gap = jnp.broadcast_to(column, (length, length)) - row
    return jnp.exp(jnp.where(causal, gap, -1e30))


def causal_mask(length):
    return lax.broadcasted_iota(jnp.int32, (length, length), 0) >= lax.broadcasted_iota(
        jnp.int32, (length, length), 1
    )


def forward_kernel(
    head_size,
    order_ref,
    raw_first,
    raw_second,
    taps_ref,
    chans_ref,
    heads_ref,
    spread_ref,
    upper_ref,
    value_ref,
    square_ref,
    mixed_ref,
    state_ref,
    carry,
    window_first,
    window_second,
):
    length, width, state = raw_first.shape[0], chans_ref.shape[1], carry.shape[1]
    conv_width = width + 2 * state
    head_count = width // head_size
    pair = LANES // head_size
    step = pl.program_id(0)

    @pl.when(step == 0)
    def _():
        carry[...] = jnp.zeros_like(carry)
        window_first[0:ROWS, :] = jnp.zeros((ROWS, conv_width), F32)

    raws = [raw_first[...], raw_second[...]]
    windows = [window_first, window_second]
    for raw, window in zip(raws, windows):
        window[ROWS : ROWS + length, :] = raw[:, width : width + conv_width].astype(BF16).astype(F32)
    window_second[0:ROWS, :] = window_first[length : length + ROWS, :]
    taps, heads = taps_ref[...], heads_ref[...]
    fronts = [
        front(raw, window, taps, heads, spread_ref[...], upper_ref[...], width, state, [])
        for raw, window in zip(raws, windows)
    ]
    window_first[0:ROWS, :] = window_second[length : length + ROWS, :]
    causal = causal_mask(length)
    lane = lax.broadcasted_iota(jnp.int32, (length, LANES), 1) // head_size
    insides, steppeds = [], []
    for parts in fronts:
        stepped = parts["inputs"] * parts["steps_wide"]
        stepped_low = stepped.astype(BF16)
        scores = dot(parts["queries"], parts["keys"], 1, 1)
        columns = []
        for block in range(head_count // pair):
            source = stepped_low[:, block * LANES : (block + 1) * LANES]
            joined = None
            for k in range(pair):
                mixing = (scores * decay_matrix(parts, block * pair + k, causal)).astype(BF16)
                got = dot(mixing, source)
                joined = got if joined is None else jnp.where(lane == k, got, joined)
            columns.append(joined)
        insides.append(jnp.concatenate(columns, axis=1))
        steppeds.append(stepped)
    updates = [
        dot((stepped * parts["tail_wide"]).astype(BF16), parts["keys"], 0, 0)
        for stepped, parts in zip(steppeds, fronts)
    ]
    before = carry[...]
    for sub, (raw, parts, inside, update) in enumerate(zip(raws, fronts, insides, updates)):
        inputs = parts["inputs"]
        state_ref[sub] = before
        carried = dot(parts["queries"], before.astype(BF16), 1, 1)
        mixed = inside + carried * parts["grown_wide"] + chans_ref[0:1, :] * inputs
        before = per_row(parts["whole_decay"], head_count, head_size) * before + update
        gate_part = raw[:, :width]
        gated = mixed * (gate_part * jax.nn.sigmoid(gate_part))
        rows = pl.ds(pl.multiple_of(order_ref[2 * step + sub] * length, length), length)
        mixed_ref[rows, :] = mixed
        value_ref[rows, :] = (gated * chans_ref[1:2, :]).astype(BF16)
        squares = jnp.sum(gated * gated, axis=1, keepdims=True)
        square_ref[sub * ROWS : (sub + 1) * ROWS, :] = jnp.transpose(
            jnp.broadcast_to(squares, (length, length))
        )[:ROWS]
    carry[...] = before


def backward_kernel(
    head_size,
    inner_count,
    order_ref,
    grad_first,
    grad_second,
    raw_first,
    raw_second,
    past_ref,
    mixed_first,
    mixed_second,
    state_ref,
    token_ref,
    taps_ref,
    chans_ref,
    heads_ref,
    spread_ref,
    upper_ref,
    picker_ref,
    back_ref,
    taps_out,
    chans_out,
    heads_out,
    carry,
    window_first,
    window_second,
    later_first,
    later_second,
):
    length, width, state = raw_first.shape[0], chans_ref.shape[1], carry.shape[1]
    conv_width = width + 2 * state
    head_count = width // head_size
    pair = LANES // head_size
    step, count = pl.program_id(0), pl.num_programs(0)

    @pl.when(step == 0)
    def _():
        carry[...] = jnp.zeros_like(carry)
        later_first[length : length + ROWS, :] = jnp.zeros((ROWS, conv_width), F32)
        taps_out[...] = jnp.zeros_like(taps_out)
        chans_out[...] = jnp.zeros_like(chans_out)
        heads_out[...] = jnp.zeros_like(heads_out)

    raws = [raw_first[...], raw_second[...]]
    windows, laters = [window_first, window_second], [later_first, later_second]
    conv = slice(width, width + conv_width)
    for raw, window in zip(raws, windows):
        window[ROWS : ROWS + length, :] = raw[:, conv].astype(BF16).astype(F32)
    window_first[0:ROWS, :] = window_second[length : length + ROWS, :]
    past = past_ref[:, conv].astype(BF16).astype(F32)
    window_second[0:ROWS, :] = jnp.where(step == count - 1, 0.0, past)
    taps, heads, picker = taps_ref[...], heads_ref[...], picker_ref[...]
    skip, gain = chans_ref[0:1, :], chans_ref[1:2, :]
    causal = causal_mask(length)
    lane = lax.broadcasted_iota(jnp.int32, (length, LANES), 1)
    head_lane = lane // head_size
    places_of = [
        pl.ds(pl.multiple_of(order_ref[2 * count - 1 - 2 * step - sub] * length, length), length)
        for sub in range(2)
    ]

    fronts, held = [], []
    for sub, (raw, window, grad_ref, mixed_ref) in enumerate(
        zip(raws, windows, (grad_first, grad_second), (mixed_first, mixed_second))
    ):
        token = token_ref[(1 - sub) * ROWS : (2 - sub) * ROWS, :]
        parts = front(
            raw, window, taps, heads, spread_ref[...], upper_ref[...], width, state, [token]
        )
        fronts.append(parts)
        inputs = parts["inputs"]
        scale = parts["columns"][:, 4 * ROWS : 4 * ROWS + 1]
        inner = parts["columns"][:, 4 * ROWS + 1 : 4 * ROWS + 2]
        gate_part, mixed = raw[:, :width], mixed_ref[...]
        gate_sig = jax.nn.sigmoid(gate_part)
        gate_silu = gate_part * gate_sig
        gated = mixed * gate_silu
        grad = grad_ref[...]
        gain_term = jnp.sum(grad * (gated * scale), axis=0, keepdims=True)
        grad_gated = scale * (grad * gain) - gated * (scale * scale * scale * inner / inner_count)
        grad_mixed = grad_gated * gate_silu
        back_ref[places_of[sub], :width] = (
            grad_gated * mixed * (gate_sig + gate_silu * (1.0 - gate_sig))
        ).astype(BF16)
        chans_out[0:1, :] += jnp.sum(grad_mixed * inputs, axis=0, keepdims=True)
        chans_out[1:2, :] += gain_term
        held.append(grad_mixed)

    works = []
    for parts, grad_mixed in zip(fronts, held):
        stepped = parts["inputs"] * parts["steps_wide"]
        stepped_low, grad_low = stepped.astype(BF16), grad_mixed.astype(BF16)
        scores = dot(parts["queries"], parts["keys"], 1, 1)
        grad_scores = jnp.zeros((length, length), F32)
        row_sums = jnp.zeros((length, length), F32)
        column_sums, columns = [], []
        for block in range(head_count // pair):
            cut = slice(block * LANES, (block + 1) * LANES)
            source, target = stepped_low[:, cut], grad_low[:, cut]
            joined = None
            for k in range(pair):
                h = block * pair + k
                spread_h = decay_matrix(parts, h, causal)
                own_target = jnp.where(head_lane == k, target, jnp.zeros_like(target))
                pulled = dot(own_target, source, 1, 1) * spread_h
                grad_scores = grad_scores + pulled
                moved = pulled * scores
                row_sums = jnp.where(lane == h, jnp.sum(moved, axis=1, keepdims=True), row_sums)
                column_sums.append(jnp.sum(moved, axis=0, keepdims=True))
                got = dot((scores * spread_h).astype(BF16), target, 0, 0)
                joined = got if joined is None else jnp.where(head_lane == k, got, joined)
            columns.append(joined)
        column_sums.append(jnp.zeros((ROWS - head_count, length), F32))
        differences = jnp.transpose(row_sums)[:ROWS] - jnp.concatenate(column_sums, axis=0)
        works.append((stepped, grad_scores, jnp.concatenate(columns, axis=1), differences))

    after = carry[...]
    row_lane = lax.broadcasted_iota(jnp.int32, (ROWS, length), 1)
    row_head = lax.broadcasted_iota(jnp.int32, (ROWS, length), 0)
    for sub, (parts, grad_mixed, work) in enumerate(zip(fronts, held, works)):
        inputs, keys, queries = parts["inputs"], parts["keys"], parts["queries"]
        stepped, grad_scores, inside, differences = work
        window, later = windows[sub], laters[sub]
        before = state_ref[1 - sub]
        before_low, after_low = before.astype(BF16), after.astype(BF16)
        tail_wide, grown_wide = parts["tail_wide"], parts["grown_wide"]
        through = tail_wide * dot(keys, after_low, 1, 1)
        grad_stepped = inside + through
        ended = stepped * through
        carried = dot(queries, before_low, 1, 1) * grown_wide
        kept = per_row(parts["whole_decay"], head_count, head_size) * after
        kept_sum = jnp.sum(kept * before, axis=1, keepdims=True)
        kept_heads = jnp.concatenate(
            [
                jnp.sum(kept_sum[h * head_size : (h + 1) * head_size], axis=0, keepdims=True)
                for h in range(head_count)
            ]
            + [jnp.zeros((ROWS - head_count, 1), F32)],
            axis=0,
        )
        ended_heads = head_sums(picker, ended)
        grad_running = differences + head_sums(picker, grad_mixed * carried) - ended_heads
        last = jnp.sum(ended_heads, axis=1, keepdims=True) + kept_heads
        grad_running = grad_running + jnp.where(row_lane == length - 1, last, 0.0)
        grad_decays = exact_left(grad_running, upper_ref[...], 3, 1)
        grad_steps = head_sums(picker, inputs * grad_stepped)
        grad_rates = (
            grad_steps - jnp.exp(heads[ROWS : 2 * ROWS, :]) * grad_decays
        ) * jax.nn.sigmoid(parts["rates"])
        grad_rates = jnp.where(row_head < head_count, grad_rates, 0.0)
        heads_out[0:ROWS, :] += grad_rates
        heads_out[ROWS : 2 * ROWS, :] += grad_decays * parts["decays"]
        back_ref[places_of[sub], 2 * width + 2 * state :] = jnp.transpose(
            jnp.concatenate([grad_rates, jnp.zeros((LANES - ROWS, length), F32)], axis=0)
        ).astype(BF16)

        grad_inputs = parts["steps_wide"] * grad_stepped + skip * grad_mixed
        grown_low = (grown_wide * grad_mixed).astype(BF16)
        scores_low = grad_scores.astype(BF16)
        grad_queries = dot(scores_low, keys) + dot(grown_low, before_low)
        grad_keys = dot(scores_low, queries, 0, 0) + dot(
            (stepped * tail_wide).astype(BF16), after_low
        )
        after = kept + dot(grown_low, queries, 0, 0)

        sig, summed = parts["sig"], parts["summed"]
        grad_v = jnp.concatenate([grad_inputs, grad_keys, grad_queries], axis=1) * (
            sig + summed * sig * (1.0 - sig)
        )
        later[0:length, :] = grad_v
        grad_conv = taps[3:4, :] * grad_v
        taps_out[4:5, :] += jnp.sum(grad_v, axis=0, keepdims=True)
        for tap in range(4):
            if tap < 3:
                moved = later[3 - tap : 3 - tap + length, :]
                grad_conv = grad_conv + taps[tap : tap + 1, :] * moved
            taps_out[tap : tap + 1, :] += jnp.sum(
                grad_v * window[5 + tap : 5 + tap + length, :], axis=0, keepdims=True
            )
        laters[1 - sub][length : length + ROWS, :] = grad_v[0:ROWS]
        back_ref[places_of[sub], conv] = grad_conv.astype(BF16)
    carry[...] = after


def tables(width, head_size):
    channel_head = jnp.arange(width)[None, :] // head_size
    rows = jnp.arange(LANES)[:, None]
    spread = jnp.concatenate(
        [rows % (LANES // 2) == channel_head + ROWS * kind for kind in (0, 2, 3)], axis=1
    ).astype(BF16)
    upper = (rows <= jnp.arange(LANES)[None, :]).astype(BF16)
    picker = (jnp.arange(ROWS)[:, None] == channel_head).astype(BF16)
    return spread, upper, picker


def fixed(shape):
    return pl.BlockSpec(shape, lambda i, order: (0,) * len(shape))


def mix_forward(raw, order, small, tabs, head_size, width, state):
    taps, chans, heads = small
    spread, upper, _ = tabs
    tokens, columns = raw.shape
    count = tokens // STRETCH

    def moved(sub):
        return pl.BlockSpec((STRETCH, columns), lambda i, order: (order[2 * i + sub], 0))

    return pl.pallas_call(
        lambda *refs: forward_kernel(head_size, *refs),
        grid_spec=pltpu.PrefetchScalarGridSpec(
            num_scalar_prefetch=1,
            grid=(count // 2,),
            in_specs=[
                moved(0),
                moved(1),
                fixed(taps.shape),
                fixed(chans.shape),
                fixed(heads.shape),
                fixed(spread.shape),
                fixed(upper.shape),
            ],
            out_specs=[
                fixed((tokens, width)),
                pl.BlockSpec((2 * ROWS, LANES), lambda i, order: (i, 0)),
                fixed((tokens, width)),
                pl.BlockSpec((2, width, state), lambda i, order: (i, 0, 0)),
            ],
            scratch_shapes=[
                pltpu.VMEM((width, state), F32),
                pltpu.VMEM((STRETCH + ROWS, width + 2 * state), F32),
                pltpu.VMEM((STRETCH + ROWS, width + 2 * state), F32),
            ],
        ),
        out_shape=[
            jax.ShapeDtypeStruct((tokens, width), BF16),
            jax.ShapeDtypeStruct((count * ROWS, LANES), F32),
            jax.ShapeDtypeStruct((tokens, width), F32),
            jax.ShapeDtypeStruct((count, width, state), F32),
        ],
        compiler_params=pltpu.CompilerParams(
            dimension_semantics=("arbitrary",), vmem_limit_bytes=20 * 2**20
        ),
        cost_estimate=pl.CostEstimate(
            flops=11_000_000_000, bytes_accessed=10_000_000, transcendentals=0
        ),
    )(order, raw, raw, taps, chans, heads, spread, upper)


def mix_backward(grad, raw, mixed, states, token_rows, order, small, tabs, head_size, inner_count):
    taps, chans, heads = small
    spread, upper, picker = tabs
    tokens, columns = raw.shape
    width, state = states.shape[1:]
    count = tokens // STRETCH
    per = STRETCH // ROWS

    steps = count // 2

    def moved(sub, extent):
        return pl.BlockSpec(
            (STRETCH, extent), lambda i, order: (order[count - 1 - 2 * i - sub], 0)
        )

    def past(i, order):
        return (order[jnp.maximum(count - 3 - 2 * i, 0)] * per + per - 1, 0)

    return pl.pallas_call(
        lambda *refs: backward_kernel(head_size, inner_count, *refs),
        grid_spec=pltpu.PrefetchScalarGridSpec(
            num_scalar_prefetch=1,
            grid=(steps,),
            in_specs=[
                moved(0, width),
                moved(1, width),
                moved(0, columns),
                moved(1, columns),
                pl.BlockSpec((ROWS, columns), past),
                moved(0, width),
                moved(1, width),
                pl.BlockSpec((2, width, state), lambda i, order: (steps - 1 - i, 0, 0)),
                pl.BlockSpec((2 * ROWS, LANES), lambda i, order: (steps - 1 - i, 0)),
                fixed(taps.shape),
                fixed(chans.shape),
                fixed(heads.shape),
                fixed(spread.shape),
                fixed(upper.shape),
                fixed(picker.shape),
            ],
            out_specs=[
                fixed((tokens, columns)),
                fixed(taps.shape),
                fixed(chans.shape),
                fixed(heads.shape),
            ],
            scratch_shapes=[pltpu.VMEM((width, state), F32)]
            + [pltpu.VMEM((STRETCH + ROWS, width + 2 * state), F32) for _ in range(4)],
        ),
        out_shape=[
            jax.ShapeDtypeStruct((tokens, columns), BF16),
            jax.ShapeDtypeStruct(taps.shape, F32),
            jax.ShapeDtypeStruct(chans.shape, F32),
            jax.ShapeDtypeStruct(heads.shape, F32),
        ],
        compiler_params=pltpu.CompilerParams(
            dimension_semantics=("arbitrary",), vmem_limit_bytes=24 * 2**20
        ),
        cost_estimate=pl.CostEstimate(
            flops=23_000_000_000, bytes_accessed=16_000_000, transcendentals=0
        ),
    )(
        order,
        grad,
        grad,
        raw,
        raw,
        raw,
        mixed,
        mixed,
        states,
        token_rows,
        taps,
        chans,
        heads,
        spread,
        upper,
        picker,
    )


def small_kernel(layers, heads_here, head_count, state, spot_ref, place_ref, arrived_ref, out_ref):
    share = arrived_ref.shape[1]
    rows = share // layers
    row = lax.broadcasted_iota(jnp.int32, (LANES, LANES), 0)
    lane = lax.broadcasted_iota(jnp.int32, (LANES, LANES), 1)
    chosen = []
    for layer in range(layers):
        source = lane + layer * heads_here + place_ref[0] * head_count
        chosen.append(((row == source) & (lane < head_count)).astype(BF16))
    for index in range(out_ref.shape[1] // share):
        pair = [arrived_ref[spot_ref[2 * index + which]] for which in range(2)]
        own = jnp.where(place_ref[1] == 0, pair[0][:, 2 * state :], pair[1][:, 2 * state :])
        turned = jnp.concatenate([own.astype(F32), jnp.zeros((LANES - share, LANES), F32)], axis=0)
        turned = jnp.transpose(turned)[:share].astype(BF16)
        spot = index * share
        for layer in range(layers):
            cut = slice(layer * rows, (layer + 1) * rows)
            out_ref[layer, spot : spot + rows, : 2 * state] = pair[0][cut, : 2 * state]
            out_ref[layer, spot + rows : spot + share, : 2 * state] = pair[1][cut, : 2 * state]
            out_ref[layer, spot : spot + share, 2 * state :] = dot(turned, chosen[layer]).astype(BF16)


def small_unpack(arrived, order, layers, heads_here, head_count, state):
    line, share, columns = arrived.shape[0] // 8, arrived.shape[1], arrived.shape[2]
    place, core = lax.axis_index("seq"), lax.axis_index("tensor")
    back = (lax.axis_index("dp") - jnp.arange(line)) % line
    spots = (order[None, :] * line + back[:, None]).reshape(-1).astype(jnp.int32)
    scalars = pl.BlockSpec(memory_space=pltpu.SMEM)
    return pl.pallas_call(
        lambda *refs: small_kernel(layers, heads_here, head_count, state, *refs),
        in_specs=[scalars, scalars, pl.BlockSpec(memory_space=pltpu.VMEM)],
        out_shape=jax.ShapeDtypeStruct((layers, line * 4 * share, columns), BF16),
        compiler_params=pltpu.CompilerParams(vmem_limit_bytes=14 * 2**20),
    )(spots, jnp.stack([place, core]).astype(jnp.int32), arrived)


def finish_kernel(
    head_count, state, first_ref, second_ref, first_out, second_out, inner_ref, out_ref, state_ref, rate_ref
):
    width = out_ref.shape[2] // 4
    share = out_ref.shape[1]
    for layer, (ref, more) in enumerate(((first_ref, first_out), (second_ref, second_out))):
        states = jnp.zeros((share, 2 * state), F32)
        rates = []
        for index in range(4):
            value = ref[index].astype(F32)
            spot = slice(index * width, (index + 1) * width)
            inner_ref[layer, :, 0, spot] = value[:, :width]
            inner_ref[layer, :, 1, spot] = value[:, width : 2 * width]
            states = states + value[:, 2 * width : 2 * width + 2 * state]
            rate = jnp.concatenate(
                [value[:, 2 * width + 2 * state :], jnp.zeros((LANES - share, LANES), F32)], axis=0
            )
            rates.append(jnp.transpose(rate)[:head_count, :share])
            out_ref[layer, :, spot] = more[index].astype(F32)
        rate_ref[layer] = jnp.concatenate(rates, axis=0)
        state_ref[layer] = states


def finish(first, second, first_out, second_out, head_count, state, width):
    share = first.shape[1]
    return pl.pallas_call(
        lambda *refs: finish_kernel(head_count, state, *refs),
        out_shape=[
            jax.ShapeDtypeStruct((2, share, 2, 4 * width), F32),
            jax.ShapeDtypeStruct((2, share, 4 * width), F32),
            jax.ShapeDtypeStruct((2, share, 2 * state), F32),
            jax.ShapeDtypeStruct((2, 4 * head_count, share), F32),
        ],
        compiler_params=pltpu.CompilerParams(vmem_limit_bytes=14 * 2**20),
    )(first, second, first_out, second_out)


def norm_scale(hidden):
    return lax.rsqrt(jnp.mean(hidden * hidden, axis=1, keepdims=True) + EPSILON)


PLAN = (
    "v a l ga",
    "gb a v a",
    "b ga gb a",
    "b a b ga",
    "gb a b a",
    "b a b l",
    "a b a b",
    "a b a b",
    "a b a b",
    "a b a b",
    "a b a b",
    "a b oa1 a",
    "b xo a b",
    "a ob1 b a",
    "q ia1 b xo",
    "a b ib1 r",
    "a b oa0 a",
    "b a a b",
    "ob0 y ia0 b",
    "ib0 u a b",
    "a m b y",
    "q m b q",
    "m y b xg",
    "m r m r",
    "xg m u u",
)


def gate(value, token):
    return value if token is None else lax.optimization_barrier((value, token))[0]


def gather_steps(block):
    from_near, from_far = hop(block, 1, 2), hop(block, 2, 1)
    token = yield block
    from_near = gate(from_near, token)
    from_across = hop(from_near, 2, 1)
    token = yield from_near
    four = jnp.stack([block, from_near, gate(from_far, token), gate(from_across, token)])
    twin = swap(four)
    token = yield four
    return jnp.concatenate([four, gate(twin, token)])


def scatter_steps(own, other, tiny=None):
    got = swap(other)
    moved = None if tiny is None else hop(tiny, 1, 2)
    token = yield other
    got = gate(got, token)
    to_far = (own[2:].astype(F32) + got[2:].astype(F32)).astype(BF16)
    from_far = hop(to_far, 2, 1)
    if tiny is not None:
        tiny = tiny + gate(moved, token)
        moved = hop(tiny, 2, 1)
    token = yield to_far
    from_far = gate(from_far, token)
    both = own[:2].astype(F32) + got[:2].astype(F32) + from_far.astype(F32)
    side = both[1].astype(BF16)
    from_near = hop(side, 1, 2)
    if tiny is not None:
        tiny = tiny + gate(moved, token)
        moved = swap(tiny)
    token = yield (side, both[0])
    total = both[0] + gate(from_near, token).astype(F32)
    if tiny is not None:
        tiny = tiny + gate(moved, token)
    return total, tiny


def arrival_order():
    place, core = lax.axis_index("seq"), lax.axis_index("tensor")
    block = jnp.arange(8)
    turn, their = block // 2 ^ place, block % 2
    first = jnp.where(their == 0, turn, jnp.where(turn == 1, 2, jnp.where(turn == 2, 1, turn)))
    return (first + jnp.where(their == core, 0, 4)).astype(jnp.int32)


class Track:
    def __init__(self):
        self.token = None
        self.chains = {}

    def begin(self, name, chain):
        next(chain)
        self.chains[name] = chain

    def run(self, *plan):
        for name in " ".join(plan).split():
            name, _, count = name.partition("*")
            for _ in range(int(count or 1)):
                try:
                    self.token = self.chains[name].send(self.token)
                except StopIteration:
                    pass


def late_gather(store, key, block):
    token = yield None
    store[key] = yield from gather_steps(gate(block, token))


def kept_result(store, key, chain):
    yield None
    store[key] = yield from chain


def together(main, side):
    token = yield (next(main), next(side))
    result, running = None, [True, True]
    while any(running):
        values = []
        for index, chain in enumerate((main, side)):
            if running[index]:
                try:
                    values.append(chain.send(token))
                except StopIteration as stop:
                    running[index] = False
                    result = stop.value if index == 0 else result
        if any(running):
            token = yield tuple(values)
    return result


def sum_steps(value, store, key):
    moved = hop(value, 1, 2)
    token = yield value
    value = value + gate(moved, token)
    moved = hop(value, 2, 1)
    token = yield value
    value = value + gate(moved, token)
    moved = swap(value)
    token = yield value
    store[key] = value + gate(moved, token)


def head_body(
    tokens,
    cotangent,
    norm_gain,
    inner_weight,
    rate_weight,
    state_weight,
    conv_inner,
    bias_inner,
    conv_state,
    bias_state,
    rate_bias,
    decay_log,
    skip_gain,
    gate_gain,
    out_weight,
):
    layers, batches = norm_gain.shape[0], tokens.shape[0]
    model = tokens.shape[3]
    place, core = lax.axis_index("seq"), lax.axis_index("tensor")
    line = lax.axis_size("dp")
    share, half_width = inner_weight.shape[1], inner_weight.shape[3]
    inner_count = half_width * 2
    width = half_width // 4
    head_count = rate_bias.shape[1] // 4
    head_size = width // head_count
    state_share, state = state_weight.shape[1], state_weight.shape[2] // 2
    own_rows = tokens.shape[2] // 2
    length = own_rows * 8
    conv_width = width + 2 * state
    columns = 2 * width + 2 * state + LANES
    heads_here = rate_weight.shape[2]
    tabs = tables(width, head_size)

    def own(array):
        return lax.dynamic_slice_in_dim(array, core * own_rows, own_rows, 0)

    def quarter(array, count):
        return lax.dynamic_slice_in_dim(array, place * count, count, array.ndim - 1)

    def out_share(layer):
        turned = out_weight[layer].T.reshape(share, 4, width)
        return turned.transpose(1, 0, 2)

    def inner_share(layer):
        cut = inner_weight[layer].reshape(share, 2, 4, width)
        return cut.transpose(2, 0, 1, 3).reshape(4, share, 2 * width)

    def first_for(taker):
        cut = lax.dynamic_slice(inner_weight[0], (0, 0, taker * width), (share, 2, width))
        return jnp.concatenate([cut[:, 0], cut[:, 1]], axis=1)

    out_weights, in_weights = {}, {}

    def first_out():
        token = yield None
        traded = yield from trade_steps(gate(out_share(0), token))
        traded = traded.reshape(4 * share, width)
        got = [line_shift(traded, "dp", step) for step in range(1, line)]
        token = yield traded
        out_weights[0] = line_place([traded] + gate(got, token), width)

    def later(layer):
        token = yield None
        mixed_share = jnp.concatenate([inner_share(layer), out_share(layer)], axis=2)
        traded = yield from trade_steps(gate(mixed_share, token))
        full = lax.all_gather(traded.reshape(4 * share, -1), "dp").reshape(model, -1)
        token = yield traded
        full = gate(full, token)
        out_weights[layer] = full[:, 2 * width :]
        in_weights[layer] = jnp.concatenate([full[:, : 2 * width], small_full[layer]], axis=1)
        yield in_weights[layer]

    first = put(jnp.zeros((4, share, 2 * width), BF16), first_for(place), place)
    first_sent = [first_for(place ^ turn) for turn in (1, 2, 3)]
    for turn, value in zip((1, 2, 3), first_sent):
        pairs = [(i, i ^ turn) for i in range(4)]
        first = put(first, lax.ppermute(value, "seq", pairs), place ^ turn)
    first = first.reshape(4 * share, 2 * width)
    rate_rows = rate_weight.transpose(0, 2, 1).reshape(layers * heads_here, share)
    rate_rows = jnp.pad(rate_rows, ((0, share - layers * heads_here), (0, LANES - share)))
    small_share = jnp.concatenate([state_weight.reshape(share, 2 * state), rate_rows], axis=1)
    small_near = line_near(small_share)

    smalls = []

    def prepare():
        token = yield None
        given = (conv_inner, conv_state, bias_inner, bias_state, skip_gain, gate_gain, rate_bias, decay_log)
        (
            conv_inner_,
            conv_state_,
            bias_inner_,
            bias_state_,
            skip_gain_,
            gate_gain_,
            rate_bias_,
            decay_log_,
        ) = gate(given, token)
        for layer in range(layers):
            taps = jnp.concatenate([quarter(conv_inner_[layer], width), conv_state_[layer]], axis=1)
            bias = jnp.concatenate([quarter(bias_inner_[layer], width), bias_state_[layer]])
            taps = jnp.concatenate([taps, bias[None], jnp.zeros((3, conv_width), F32)], axis=0)
            skip = jnp.repeat(quarter(skip_gain_[layer], head_count), head_size)
            chans = jnp.stack([skip, quarter(gate_gain_[layer], width)])
            chans = jnp.concatenate([chans, jnp.zeros((ROWS - 2, width), F32)], axis=0)
            heads = jnp.stack(
                [quarter(rate_bias_[layer], head_count), quarter(decay_log_[layer], head_count)]
            )
            heads = jnp.pad(heads, ((0, 0), (0, ROWS - head_count))).reshape(2 * ROWS, 1)
            smalls.append((taps, chans, jnp.broadcast_to(heads, (2 * ROWS, LANES))))
        yield smalls

    order = arrival_order()
    track = Track()
    track.token = (first_sent, small_share)
    hiddens = [own(tokens[batch, 0]).astype(F32) for batch in range(batches)]
    row_scales, normed_all, whole = [], {}, {}
    for batch in range(batches):
        row_scales.append(norm_scale(hiddens[batch]))
        normed = (hiddens[batch] * row_scales[batch] * norm_gain[0][None, :]).astype(BF16)
        normed = gate(normed, track.token)
        track.begin(str(batch), kept_result(normed_all, (0, batch), gather_steps(normed)))
    track.begin("s", kept_result(whole, "small", gather_steps(gate(small_near, first))))
    track.begin("p", prepare())
    grads, grad_all = [], {}
    for batch, name in enumerate(("ga", "gb")):
        low_part = own(gate(cotangent[batch, 0], first_sent))
        grads.append(low_part.astype(F32))
        track.begin(name, late_gather(grad_all, (layers - 1, batch), low_part))
    track.run("0 1")
    first_got = [line_shift(first, "dp", step) for step in range(1, line)]
    track.token = first
    track.run("s")
    track.token = first_got[0]
    track.run("0 1 s p", "0 1 s ga", "gb 0 1 s")
    track.begin("v", first_out())
    track.begin("l", later(1))
    track.run("v l")
    first_full = line_place(gate([first] + first_got, track.token), columns)
    small_full = small_unpack(
        whole["small"].reshape(-1, share, small_share.shape[1]),
        order,
        layers,
        heads_here,
        head_count,
        state,
    )
    in_weights[0] = lax.dynamic_update_slice(first_full, small_full[0], (0, 2 * width))
    track.token = first_full
    gradients, inners, terms, outputs = {}, {}, {}, {}

    def inner_products(grad_low, summed):
        inner = jnp.sum(grad_low.astype(F32) * summed, axis=1)
        return put(jnp.zeros((8, own_rows), F32), inner, place * 2 + core)

    moves = order[None, :] == jnp.arange(8)[:, None]

    def halves_of(value, weight):
        half = length // 2
        other = dot(value[half:], weight, 1, 1).astype(BF16)
        return (
            dot(value[:half], weight, 1, 1).astype(BF16).reshape(4, own_rows, model),
            other.reshape(4, own_rows, model),
        )

    def batch_chain(batch):
        token = yield None
        hidden, row_scale = hiddens[batch], row_scales[batch]
        normed = normed_all[0, batch]
        kept = {}
        for layer in range(layers):
            normed = normed.reshape(length, model)
            raw = dot(gate(normed, token), in_weights[layer])
            token = yield raw
            value, squares, mixed, states = mix_forward(
                gate(raw, token), order, smalls[layer], tabs, head_size, width, state
            )
            token = yield value
            halves = halves_of(gate(value, token), out_weights[layer])
            summed, squares = yield from scatter_steps(
                *halves, squares.reshape(-1, ROWS, LANES)[:, 0]
            )
            scales = lax.rsqrt(squares / inner_count + EPSILON)
            flat_scales = scales.reshape(8, own_rows)
            own_scale = pick(flat_scales, place * 2 + core)[:, None]
            arrived = jnp.sum(jnp.where(moves[:, :, None], flat_scales[None], 0.0), axis=1)
            normed_out = (value.astype(F32) * arrived.reshape(length, 1)).astype(BF16)
            kept[layer] = (hidden, row_scale, normed, raw, mixed, states, summed, scales, normed_out)
            hidden = hidden + own_scale * summed
            if layer + 1 < layers:
                row_scale = norm_scale(hidden)
                normed = (hidden * row_scale * norm_gain[layer + 1][None, :]).astype(BF16)
                normed = yield from gather_steps(normed)
                token = None
        outputs[batch] = hidden
        grad_hidden = grads[batch]
        top_inner = inner_products(grad_hidden.astype(BF16), kept[layers - 1][6])
        yield from sum_steps(top_inner, inners, (layers - 1, batch))
        token = None
        for layer in reversed(range(layers)):
            hidden, row_scale, normed, raw, mixed, states, summed, scales, normed_out = kept[layer]
            whole_grad = grad_all[layer, batch].reshape(length, model)
            terms[layer, batch] = [whole_grad, normed_out, normed, None]
            grad_value = dot(gate(whole_grad, token), out_weights[layer])
            token = yield grad_value
            token_rows = jnp.stack([scales, inners[layer, batch].reshape(-1, LANES)], axis=1)
            token_rows = jnp.pad(token_rows, ((0, 0), (0, ROWS - 2), (0, 0)))
            back, taps_grad, chans_grad, heads_grad = mix_backward(
                gate(grad_value, token),
                raw,
                mixed,
                states,
                token_rows.reshape(-1, LANES),
                order,
                smalls[layer],
                tabs,
                head_size,
                inner_count,
            )
            terms[layer, batch][3] = back
            token = yield back
            halves = halves_of(gate(back, token), in_weights[layer])
            gain_term = sum(
                jnp.sum(part.reshape(-1, model).astype(F32) * cut.astype(F32), axis=0)
                for part, cut in zip(halves, (normed[: length // 2], normed[length // 2 :]))
            )
            gradients[layer, batch] = (
                taps_grad,
                chans_grad,
                heads_grad,
                gain_term / norm_gain[layer],
            )
            grad_normed, _ = yield from scatter_steps(*halves)
            weighted = grad_normed * norm_gain[layer][None, :]
            mean = jnp.mean(weighted * hidden, axis=1, keepdims=True)
            grad_hidden = (
                grad_hidden
                + row_scale * weighted
                - hidden * (row_scale * row_scale * row_scale) * mean
            )
            if layer > 0:
                grad_low = grad_hidden.astype(BF16)
                inner = inner_products(grad_low, kept[layer - 1][6])
                grad_all[layer - 1, batch] = yield from together(
                    gather_steps(grad_low), sum_steps(inner, inners, (layer - 1, batch))
                )
                token = None
        grads[batch] = grad_hidden
        yield grad_hidden

    totals = {}

    def term(key, layer, batch, left, right):
        value = dot(left, right, 0, 0)
        if batch > 0:
            value = value + totals[key, layer, batch - 1].astype(F32)
        totals[key, layer, batch] = value.astype(BF16)
        return totals[key, layer, batch]

    def out_term(layer, batch):
        token = yield None
        whole_grad, normed_out, _, _ = terms[layer, batch]
        yield term("out", layer, batch, gate(whole_grad, token), normed_out)

    def in_term(layer, batch):
        token = yield None
        _, _, normed, back = terms[layer, batch]
        yield term("in", layer, batch, gate(normed, token), back)

    rows = 4 * share

    def line_cut(array, index):
        return lax.dynamic_slice_in_dim(array, index * rows, rows, 0)

    def out_part(layer):
        total = totals["out", layer, batches - 1]
        return lambda index: line_cut(total, index).astype(F32)

    shares = {}

    def line_sum(total):
        return lax.psum_scatter(total, "dp", scatter_dimension=0, tiled=True)

    def first_sums(key):
        yield None
        if key == "out":
            total = yield from line_sum_steps(out_part(0))
            total = total.astype(BF16)
        else:
            packed = totals["in", 0, batches - 1]
            total = line_sum(packed)
            token = yield packed
            total = gate(total, token)
        shares[key, 0] = yield from trade_steps(total.reshape(4, share, -1))

    def later_sums(key, layer):
        token = yield None
        packed = totals[key, layer, batches - 1]
        total = line_sum(gate(packed, token))
        token = yield packed
        shares[key, layer] = yield from trade_steps(gate(total, token).reshape(4, share, -1))
        yield shares[key, layer]

    def both_cores(values, store, key):
        yield None
        others = [swap(value) for value in values()]
        token = yield values()
        both = []
        for value, other in zip(values(), gate(others, token)):
            first = jnp.where(core == 0, value, other)
            second = jnp.where(core == 0, other, value)
            both.append(jnp.concatenate([first, second], axis=0))
        store[key] = jnp.stack(both)[:, None]
        yield store[key]

    def small_sums():
        yield None
        flats = []
        for layer in range(layers):
            taps_grad, chans_grad, heads_grad, gain_term = (
                sum(values) for values in zip(*(gradients[layer, batch] for batch in range(batches)))
            )
            both = jnp.concatenate([gain_term, taps_grad[:5, width:].reshape(-1)])
            head_rows = jnp.stack(
                [
                    jnp.sum(heads_grad[:ROWS], axis=1)[:head_count],
                    jnp.sum(heads_grad[ROWS:], axis=1)[:head_count],
                    jnp.sum(chans_grad[0].reshape(head_count, head_size), axis=1),
                ]
            )
            flat = jnp.concatenate(
                [
                    both,
                    slot(taps_grad[:5, :width], width).reshape(-1),
                    slot(chans_grad[1], width),
                    slot(head_rows, head_count).reshape(-1),
                ]
            )
            flats.append(jnp.pad(flat, (0, -flat.shape[0] % LANES)))
        flat = jnp.stack(flats)
        shared = model + 10 * state
        moved = swap(flat[:, :shared])
        token = yield flat
        flat = lax.dynamic_update_slice(flat, flat[:, :shared] + gate(moved, token), (0, 0))
        finished["flat"] = yield from mesh_sum_steps(flat)

    def slot(array, count):
        shape = array.shape[:-1] + (4 * count,)
        spots = (0,) * (array.ndim - 1) + (place * count,)
        return lax.dynamic_update_slice(jnp.zeros(shape, F32), array, spots)

    finished = {}
    for batch, name in enumerate("ab"):
        track.begin(name, batch_chain(batch))
        for layer in range(layers):
            track.begin(f"o{name}{layer}", out_term(layer, batch))
            track.begin(f"i{name}{layer}", in_term(layer, batch))
    track.begin("y", first_sums("out"))
    track.begin("u", first_sums("in"))
    track.begin("r", later_sums("in", 1))
    track.begin("q", later_sums("out", 1))
    track.begin("xo", both_cores(lambda: [outputs[0], outputs[1]], finished, "output"))
    track.begin("xg", both_cores(lambda: [grads[0], grads[1]], finished, "input_grad"))
    track.begin("m", small_sums())
    track.run(*PLAN)

    inner_grad, out_grad, state_terms, rate_grad = finish(
        shares["in", 0],
        shares["in", 1],
        shares["out", 0],
        shares["out", 1],
        head_count,
        state,
        width,
    )
    state_terms = state_terms.reshape(layers, 2, state_share, 2 * state)
    state_grad = pick(state_terms, core, 1) + swap(pick(state_terms, 1 - core, 1))
    flat = finished["flat"]
    taken, small_out = 0, []
    for shape in ((model,), (5, 2 * state), (5, half_width), (half_width,), (3, 4 * head_count)):
        size = 1
        for extent in shape:
            size *= extent
        small_out.append(flat[:, taken : taken + size].reshape((layers,) + shape))
        taken += size

    return (
        finished["output"],
        finished["input_grad"],
        small_out[0],
        inner_grad,
        rate_grad.transpose(0, 2, 1),
        state_grad,
        small_out[2][:, :4],
        small_out[2][:, 4],
        small_out[1][:, :4],
        small_out[1][:, 4],
        small_out[4][:, 0],
        small_out[4][:, 1],
        small_out[4][:, 2],
        small_out[3],
        out_grad.transpose(0, 2, 1),
    )


def by_heads(mesh, tokens, inner_weight, rate_bias, conv_state, state_weight):
    place_count, core_count, line = mesh.shape["seq"], mesh.shape["tensor"], mesh.shape["dp"]
    if place_count != 4 or core_count != 2:
        return False
    heads, inner = rate_bias.shape[1], inner_weight.shape[3]
    rows = tokens.shape[2] // 8
    return (
        tokens.shape[1] == line
        and tokens.shape[2] % 8 == 0
        and rows == STRETCH
        and tokens.shape[0] == 2
        and line >= 2
        and inner_weight.shape[0] == 2
        and heads % 8 == 0
        and heads // 8 <= ROWS
        and (inner // 8) % LANES == 0
        and LANES % (inner // heads) == 0
        and conv_state.shape[1] == 4
        and state_weight.shape[2] == 2 * LANES
        and inner_weight.shape[1] % (line * 4 * 32) == 0
    )


def solution(mesh):
    in_specs = (
        P(None, "dp", "seq", None),
        P(None, "dp", "seq", None),
        P(),
        P(None, ("dp", "seq"), None, "tensor"),
        P(None, ("dp", "seq"), "tensor"),
        P(None, ("dp", "seq", "tensor"), None),
        P(None, None, "tensor"),
        P(None, "tensor"),
        P(),
        P(),
        P(None, "tensor"),
        P(None, "tensor"),
        P(None, "tensor"),
        P(None, "tensor"),
        P(None, "tensor", ("dp", "seq")),
    )
    out_specs = (
        P(None, "dp", "seq", None),
        P(None, "dp", "seq", None),
        P(),
        P(None, ("dp", "seq"), None, "tensor"),
        P(None, ("dp", "seq"), "tensor"),
        P(None, ("dp", "seq", "tensor"), None),
        P(None, None, "tensor"),
        P(None, "tensor"),
        P(),
        P(),
        P(None, "tensor"),
        P(None, "tensor"),
        P(None, "tensor"),
        P(None, "tensor"),
        P(None, "tensor", ("dp", "seq")),
    )
    def run(*arrays):
        by_name = (arrays[0], arrays[3], arrays[10], arrays[8], arrays[5])
        chosen = head_body if by_heads(mesh, *by_name) else span_body
        return jax.shard_map(
            chosen, mesh=mesh, in_specs=in_specs, out_specs=out_specs, check_vma=False
        )(*arrays)

    return run
```

```python
import jax
import jax.numpy as jnp
from jax import lax
from jax.experimental import pallas as pl
from jax.experimental.pallas import tpu as pltpu
from jax.sharding import PartitionSpec as P

DI = 3072
STRETCH = 128


EPSILON = 1e-05
HIGHEST = lax.Precision.HIGHEST


def shifted(value, axis, steps):
    count = lax.axis_size(axis)
    leading, last = (max(0, -steps), min(count, count - steps))
    return lax.ppermute(value, axis, [(source, source + steps) for source in range(leading, last)])


def carried_in(array, axis, combine, identity):
    length, place = (lax.axis_size(axis), lax.axis_index(axis))
    everything = jax.tree.map(
        lambda part, kind: lax.all_gather(part.astype(kind), axis),
        array,
        (jnp.bfloat16, jnp.bfloat16),
    )
    start = jax.tree.map(
        lambda part, zero: jnp.broadcast_to(jnp.asarray(zero, part.dtype), part.shape),
        array,
        identity,
    )

    def turn(k, before):
        reached = k < place
        new = combine(
            before, jax.tree.map(lambda part, own: part[k].astype(own.dtype), everything, array)
        )
        return jax.tree.map(lambda a, b: jnp.where(reached, a, b), new, before)

    return lax.fori_loop(0, length, turn, start)


def carried_in_2(array, axis, join, neutral):
    count = lax.axis_size(axis)
    place = lax.axis_index(axis)
    ahead = count - 1 - place
    gathered = jax.tree.map(
        lambda a, kind: lax.all_gather(a.astype(kind), axis),
        array,
        jax.tree.map(lambda a: jnp.bfloat16 if a.dtype == jnp.float32 else a.dtype, array),
    )
    state = jax.tree.map(lambda a, e: jnp.zeros_like(a) + jnp.asarray(e, a.dtype), array, neutral)

    def one(turn, state):
        source = count - 1 - turn
        return join(
            state,
            jax.tree.map(
                lambda a, own: lax.dynamic_index_in_dim(a, source, 0, False).astype(own.dtype),
                gathered,
                array,
            ),
        )

    return lax.fori_loop(0, ahead, one, state)


def product(left_side, right_side):
    return jnp.dot(left_side, right_side, precision=HIGHEST, preferred_element_type=jnp.float32)


def conv_silu(padded, weight, conv_bias):
    conv_width = weight.shape[0]
    out_rows = padded.shape[0] - conv_width + 1
    summed = conv_bias[None, :] + weight[0][None, :] * padded[0:out_rows]
    for offset in range(1, conv_width):
        summed = summed + weight[offset][None, :] * padded[offset : offset + out_rows]
    return jax.nn.silu(summed)


def block_step(carry_state, pieces):
    inputs, keys_b, queries_c, step_rates, decays = pieces
    running = jnp.cumsum(decays, axis=0)
    block_len = inputs.shape[0]
    causal = jnp.arange(block_len)[:, None] >= jnp.arange(block_len)[None, :]
    spread = running.T[:, :, None] - running.T[:, None, :]
    weights = jnp.exp(jnp.where(causal[None, :, :], spread, -jnp.inf))
    scores = product(queries_c, keys_b.T)
    mixing = scores[None, :, :] * weights * step_rates.T[:, None, :]
    inside = jnp.einsum("hts,shp->thp", mixing, inputs, precision=HIGHEST)
    carried = (
        jnp.einsum("tn,hpn->thp", queries_c, carry_state, precision=HIGHEST)
        * jnp.exp(running)[:, :, None]
    )
    tail_weight = jnp.exp(running[-1][None, :] - running) * step_rates
    update = jnp.einsum("shp,sn->hpn", tail_weight[:, :, None] * inputs, keys_b, precision=HIGHEST)
    return (jnp.exp(running[-1])[:, None, None] * carry_state + update, inside + carried)


def state_step(carry_state, pieces):
    inputs, keys_b, step_rates, decays = pieces
    running = jnp.cumsum(decays, axis=0)
    tail_weight = jnp.exp(running[-1][None, :] - running) * step_rates
    update = jnp.einsum("shp,sn->hpn", tail_weight[:, :, None] * inputs, keys_b, precision=HIGHEST)
    return (jnp.exp(running[-1])[:, None, None] * carry_state + update, None)


def to_blocks(values):
    return values.reshape((values.shape[0] // STRETCH, STRETCH) + values.shape[1:])


def span_summary(inputs, keys_b, step_rates, decays):
    zero_state = jnp.zeros((inputs.shape[1], inputs.shape[2], keys_b.shape[1]), jnp.float32)
    end_state, _ = lax.scan(
        state_step,
        zero_state,
        (to_blocks(inputs), to_blocks(keys_b), to_blocks(step_rates), to_blocks(decays)),
    )
    return (jnp.exp(jnp.sum(decays, axis=0)), end_state)


def span_output(inputs, keys_b, queries_c, step_rates, decays, entry_state, skip_gain):
    _, block_out = lax.scan(
        block_step,
        entry_state,
        (
            to_blocks(inputs),
            to_blocks(keys_b),
            to_blocks(queries_c),
            to_blocks(step_rates),
            to_blocks(decays),
        ),
    )
    mixed_out = block_out.reshape(inputs.shape) + skip_gain[None, :, None] * inputs
    return mixed_out.reshape(inputs.shape[0], -1)


def rate_piece(rate_raw, rate_bias, decay_log):
    step_rates = jax.nn.softplus(rate_raw + rate_bias[None, :])
    return (step_rates, -jnp.exp(decay_log)[None, :] * step_rates)


def norm_piece(hidden, norm_gain):
    row_scale = lax.rsqrt(jnp.mean(hidden * hidden, axis=1, keepdims=True) + EPSILON)
    return hidden * row_scale * norm_gain[None, :]


def chain_combine(earlier, following):
    return (earlier[0] * following[0], following[1] + following[0][:, None, None] * earlier[1])


def gather_layer(inner_weight, rate_weight, state_weight, out_weight, layer_index):
    inner_full, rate_full, out_full = (
        lax.all_gather(inner_weight[layer_index], ("dp", "seq"), axis=0, tiled=True),
        lax.all_gather(rate_weight[layer_index], ("dp", "seq"), axis=0, tiled=True),
        lax.all_gather(out_weight[layer_index], ("dp", "seq"), axis=1, tiled=True),
    )
    state_full = lax.all_gather(
        state_weight[layer_index], ("dp", "seq", "tensor"), axis=0, tiled=True
    )
    return (inner_full.reshape(inner_full.shape[0], -1), rate_full, state_full, out_full)


def forward_layer(hidden, weights, small_params, layer_index):
    inner_full, rate_full, state_full, out_full = weights
    (
        norm_gain,
        conv_inner,
        bias_inner,
        conv_state,
        bias_state,
        rate_bias,
        decay_log,
        skip_gain,
        gate_gain,
    ) = small_params
    seq_rows = hidden.shape[0]
    normed_full, norm_pull = jax.vjp(norm_piece, hidden, norm_gain[layer_index])
    normed = normed_full.astype(jnp.bfloat16)
    gate_inner = jnp.dot(normed, inner_full, preferred_element_type=jnp.float32)
    rate_raw = jnp.dot(normed, rate_full, preferred_element_type=jnp.float32)
    state_raw = jnp.dot(normed, state_full, preferred_element_type=jnp.float32)
    local_width = gate_inner.shape[1] // 2
    gate_part = gate_inner[:, :local_width]
    conv_input = jnp.concatenate([gate_inner[:, local_width:], state_raw], axis=1).astype(
        jnp.bfloat16
    )
    edge_count = conv_inner.shape[1] - 1
    edge_rows = shifted(conv_input[seq_rows - edge_count :], "seq", 1)
    padded = jnp.concatenate([edge_rows, conv_input], axis=0).astype(jnp.float32)
    conv_weight = jnp.concatenate([conv_inner[layer_index], conv_state[layer_index]], axis=1)
    conv_bias = jnp.concatenate([bias_inner[layer_index], bias_state[layer_index]])
    activated, conv_pull = jax.vjp(conv_silu, padded, conv_weight, conv_bias)
    state_size = state_raw.shape[1] // 2
    head_count = rate_bias.shape[1]
    inputs = activated[:, :local_width].reshape(seq_rows, head_count, local_width // head_count)
    keys_b = activated[:, local_width : local_width + state_size]
    queries_c = activated[:, local_width + state_size :]
    (step_rates, decays), rate_pull = jax.vjp(
        rate_piece, rate_raw, rate_bias[layer_index], decay_log[layer_index]
    )
    (span_decay, span_state), summary_pull = jax.vjp(
        span_summary, inputs, keys_b, step_rates, decays
    )
    identity = (jnp.ones_like(span_decay), jnp.zeros_like(span_state))
    entry_state = carried_in((span_decay, span_state), "seq", chain_combine, identity)[1]
    mixed_out, output_pull = jax.vjp(
        span_output,
        inputs,
        keys_b,
        queries_c,
        step_rates,
        decays,
        entry_state,
        skip_gain[layer_index],
    )
    gate_silu, silu_pull = jax.vjp(jax.nn.silu, gate_part)
    gated_out = mixed_out * gate_silu
    square_sum = lax.psum(jnp.sum(gated_out * gated_out, axis=1), "tensor")
    gate_scale = lax.rsqrt(square_sum / DI + EPSILON)[:, None]
    normed_out = (gated_out * gate_scale * gate_gain[layer_index][None, :]).astype(jnp.bfloat16)
    partial_out = jnp.dot(normed_out, out_full, preferred_element_type=jnp.float32)
    new_hidden = hidden + lax.psum(partial_out, "tensor")
    kept_values = (
        norm_pull,
        normed,
        silu_pull,
        gate_silu,
        mixed_out,
        gated_out,
        gate_scale,
        normed_out,
        conv_pull,
        rate_pull,
        summary_pull,
        output_pull,
        span_decay,
        entry_state,
        identity,
        local_width,
        edge_count,
    )
    return (new_hidden, kept_values)


def backward_layer(grad_hidden, weights, small_params, kept_values, layer_index):
    inner_full, rate_full, state_full, out_full = weights
    gate_gain = small_params[8]
    (
        norm_pull,
        normed,
        silu_pull,
        gate_silu,
        mixed_out,
        gated_out,
        gate_scale,
        normed_out,
        conv_pull,
        rate_pull,
        summary_pull,
        output_pull,
        span_decay,
        entry_state,
        identity,
        local_width,
        edge_count,
    ) = kept_values
    seq_rows = normed.shape[0]
    grad_low = grad_hidden.astype(jnp.bfloat16)
    grad_out_weight = jnp.dot(normed_out.T, grad_low, preferred_element_type=jnp.float32)
    grad_normed_out = jnp.dot(grad_low, out_full.T, preferred_element_type=jnp.float32)
    grad_gate_gain = jnp.sum(grad_normed_out * gated_out * gate_scale, axis=0)
    scaled_grad = grad_normed_out * gate_gain[layer_index][None, :]
    inner_sum = lax.psum(jnp.sum(scaled_grad * gated_out, axis=1), "tensor")
    scale_cube = gate_scale * gate_scale * gate_scale
    grad_gated = gate_scale * scaled_grad - gated_out * scale_cube * (inner_sum[:, None] / DI)
    grad_mixed = grad_gated * gate_silu
    grad_gate = silu_pull(grad_gated * mixed_out)[0]
    grad_inputs, grad_keys, grad_queries, grad_rates, grad_decays, grad_entry, grad_skip_gain = (
        output_pull(grad_mixed)
    )
    end_grads = carried_in_2((span_decay, grad_entry), "seq", chain_combine, identity)[1]
    grad_span_decay = jnp.sum(end_grads * entry_state, axis=(1, 2))
    more_inputs, more_keys, more_rates, more_decays = summary_pull((grad_span_decay, end_grads))
    grad_raw, grad_rate_bias, grad_decay_log = rate_pull(
        (grad_rates + more_rates, grad_decays + more_decays)
    )
    grad_activated = jnp.concatenate(
        [(grad_inputs + more_inputs).reshape(seq_rows, -1), grad_keys + more_keys, grad_queries],
        axis=1,
    )
    grad_padded, grad_conv_weight, grad_conv_bias = conv_pull(grad_activated)
    edge_back = shifted(grad_padded[:edge_count], "seq", -1)
    grad_conv_input = grad_padded[edge_count:]
    grad_conv_input = jnp.concatenate(
        [
            grad_conv_input[: seq_rows - edge_count],
            grad_conv_input[seq_rows - edge_count :] + edge_back,
        ],
        axis=0,
    )
    grad_inner_low = jnp.concatenate([grad_gate, grad_conv_input[:, :local_width]], axis=1).astype(
        jnp.bfloat16
    )
    grad_state_raw = grad_conv_input[:, local_width:]
    grad_rate_low = grad_raw.astype(jnp.bfloat16)
    grad_inner_weight = jnp.dot(normed.T, grad_inner_low, preferred_element_type=jnp.float32)
    grad_rate_weight = jnp.dot(normed.T, grad_rate_low, preferred_element_type=jnp.float32)
    grad_state_weight = product(normed.astype(jnp.float32).T, grad_state_raw)
    grad_normed_part = (
        jnp.dot(grad_inner_low, inner_full.T, preferred_element_type=jnp.float32)
        + jnp.dot(grad_rate_low, rate_full.T, preferred_element_type=jnp.float32)
        + product(grad_state_raw, state_full.astype(jnp.float32).T)
    )
    grad_normed, grad_conv_state, grad_bias_state = (
        lax.psum(grad_normed_part.astype(jnp.bfloat16), "tensor").astype(jnp.float32),
        lax.psum(grad_conv_weight[:, local_width:].astype(jnp.bfloat16), "tensor").astype(
            jnp.float32
        ),
        lax.psum(grad_conv_bias[local_width:].astype(jnp.bfloat16), "tensor").astype(jnp.float32),
    )
    grad_hidden_norm, grad_norm_gain = norm_pull(grad_normed)
    layer_grads = (
        grad_inner_weight.reshape(grad_inner_weight.shape[0], 2, local_width),
        grad_rate_weight,
        grad_state_weight,
        grad_out_weight,
        grad_norm_gain,
        grad_conv_weight[:, :local_width],
        grad_conv_bias[:local_width],
        grad_conv_state,
        grad_bias_state,
        grad_rate_bias,
        grad_decay_log,
        grad_skip_gain,
        grad_gate_gain,
    )
    return (grad_hidden + grad_hidden_norm, layer_grads)


def stack_layers(layer_sums, position):
    return jnp.stack([grads_here[position] for grads_here in layer_sums])


def span_body(
    tokens,
    cotangent,
    norm_gain,
    inner_weight,
    rate_weight,
    state_weight,
    conv_inner,
    bias_inner,
    conv_state,
    bias_state,
    rate_bias,
    decay_log,
    skip_gain,
    gate_gain,
    out_weight,
):
    small_params = (
        norm_gain,
        conv_inner,
        bias_inner,
        conv_state,
        bias_state,
        rate_bias,
        decay_log,
        skip_gain,
        gate_gain,
    )
    layer_count = norm_gain.shape[0]
    batch_count = tokens.shape[0]
    results = []
    kept_batches = []
    for batch_index in range(batch_count):
        hidden = tokens[batch_index, 0].astype(jnp.float32)
        kept_layers = []
        for layer_index in range(layer_count):
            weights = gather_layer(inner_weight, rate_weight, state_weight, out_weight, layer_index)
            hidden, kept_values = forward_layer(hidden, weights, small_params, layer_index)
            kept_layers.append(kept_values)
        results.append(hidden)
        kept_batches.append(kept_layers)
    layer_sums = [None] * layer_count
    seq_grads = []
    for batch_index in range(batch_count):
        grad_hidden = cotangent[batch_index, 0].astype(jnp.float32)
        for layer_index in reversed(range(layer_count)):
            weights = gather_layer(inner_weight, rate_weight, state_weight, out_weight, layer_index)
            grad_hidden, layer_grads = backward_layer(
                grad_hidden,
                weights,
                small_params,
                kept_batches[batch_index][layer_index],
                layer_index,
            )
            if layer_sums[layer_index] is None:
                layer_sums[layer_index] = layer_grads
            else:
                layer_sums[layer_index] = tuple(
                    (older + newer for older, newer in zip(layer_sums[layer_index], layer_grads))
                )
        seq_grads.append(grad_hidden)
    shard_inner, shard_rate, shard_out = (
        lax.psum_scatter(
            stack_layers(layer_sums, 0), ("dp", "seq"), scatter_dimension=1, tiled=True
        ),
        lax.psum_scatter(
            stack_layers(layer_sums, 1), ("dp", "seq"), scatter_dimension=1, tiled=True
        ),
        lax.psum_scatter(
            stack_layers(layer_sums, 3), ("dp", "seq"), scatter_dimension=2, tiled=True
        ),
    )
    shard_state = lax.psum_scatter(
        stack_layers(layer_sums, 2), ("dp", "seq", "tensor"), scatter_dimension=1, tiled=True
    )
    summed_small = lax.psum(
        (
            stack_layers(layer_sums, 4),
            stack_layers(layer_sums, 5),
            stack_layers(layer_sums, 6),
            stack_layers(layer_sums, 7),
            stack_layers(layer_sums, 8),
            stack_layers(layer_sums, 9),
            stack_layers(layer_sums, 10),
            stack_layers(layer_sums, 11),
            stack_layers(layer_sums, 12),
        ),
        ("dp", "seq"),
    )
    output = jnp.stack(results)[:, None]
    input_grad = jnp.stack(seq_grads)[:, None]
    return (
        output,
        input_grad,
        summed_small[0],
        shard_inner,
        shard_rate,
        shard_state,
        summed_small[1],
        summed_small[2],
        summed_small[3],
        summed_small[4],
        summed_small[5],
        summed_small[6],
        summed_small[7],
        summed_small[8],
        shard_out,
    )


GROUP = ("seq", "tensor")
LANES = 128
ROWS = 8
BF16, F32 = jnp.bfloat16, jnp.float32


def hop(value, first, second):
    pairs = [
        (place * 2 + core, (place ^ (second if core else first)) * 2 + core)
        for place in range(4)
        for core in range(2)
    ]
    return lax.ppermute(value, GROUP, pairs)


def swap(value):
    return lax.ppermute(value, "tensor", [(0, 1), (1, 0)])


def places():
    place, core = lax.axis_index("seq"), lax.axis_index("tensor")
    return place, core, place ^ (1 + core), place ^ (2 - core), place ^ 3


def put(buffer, block, *index):
    spots = index + (0,) * (buffer.ndim - len(index))
    return lax.dynamic_update_slice(buffer, block.reshape((1,) * len(index) + block.shape), spots)


def pick(array, index, axis=0):
    return lax.dynamic_index_in_dim(array, index, axis, False)


def line_shift(value, axis, step):
    count = lax.axis_size(axis)
    return lax.ppermute(value, axis, [(i, (i + step) % count) for i in range(count)])


def line_place(blocks, columns):
    count, place, rows = lax.axis_size("dp"), lax.axis_index("dp"), blocks[0].shape[0]
    out = jnp.zeros((count * rows, columns), blocks[0].dtype)
    for step, block in enumerate(blocks):
        out = lax.dynamic_update_slice(out, block, ((place - step) % count * rows, 0))
    return out


def line_near(block):
    count = lax.axis_size("dp")
    return jnp.stack([block] + [line_shift(block, "dp", step) for step in range(1, count)])


def line_sum_steps(part):
    count, place = lax.axis_size("dp"), lax.axis_index("dp")
    sent = [part((place + step) % count).astype(BF16) for step in range(1, count)]
    got = [line_shift(value, "dp", step + 1) for step, value in enumerate(sent)]
    token = yield sent
    total = part(place)
    for value in gate(got, token):
        total = total + value.astype(F32)
    return total


def seq_trade(parts):
    place = lax.axis_index("seq")
    out = put(jnp.zeros_like(parts), pick(parts, place), place)
    for turn in (1, 2, 3):
        got = lax.ppermute(pick(parts, place ^ turn), "seq", [(i, i ^ turn) for i in range(4)])
        out = put(out, got, place ^ turn)
    return out


def mesh_sum_steps(value):
    count = lax.axis_size("dp")
    turns = [("seq", 4, 1), ("seq", 4, 2)]
    turns += [("dp", count, 1 << bit) for bit in range(count.bit_length() - 1)]
    for axis, size, turn in turns:
        moved = lax.ppermute(value, axis, [(i, i ^ turn) for i in range(size)])
        token = yield value
        value = value + gate(moved, token)
    return value


def trade_steps(parts):
    place = lax.axis_index("seq")
    sent = [pick(parts, place ^ turn) for turn in (1, 2, 3)]
    got = [
        lax.ppermute(value, "seq", [(i, i ^ turn) for i in range(4)])
        for turn, value in zip((1, 2, 3), sent)
    ]
    token = yield sent
    out = put(jnp.zeros_like(parts), pick(parts, place), place)
    for turn, value in zip((1, 2, 3), gate(got, token)):
        out = put(out, value, place ^ turn)
    return out


def dot(left, right, left_dim=1, right_dim=0):
    return lax.dot_general(
        left, right, (((left_dim,), (right_dim,)), ((), ())), preferred_element_type=F32
    )


def split(value, count):
    pieces = []
    for _ in range(count):
        piece = value.astype(BF16)
        pieces.append(piece)
        value = value - piece.astype(F32)
    return pieces


def exact_left(value, ones, count, right_dim=0):
    rows = value.shape[0]
    stacked = dot(jnp.concatenate(split(value, count), axis=0), ones, 1, right_dim)
    total = stacked[:rows]
    for index in range(1, count):
        total = total + stacked[index * rows : (index + 1) * rows]
    return total


def head_sums(picker, value):
    high, low_part = split(value, 2)
    return dot(picker, high, 1, 1) + dot(picker, low_part, 1, 1)


def front(raw, window, taps, heads, spread, upper, width, state, extra):
    length = raw.shape[0]
    summed = taps[4:5, :] + taps[0:1, :] * window[5 : 5 + length, :]
    for tap in range(1, 4):
        summed = summed + taps[tap : tap + 1, :] * window[5 + tap : 5 + tap + length, :]
    sig = jax.nn.sigmoid(summed)
    activated = summed * sig
    rates = jnp.transpose(raw[:, 2 * width + 2 * state :])[:ROWS] + heads[0:ROWS, :]
    steps = jnp.maximum(rates, 0.0) + jnp.log1p(jnp.exp(-jnp.abs(rates)))
    decays = -jnp.exp(heads[ROWS : 2 * ROWS, :]) * steps
    running = exact_left(decays, upper, 3)
    ending = running[:, length - 1 : length]
    grown = jnp.exp(running)
    tail = jnp.exp(ending - running)
    rows = [steps, running, grown, tail] + extra
    rows.append(jnp.zeros((LANES // 2 - ROWS * len(rows), length), F32))
    rows = jnp.concatenate(rows, axis=0)
    high = rows.astype(BF16).astype(F32)
    halves = jnp.transpose(jnp.concatenate([high, rows - high], axis=0))
    columns = halves[:, : LANES // 2] + halves[:, LANES // 2 :]
    wide = dot(halves.astype(BF16), spread)
    whole_decay = jnp.exp(jnp.broadcast_to(ending, (ROWS, LANES)))
    inputs = activated[:, :width]
    return dict(
        summed=summed,
        sig=sig,
        inputs=inputs,
        keys=activated[:, width : width + state].astype(BF16),
        queries=activated[:, width + state :].astype(BF16),
        rates=rates,
        decays=decays,
        running=running,
        columns=columns,
        steps_wide=wide[:, :width],
        grown_wide=wide[:, width : 2 * width],
        tail_wide=wide[:, 2 * width : 3 * width],
        whole_decay=whole_decay,
    )


def per_row(whole_decay, head_count, head_size):
    return jnp.concatenate(
        [
            jnp.broadcast_to(whole_decay[h : h + 1, :], (head_size, LANES))
            for h in range(head_count)
        ],
        axis=0,
    )


def decay_matrix(parts, h, causal):
    length = causal.shape[0]
    column = parts["columns"][:, ROWS + h : ROWS + h + 1]
    row = parts["running"][h : h + 1, :]
    gap = jnp.broadcast_to(column, (length, length)) - row
    return jnp.exp(jnp.where(causal, gap, -1e30))


def causal_mask(length):
    return lax.broadcasted_iota(jnp.int32, (length, length), 0) >= lax.broadcasted_iota(
        jnp.int32, (length, length), 1
    )


def forward_kernel(
    head_size,
    order_ref,
    raw_first,
    raw_second,
    taps_ref,
    chans_ref,
    heads_ref,
    spread_ref,
    upper_ref,
    value_ref,
    square_ref,
    mixed_ref,
    state_ref,
    carry,
    window_first,
    window_second,
):
    length, width, state = raw_first.shape[0], chans_ref.shape[1], carry.shape[1]
    conv_width = width + 2 * state
    head_count = width // head_size
    pair = LANES // head_size
    step = pl.program_id(0)

    @pl.when(step == 0)
    def _():
        carry[...] = jnp.zeros_like(carry)
        window_first[0:ROWS, :] = jnp.zeros((ROWS, conv_width), F32)

    raws = [raw_first[...], raw_second[...]]
    windows = [window_first, window_second]
    for raw, window in zip(raws, windows):
        window[ROWS : ROWS + length, :] = raw[:, width : width + conv_width].astype(BF16).astype(F32)
    window_second[0:ROWS, :] = window_first[length : length + ROWS, :]
    taps, heads = taps_ref[...], heads_ref[...]
    fronts = [
        front(raw, window, taps, heads, spread_ref[...], upper_ref[...], width, state, [])
        for raw, window in zip(raws, windows)
    ]
    window_first[0:ROWS, :] = window_second[length : length + ROWS, :]
    causal = causal_mask(length)
    lane = lax.broadcasted_iota(jnp.int32, (length, LANES), 1) // head_size
    insides, steppeds = [], []
    for parts in fronts:
        stepped = parts["inputs"] * parts["steps_wide"]
        stepped_low = stepped.astype(BF16)
        scores = dot(parts["queries"], parts["keys"], 1, 1)
        columns = []
        for block in range(head_count // pair):
            source = stepped_low[:, block * LANES : (block + 1) * LANES]
            joined = None
            for k in range(pair):
                mixing = (scores * decay_matrix(parts, block * pair + k, causal)).astype(BF16)
                got = dot(mixing, source)
                joined = got if joined is None else jnp.where(lane == k, got, joined)
            columns.append(joined)
        insides.append(jnp.concatenate(columns, axis=1))
        steppeds.append(stepped)
    updates = [
        dot((stepped * parts["tail_wide"]).astype(BF16), parts["keys"], 0, 0)
        for stepped, parts in zip(steppeds, fronts)
    ]
    before = carry[...]
    for sub, (raw, parts, inside, update) in enumerate(zip(raws, fronts, insides, updates)):
        inputs = parts["inputs"]
        state_ref[sub] = before
        carried = dot(parts["queries"], before.astype(BF16), 1, 1)
        mixed = inside + carried * parts["grown_wide"] + chans_ref[0:1, :] * inputs
        before = per_row(parts["whole_decay"], head_count, head_size) * before + update
        gate_part = raw[:, :width]
        gated = mixed * (gate_part * jax.nn.sigmoid(gate_part))
        rows = pl.ds(pl.multiple_of(order_ref[2 * step + sub] * length, length), length)
        mixed_ref[rows, :] = mixed
        value_ref[rows, :] = (gated * chans_ref[1:2, :]).astype(BF16)
        squares = jnp.sum(gated * gated, axis=1, keepdims=True)
        square_ref[sub * ROWS : (sub + 1) * ROWS, :] = jnp.transpose(
            jnp.broadcast_to(squares, (length, length))
        )[:ROWS]
    carry[...] = before


def backward_kernel(
    head_size,
    inner_count,
    order_ref,
    grad_first,
    grad_second,
    raw_first,
    raw_second,
    past_ref,
    mixed_first,
    mixed_second,
    state_ref,
    token_ref,
    taps_ref,
    chans_ref,
    heads_ref,
    spread_ref,
    upper_ref,
    picker_ref,
    back_ref,
    taps_out,
    chans_out,
    heads_out,
    carry,
    window_first,
    window_second,
    later_first,
    later_second,
):
    length, width, state = raw_first.shape[0], chans_ref.shape[1], carry.shape[1]
    conv_width = width + 2 * state
    head_count = width // head_size
    pair = LANES // head_size
    step, count = pl.program_id(0), pl.num_programs(0)

    @pl.when(step == 0)
    def _():
        carry[...] = jnp.zeros_like(carry)
        later_first[length : length + ROWS, :] = jnp.zeros((ROWS, conv_width), F32)
        taps_out[...] = jnp.zeros_like(taps_out)
        chans_out[...] = jnp.zeros_like(chans_out)
        heads_out[...] = jnp.zeros_like(heads_out)

    raws = [raw_first[...], raw_second[...]]
    windows, laters = [window_first, window_second], [later_first, later_second]
    conv = slice(width, width + conv_width)
    for raw, window in zip(raws, windows):
        window[ROWS : ROWS + length, :] = raw[:, conv].astype(BF16).astype(F32)
    window_first[0:ROWS, :] = window_second[length : length + ROWS, :]
    past = past_ref[:, conv].astype(BF16).astype(F32)
    window_second[0:ROWS, :] = jnp.where(step == count - 1, 0.0, past)
    taps, heads, picker = taps_ref[...], heads_ref[...], picker_ref[...]
    skip, gain = chans_ref[0:1, :], chans_ref[1:2, :]
    causal = causal_mask(length)
    lane = lax.broadcasted_iota(jnp.int32, (length, LANES), 1)
    head_lane = lane // head_size
    places_of = [
        pl.ds(pl.multiple_of(order_ref[2 * count - 1 - 2 * step - sub] * length, length), length)
        for sub in range(2)
    ]

    fronts, held = [], []
    for sub, (raw, window, grad_ref, mixed_ref) in enumerate(
        zip(raws, windows, (grad_first, grad_second), (mixed_first, mixed_second))
    ):
        token = token_ref[(1 - sub) * ROWS : (2 - sub) * ROWS, :]
        parts = front(
            raw, window, taps, heads, spread_ref[...], upper_ref[...], width, state, [token]
        )
        fronts.append(parts)
        inputs = parts["inputs"]
        scale = parts["columns"][:, 4 * ROWS : 4 * ROWS + 1]
        inner = parts["columns"][:, 4 * ROWS + 1 : 4 * ROWS + 2]
        gate_part, mixed = raw[:, :width], mixed_ref[...]
        gate_sig = jax.nn.sigmoid(gate_part)
        gate_silu = gate_part * gate_sig
        gated = mixed * gate_silu
        grad = grad_ref[...]
        gain_term = jnp.sum(grad * (gated * scale), axis=0, keepdims=True)
        grad_gated = scale * (grad * gain) - gated * (scale * scale * scale * inner / inner_count)
        grad_mixed = grad_gated * gate_silu
        back_ref[places_of[sub], :width] = (
            grad_gated * mixed * (gate_sig + gate_silu * (1.0 - gate_sig))
        ).astype(BF16)
        chans_out[0:1, :] += jnp.sum(grad_mixed * inputs, axis=0, keepdims=True)
        chans_out[1:2, :] += gain_term
        held.append(grad_mixed)

    works = []
    for parts, grad_mixed in zip(fronts, held):
        stepped = parts["inputs"] * parts["steps_wide"]
        stepped_low, grad_low = stepped.astype(BF16), grad_mixed.astype(BF16)
        scores = dot(parts["queries"], parts["keys"], 1, 1)
        grad_scores = jnp.zeros((length, length), F32)
        row_sums = jnp.zeros((length, length), F32)
        column_sums, columns = [], []
        for block in range(head_count // pair):
            cut = slice(block * LANES, (block + 1) * LANES)
            source, target = stepped_low[:, cut], grad_low[:, cut]
            joined = None
            for k in range(pair):
                h = block * pair + k
                spread_h = decay_matrix(parts, h, causal)
                own_target = jnp.where(head_lane == k, target, jnp.zeros_like(target))
                pulled = dot(own_target, source, 1, 1) * spread_h
                grad_scores = grad_scores + pulled
                moved = pulled * scores
                row_sums = jnp.where(lane == h, jnp.sum(moved, axis=1, keepdims=True), row_sums)
                column_sums.append(jnp.sum(moved, axis=0, keepdims=True))
                got = dot((scores * spread_h).astype(BF16), target, 0, 0)
                joined = got if joined is None else jnp.where(head_lane == k, got, joined)
            columns.append(joined)
        column_sums.append(jnp.zeros((ROWS - head_count, length), F32))
        differences = jnp.transpose(row_sums)[:ROWS] - jnp.concatenate(column_sums, axis=0)
        works.append((stepped, grad_scores, jnp.concatenate(columns, axis=1), differences))

    after = carry[...]
    row_lane = lax.broadcasted_iota(jnp.int32, (ROWS, length), 1)
    row_head = lax.broadcasted_iota(jnp.int32, (ROWS, length), 0)
    for sub, (parts, grad_mixed, work) in enumerate(zip(fronts, held, works)):
        inputs, keys, queries = parts["inputs"], parts["keys"], parts["queries"]
        stepped, grad_scores, inside, differences = work
        window, later = windows[sub], laters[sub]
        before = state_ref[1 - sub]
        before_low, after_low = before.astype(BF16), after.astype(BF16)
        tail_wide, grown_wide = parts["tail_wide"], parts["grown_wide"]
        through = tail_wide * dot(keys, after_low, 1, 1)
        grad_stepped = inside + through
        ended = stepped * through
        carried = dot(queries, before_low, 1, 1) * grown_wide
        kept = per_row(parts["whole_decay"], head_count, head_size) * after
        kept_sum = jnp.sum(kept * before, axis=1, keepdims=True)
        kept_heads = jnp.concatenate(
            [
                jnp.sum(kept_sum[h * head_size : (h + 1) * head_size], axis=0, keepdims=True)
                for h in range(head_count)
            ]
            + [jnp.zeros((ROWS - head_count, 1), F32)],
            axis=0,
        )
        ended_heads = head_sums(picker, ended)
        grad_running = differences + head_sums(picker, grad_mixed * carried) - ended_heads
        last = jnp.sum(ended_heads, axis=1, keepdims=True) + kept_heads
        grad_running = grad_running + jnp.where(row_lane == length - 1, last, 0.0)
        grad_decays = exact_left(grad_running, upper_ref[...], 3, 1)
        grad_steps = head_sums(picker, inputs * grad_stepped)
        grad_rates = (
            grad_steps - jnp.exp(heads[ROWS : 2 * ROWS, :]) * grad_decays
        ) * jax.nn.sigmoid(parts["rates"])
        grad_rates = jnp.where(row_head < head_count, grad_rates, 0.0)
        heads_out[0:ROWS, :] += grad_rates
        heads_out[ROWS : 2 * ROWS, :] += grad_decays * parts["decays"]
        back_ref[places_of[sub], 2 * width + 2 * state :] = jnp.transpose(
            jnp.concatenate([grad_rates, jnp.zeros((LANES - ROWS, length), F32)], axis=0)
        ).astype(BF16)

        grad_inputs = parts["steps_wide"] * grad_stepped + skip * grad_mixed
        grown_low = (grown_wide * grad_mixed).astype(BF16)
        scores_low = grad_scores.astype(BF16)
        grad_queries = dot(scores_low, keys) + dot(grown_low, before_low)
        grad_keys = dot(scores_low, queries, 0, 0) + dot(
            (stepped * tail_wide).astype(BF16), after_low
        )
        after = kept + dot(grown_low, queries, 0, 0)

        sig, summed = parts["sig"], parts["summed"]
        grad_v = jnp.concatenate([grad_inputs, grad_keys, grad_queries], axis=1) * (
            sig + summed * sig * (1.0 - sig)
        )
        later[0:length, :] = grad_v
        grad_conv = taps[3:4, :] * grad_v
        taps_out[4:5, :] += jnp.sum(grad_v, axis=0, keepdims=True)
        for tap in range(4):
            if tap < 3:
                moved = later[3 - tap : 3 - tap + length, :]
                grad_conv = grad_conv + taps[tap : tap + 1, :] * moved
            taps_out[tap : tap + 1, :] += jnp.sum(
                grad_v * window[5 + tap : 5 + tap + length, :], axis=0, keepdims=True
            )
        laters[1 - sub][length : length + ROWS, :] = grad_v[0:ROWS]
        back_ref[places_of[sub], conv] = grad_conv.astype(BF16)
    carry[...] = after


def tables(width, head_size):
    channel_head = jnp.arange(width)[None, :] // head_size
    rows = jnp.arange(LANES)[:, None]
    spread = jnp.concatenate(
        [rows % (LANES // 2) == channel_head + ROWS * kind for kind in (0, 2, 3)], axis=1
    ).astype(BF16)
    upper = (rows <= jnp.arange(LANES)[None, :]).astype(BF16)
    picker = (jnp.arange(ROWS)[:, None] == channel_head).astype(BF16)
    return spread, upper, picker


def fixed(shape):
    return pl.BlockSpec(shape, lambda i, order: (0,) * len(shape))


def mix_forward(raw, order, small, tabs, head_size, width, state):
    taps, chans, heads = small
    spread, upper, _ = tabs
    tokens, columns = raw.shape
    count = tokens // STRETCH

    def moved(sub):
        return pl.BlockSpec((STRETCH, columns), lambda i, order: (order[2 * i + sub], 0))

    return pl.pallas_call(
        lambda *refs: forward_kernel(head_size, *refs),
        grid_spec=pltpu.PrefetchScalarGridSpec(
            num_scalar_prefetch=1,
            grid=(count // 2,),
            in_specs=[
                moved(0),
                moved(1),
                fixed(taps.shape),
                fixed(chans.shape),
                fixed(heads.shape),
                fixed(spread.shape),
                fixed(upper.shape),
            ],
            out_specs=[
                fixed((tokens, width)),
                pl.BlockSpec((2 * ROWS, LANES), lambda i, order: (i, 0)),
                fixed((tokens, width)),
                pl.BlockSpec((2, width, state), lambda i, order: (i, 0, 0)),
            ],
            scratch_shapes=[
                pltpu.VMEM((width, state), F32),
                pltpu.VMEM((STRETCH + ROWS, width + 2 * state), F32),
                pltpu.VMEM((STRETCH + ROWS, width + 2 * state), F32),
            ],
        ),
        out_shape=[
            jax.ShapeDtypeStruct((tokens, width), BF16),
            jax.ShapeDtypeStruct((count * ROWS, LANES), F32),
            jax.ShapeDtypeStruct((tokens, width), F32),
            jax.ShapeDtypeStruct((count, width, state), F32),
        ],
        compiler_params=pltpu.CompilerParams(
            dimension_semantics=("arbitrary",), vmem_limit_bytes=20 * 2**20
        ),
        cost_estimate=pl.CostEstimate(
            flops=11_000_000_000, bytes_accessed=10_000_000, transcendentals=0
        ),
    )(order, raw, raw, taps, chans, heads, spread, upper)


def mix_backward(grad, raw, mixed, states, token_rows, order, small, tabs, head_size, inner_count):
    taps, chans, heads = small
    spread, upper, picker = tabs
    tokens, columns = raw.shape
    width, state = states.shape[1:]
    count = tokens // STRETCH
    per = STRETCH // ROWS

    steps = count // 2

    def moved(sub, extent):
        return pl.BlockSpec(
            (STRETCH, extent), lambda i, order: (order[count - 1 - 2 * i - sub], 0)
        )

    def past(i, order):
        return (order[jnp.maximum(count - 3 - 2 * i, 0)] * per + per - 1, 0)

    return pl.pallas_call(
        lambda *refs: backward_kernel(head_size, inner_count, *refs),
        grid_spec=pltpu.PrefetchScalarGridSpec(
            num_scalar_prefetch=1,
            grid=(steps,),
            in_specs=[
                moved(0, width),
                moved(1, width),
                moved(0, columns),
                moved(1, columns),
                pl.BlockSpec((ROWS, columns), past),
                moved(0, width),
                moved(1, width),
                pl.BlockSpec((2, width, state), lambda i, order: (steps - 1 - i, 0, 0)),
                pl.BlockSpec((2 * ROWS, LANES), lambda i, order: (steps - 1 - i, 0)),
                fixed(taps.shape),
                fixed(chans.shape),
                fixed(heads.shape),
                fixed(spread.shape),
                fixed(upper.shape),
                fixed(picker.shape),
            ],
            out_specs=[
                fixed((tokens, columns)),
                fixed(taps.shape),
                fixed(chans.shape),
                fixed(heads.shape),
            ],
            scratch_shapes=[pltpu.VMEM((width, state), F32)]
            + [pltpu.VMEM((STRETCH + ROWS, width + 2 * state), F32) for _ in range(4)],
        ),
        out_shape=[
            jax.ShapeDtypeStruct((tokens, columns), BF16),
            jax.ShapeDtypeStruct(taps.shape, F32),
            jax.ShapeDtypeStruct(chans.shape, F32),
            jax.ShapeDtypeStruct(heads.shape, F32),
        ],
        compiler_params=pltpu.CompilerParams(
            dimension_semantics=("arbitrary",), vmem_limit_bytes=24 * 2**20
        ),
        cost_estimate=pl.CostEstimate(
            flops=23_000_000_000, bytes_accessed=16_000_000, transcendentals=0
        ),
    )(
        order,
        grad,
        grad,
        raw,
        raw,
        raw,
        mixed,
        mixed,
        states,
        token_rows,
        taps,
        chans,
        heads,
        spread,
        upper,
        picker,
    )


def small_kernel(layers, heads_here, head_count, state, spot_ref, place_ref, arrived_ref, out_ref):
    share = arrived_ref.shape[1]
    rows = share // layers
    row = lax.broadcasted_iota(jnp.int32, (LANES, LANES), 0)
    lane = lax.broadcasted_iota(jnp.int32, (LANES, LANES), 1)
    chosen = []
    for layer in range(layers):
        source = lane + layer * heads_here + place_ref[0] * head_count
        chosen.append(((row == source) & (lane < head_count)).astype(BF16))
    for index in range(out_ref.shape[1] // share):
        pair = [arrived_ref[spot_ref[2 * index + which]] for which in range(2)]
        own = jnp.where(place_ref[1] == 0, pair[0][:, 2 * state :], pair[1][:, 2 * state :])
        turned = jnp.concatenate([own.astype(F32), jnp.zeros((LANES - share, LANES), F32)], axis=0)
        turned = jnp.transpose(turned)[:share].astype(BF16)
        spot = index * share
        for layer in range(layers):
            cut = slice(layer * rows, (layer + 1) * rows)
            out_ref[layer, spot : spot + rows, : 2 * state] = pair[0][cut, : 2 * state]
            out_ref[layer, spot + rows : spot + share, : 2 * state] = pair[1][cut, : 2 * state]
            out_ref[layer, spot : spot + share, 2 * state :] = dot(turned, chosen[layer]).astype(BF16)


def small_unpack(arrived, order, layers, heads_here, head_count, state):
    line, share, columns = arrived.shape[0] // 8, arrived.shape[1], arrived.shape[2]
    place, core = lax.axis_index("seq"), lax.axis_index("tensor")
    back = (lax.axis_index("dp") - jnp.arange(line)) % line
    spots = (order[None, :] * line + back[:, None]).reshape(-1).astype(jnp.int32)
    scalars = pl.BlockSpec(memory_space=pltpu.SMEM)
    return pl.pallas_call(
        lambda *refs: small_kernel(layers, heads_here, head_count, state, *refs),
        in_specs=[scalars, scalars, pl.BlockSpec(memory_space=pltpu.VMEM)],
        out_shape=jax.ShapeDtypeStruct((layers, line * 4 * share, columns), BF16),
        compiler_params=pltpu.CompilerParams(vmem_limit_bytes=14 * 2**20),
    )(spots, jnp.stack([place, core]).astype(jnp.int32), arrived)


def finish_kernel(
    head_count, state, first_ref, second_ref, first_out, second_out, inner_ref, out_ref, state_ref, rate_ref
):
    width = out_ref.shape[2] // 4
    share = out_ref.shape[1]
    for layer, (ref, more) in enumerate(((first_ref, first_out), (second_ref, second_out))):
        states = jnp.zeros((share, 2 * state), F32)
        rates = []
        for index in range(4):
            value = ref[index].astype(F32)
            spot = slice(index * width, (index + 1) * width)
            inner_ref[layer, :, 0, spot] = value[:, :width]
            inner_ref[layer, :, 1, spot] = value[:, width : 2 * width]
            states = states + value[:, 2 * width : 2 * width + 2 * state]
            rate = jnp.concatenate(
                [value[:, 2 * width + 2 * state :], jnp.zeros((LANES - share, LANES), F32)], axis=0
            )
            rates.append(jnp.transpose(rate)[:head_count, :share])
            out_ref[layer, :, spot] = more[index].astype(F32)
        rate_ref[layer] = jnp.concatenate(rates, axis=0)
        state_ref[layer] = states


def finish(first, second, first_out, second_out, head_count, state, width):
    share = first.shape[1]
    return pl.pallas_call(
        lambda *refs: finish_kernel(head_count, state, *refs),
        out_shape=[
            jax.ShapeDtypeStruct((2, share, 2, 4 * width), F32),
            jax.ShapeDtypeStruct((2, share, 4 * width), F32),
            jax.ShapeDtypeStruct((2, share, 2 * state), F32),
            jax.ShapeDtypeStruct((2, 4 * head_count, share), F32),
        ],
        compiler_params=pltpu.CompilerParams(vmem_limit_bytes=14 * 2**20),
    )(first, second, first_out, second_out)


def norm_scale(hidden):
    return lax.rsqrt(jnp.mean(hidden * hidden, axis=1, keepdims=True) + EPSILON)


PLAN = (
    "v a l ga",
    "gb a v a",
    "b ga gb a",
    "b a b ga",
    "gb a b a",
    "b a b l",
    "a b a b",
    "a b a b",
    "a b a b",
    "a b a b",
    "a b a b",
    "a b oa1 a",
    "b xo a b",
    "a ob1 b a",
    "q ia1 b xo",
    "a b ib1 r",
    "a b a b",
    "a oa0 a b",
    "ob0 y ia0 b",
    "ib0 u a b",
    "a m b y",
    "q m b q",
    "m y b xg",
    "m r m r",
    "xg m u u",
)


def gate(value, token):
    return value if token is None else lax.optimization_barrier((value, token))[0]


def gather_steps(block):
    from_near, from_far = hop(block, 1, 2), hop(block, 2, 1)
    token = yield block
    from_near = gate(from_near, token)
    from_across = hop(from_near, 2, 1)
    token = yield from_near
    four = jnp.stack([block, from_near, gate(from_far, token), gate(from_across, token)])
    twin = swap(four)
    token = yield four
    return jnp.concatenate([four, gate(twin, token)])


def scatter_steps(own, other, tiny=None):
    got = swap(other)
    moved = None if tiny is None else hop(tiny, 1, 2)
    token = yield other
    got = gate(got, token)
    to_far = (own[2:].astype(F32) + got[2:].astype(F32)).astype(BF16)
    from_far = hop(to_far, 2, 1)
    if tiny is not None:
        tiny = tiny + gate(moved, token)
        moved = hop(tiny, 2, 1)
    token = yield to_far
    from_far = gate(from_far, token)
    both = own[:2].astype(F32) + got[:2].astype(F32) + from_far.astype(F32)
    side = both[1].astype(BF16)
    from_near = hop(side, 1, 2)
    if tiny is not None:
        tiny = tiny + gate(moved, token)
        moved = swap(tiny)
    token = yield (side, both[0])
    total = both[0] + gate(from_near, token).astype(F32)
    if tiny is not None:
        tiny = tiny + gate(moved, token)
    return total, tiny


def arrival_order():
    place, core = lax.axis_index("seq"), lax.axis_index("tensor")
    block = jnp.arange(8)
    turn, their = block // 2 ^ place, block % 2
    first = jnp.where(their == 0, turn, jnp.where(turn == 1, 2, jnp.where(turn == 2, 1, turn)))
    return (first + jnp.where(their == core, 0, 4)).astype(jnp.int32)


class Track:
    def __init__(self):
        self.token = None
        self.chains = {}

    def begin(self, name, chain):
        next(chain)
        self.chains[name] = chain

    def run(self, *plan):
        for name in " ".join(plan).split():
            name, _, count = name.partition("*")
            for _ in range(int(count or 1)):
                try:
                    self.token = self.chains[name].send(self.token)
                except StopIteration:
                    pass


def late_gather(store, key, block):
    token = yield None
    store[key] = yield from gather_steps(gate(block, token))


def kept_result(store, key, chain):
    yield None
    store[key] = yield from chain


def together(main, side):
    token = yield (next(main), next(side))
    result, running = None, [True, True]
    while any(running):
        values = []
        for index, chain in enumerate((main, side)):
            if running[index]:
                try:
                    values.append(chain.send(token))
                except StopIteration as stop:
                    running[index] = False
                    result = stop.value if index == 0 else result
        if any(running):
            token = yield tuple(values)
    return result


def sum_steps(value, store, key):
    moved = hop(value, 1, 2)
    token = yield value
    value = value + gate(moved, token)
    moved = hop(value, 2, 1)
    token = yield value
    value = value + gate(moved, token)
    moved = swap(value)
    token = yield value
    store[key] = value + gate(moved, token)


def head_body(
    tokens,
    cotangent,
    norm_gain,
    inner_weight,
    rate_weight,
    state_weight,
    conv_inner,
    bias_inner,
    conv_state,
    bias_state,
    rate_bias,
    decay_log,
    skip_gain,
    gate_gain,
    out_weight,
):
    layers, batches = norm_gain.shape[0], tokens.shape[0]
    model = tokens.shape[3]
    place, core = lax.axis_index("seq"), lax.axis_index("tensor")
    line = lax.axis_size("dp")
    share, half_width = inner_weight.shape[1], inner_weight.shape[3]
    inner_count = half_width * 2
    width = half_width // 4
    head_count = rate_bias.shape[1] // 4
    head_size = width // head_count
    state_share, state = state_weight.shape[1], state_weight.shape[2] // 2
    own_rows = tokens.shape[2] // 2
    length = own_rows * 8
    conv_width = width + 2 * state
    columns = 2 * width + 2 * state + LANES
    heads_here = rate_weight.shape[2]
    tabs = tables(width, head_size)

    def own(array):
        return lax.dynamic_slice_in_dim(array, core * own_rows, own_rows, 0)

    def quarter(array, count):
        return lax.dynamic_slice_in_dim(array, place * count, count, array.ndim - 1)

    def out_share(layer):
        turned = out_weight[layer].T.reshape(share, 4, width)
        return turned.transpose(1, 0, 2)

    def inner_share(layer):
        cut = inner_weight[layer].reshape(share, 2, 4, width)
        return cut.transpose(2, 0, 1, 3).reshape(4, share, 2 * width)

    def first_for(taker):
        cut = lax.dynamic_slice(inner_weight[0], (0, 0, taker * width), (share, 2, width))
        return jnp.concatenate([cut[:, 0], cut[:, 1]], axis=1)

    out_weights, in_weights = {}, {}

    def first_out():
        token = yield None
        traded = yield from trade_steps(gate(out_share(0), token))
        traded = traded.reshape(4 * share, width)
        got = [line_shift(traded, "dp", step) for step in range(1, line)]
        token = yield traded
        out_weights[0] = line_place([traded] + gate(got, token), width)

    def later(layer):
        token = yield None
        mixed_share = jnp.concatenate([inner_share(layer), out_share(layer)], axis=2)
        traded = yield from trade_steps(gate(mixed_share, token))
        full = lax.all_gather(traded.reshape(4 * share, -1), "dp").reshape(model, -1)
        token = yield traded
        full = gate(full, token)
        out_weights[layer] = full[:, 2 * width :]
        in_weights[layer] = jnp.concatenate([full[:, : 2 * width], small_full[layer]], axis=1)
        yield in_weights[layer]

    first = put(jnp.zeros((4, share, 2 * width), BF16), first_for(place), place)
    first_sent = [first_for(place ^ turn) for turn in (1, 2, 3)]
    for turn, value in zip((1, 2, 3), first_sent):
        pairs = [(i, i ^ turn) for i in range(4)]
        first = put(first, lax.ppermute(value, "seq", pairs), place ^ turn)
    first = first.reshape(4 * share, 2 * width)
    rate_rows = rate_weight.transpose(0, 2, 1).reshape(layers * heads_here, share)
    rate_rows = jnp.pad(rate_rows, ((0, share - layers * heads_here), (0, LANES - share)))
    small_share = jnp.concatenate([state_weight.reshape(share, 2 * state), rate_rows], axis=1)
    small_near = line_near(small_share)

    smalls = []

    def prepare():
        token = yield None
        given = (conv_inner, conv_state, bias_inner, bias_state, skip_gain, gate_gain, rate_bias, decay_log)
        (
            conv_inner_,
            conv_state_,
            bias_inner_,
            bias_state_,
            skip_gain_,
            gate_gain_,
            rate_bias_,
            decay_log_,
        ) = gate(given, token)
        for layer in range(layers):
            taps = jnp.concatenate([quarter(conv_inner_[layer], width), conv_state_[layer]], axis=1)
            bias = jnp.concatenate([quarter(bias_inner_[layer], width), bias_state_[layer]])
            taps = jnp.concatenate([taps, bias[None], jnp.zeros((3, conv_width), F32)], axis=0)
            skip = jnp.repeat(quarter(skip_gain_[layer], head_count), head_size)
            chans = jnp.stack([skip, quarter(gate_gain_[layer], width)])
            chans = jnp.concatenate([chans, jnp.zeros((ROWS - 2, width), F32)], axis=0)
            heads = jnp.stack(
                [quarter(rate_bias_[layer], head_count), quarter(decay_log_[layer], head_count)]
            )
            heads = jnp.pad(heads, ((0, 0), (0, ROWS - head_count))).reshape(2 * ROWS, 1)
            smalls.append((taps, chans, jnp.broadcast_to(heads, (2 * ROWS, LANES))))
        yield smalls

    order = arrival_order()
    track = Track()
    track.token = (first_sent, small_share)
    hiddens = [own(tokens[batch, 0]).astype(F32) for batch in range(batches)]
    row_scales, normed_all, whole = [], {}, {}
    for batch in range(batches):
        row_scales.append(norm_scale(hiddens[batch]))
        normed = (hiddens[batch] * row_scales[batch] * norm_gain[0][None, :]).astype(BF16)
        normed = gate(normed, track.token)
        track.begin(str(batch), kept_result(normed_all, (0, batch), gather_steps(normed)))
    track.begin("s", kept_result(whole, "small", gather_steps(gate(small_near, first))))
    track.begin("p", prepare())
    grads, grad_all = [], {}
    for batch, name in enumerate(("ga", "gb")):
        low_part = own(gate(cotangent[batch, 0], first_sent))
        grads.append(low_part.astype(F32))
        track.begin(name, late_gather(grad_all, (layers - 1, batch), low_part))
    track.run("0 1")
    first_got = [line_shift(first, "dp", step) for step in range(1, line)]
    track.token = first
    track.run("s")
    track.token = first_got[0]
    track.run("0 1 s p", "0 1 s ga", "gb 0 1 s")
    track.begin("v", first_out())
    track.begin("l", later(1))
    track.run("v l")
    first_full = line_place(gate([first] + first_got, track.token), columns)
    small_full = small_unpack(
        whole["small"].reshape(-1, share, small_share.shape[1]),
        order,
        layers,
        heads_here,
        head_count,
        state,
    )
    in_weights[0] = lax.dynamic_update_slice(first_full, small_full[0], (0, 2 * width))
    track.token = first_full
    gradients, inners, terms, outputs = {}, {}, {}, {}

    def inner_products(grad_low, summed):
        inner = jnp.sum(grad_low.astype(F32) * summed, axis=1)
        return put(jnp.zeros((8, own_rows), F32), inner, place * 2 + core)

    moves = order[None, :] == jnp.arange(8)[:, None]

    def halves_of(value, weight):
        half = length // 2
        other = dot(value[half:], weight, 1, 1).astype(BF16)
        return (
            dot(value[:half], weight, 1, 1).astype(BF16).reshape(4, own_rows, model),
            other.reshape(4, own_rows, model),
        )

    def batch_chain(batch):
        token = yield None
        hidden, row_scale = hiddens[batch], row_scales[batch]
        normed = normed_all[0, batch]
        kept = {}
        for layer in range(layers):
            normed = normed.reshape(length, model)
            raw = dot(gate(normed, token), in_weights[layer])
            token = yield raw
            value, squares, mixed, states = mix_forward(
                gate(raw, token), order, smalls[layer], tabs, head_size, width, state
            )
            token = yield value
            halves = halves_of(gate(value, token), out_weights[layer])
            summed, squares = yield from scatter_steps(
                *halves, squares.reshape(-1, ROWS, LANES)[:, 0]
            )
            scales = lax.rsqrt(squares / inner_count + EPSILON)
            flat_scales = scales.reshape(8, own_rows)
            own_scale = pick(flat_scales, place * 2 + core)[:, None]
            arrived = jnp.sum(jnp.where(moves[:, :, None], flat_scales[None], 0.0), axis=1)
            normed_out = (value.astype(F32) * arrived.reshape(length, 1)).astype(BF16)
            kept[layer] = (hidden, row_scale, normed, raw, mixed, states, summed, scales, normed_out)
            hidden = hidden + own_scale * summed
            if layer + 1 < layers:
                row_scale = norm_scale(hidden)
                normed = (hidden * row_scale * norm_gain[layer + 1][None, :]).astype(BF16)
                normed = yield from gather_steps(normed)
                token = None
        outputs[batch] = hidden
        grad_hidden = grads[batch]
        top_inner = inner_products(grad_hidden.astype(BF16), kept[layers - 1][6])
        yield from sum_steps(top_inner, inners, (layers - 1, batch))
        token = None
        for layer in reversed(range(layers)):
            hidden, row_scale, normed, raw, mixed, states, summed, scales, normed_out = kept[layer]
            whole_grad = grad_all[layer, batch].reshape(length, model)
            terms[layer, batch] = [whole_grad, normed_out, normed, None]
            grad_value = dot(gate(whole_grad, token), out_weights[layer])
            token = yield grad_value
            token_rows = jnp.stack([scales, inners[layer, batch].reshape(-1, LANES)], axis=1)
            token_rows = jnp.pad(token_rows, ((0, 0), (0, ROWS - 2), (0, 0)))
            back, taps_grad, chans_grad, heads_grad = mix_backward(
                gate(grad_value, token),
                raw,
                mixed,
                states,
                token_rows.reshape(-1, LANES),
                order,
                smalls[layer],
                tabs,
                head_size,
                inner_count,
            )
            terms[layer, batch][3] = back
            token = yield back
            halves = halves_of(gate(back, token), in_weights[layer])
            gain_term = sum(
                jnp.sum(part.reshape(-1, model).astype(F32) * cut.astype(F32), axis=0)
                for part, cut in zip(halves, (normed[: length // 2], normed[length // 2 :]))
            )
            gradients[layer, batch] = (
                taps_grad,
                chans_grad,
                heads_grad,
                gain_term / norm_gain[layer],
            )
            grad_normed, _ = yield from scatter_steps(*halves)
            weighted = grad_normed * norm_gain[layer][None, :]
            mean = jnp.mean(weighted * hidden, axis=1, keepdims=True)
            grad_hidden = (
                grad_hidden
                + row_scale * weighted
                - hidden * (row_scale * row_scale * row_scale) * mean
            )
            if layer > 0:
                grad_low = grad_hidden.astype(BF16)
                inner = inner_products(grad_low, kept[layer - 1][6])
                grad_all[layer - 1, batch] = yield from together(
                    gather_steps(grad_low), sum_steps(inner, inners, (layer - 1, batch))
                )
                token = None
        grads[batch] = grad_hidden
        yield grad_hidden

    totals = {}

    def term(key, layer, batch, left, right):
        value = dot(left, right, 0, 0)
        if batch > 0:
            value = value + totals[key, layer, batch - 1].astype(F32)
        totals[key, layer, batch] = value.astype(BF16)
        return totals[key, layer, batch]

    def out_term(layer, batch):
        token = yield None
        whole_grad, normed_out, _, _ = terms[layer, batch]
        yield term("out", layer, batch, gate(whole_grad, token), normed_out)

    def in_term(layer, batch):
        token = yield None
        _, _, normed, back = terms[layer, batch]
        yield term("in", layer, batch, gate(normed, token), back)

    rows = 4 * share

    def line_cut(array, index):
        return lax.dynamic_slice_in_dim(array, index * rows, rows, 0)

    def out_part(layer):
        total = totals["out", layer, batches - 1]
        return lambda index: line_cut(total, index).astype(F32)

    shares = {}

    def line_sum(total):
        return lax.psum_scatter(total, "dp", scatter_dimension=0, tiled=True)

    def first_sums(key):
        yield None
        if key == "out":
            total = yield from line_sum_steps(out_part(0))
            total = total.astype(BF16)
        else:
            packed = totals["in", 0, batches - 1]
            total = line_sum(packed)
            token = yield packed
            total = gate(total, token)
        shares[key, 0] = yield from trade_steps(total.reshape(4, share, -1))

    def later_sums(key, layer):
        token = yield None
        packed = totals[key, layer, batches - 1]
        total = line_sum(gate(packed, token))
        token = yield packed
        shares[key, layer] = yield from trade_steps(gate(total, token).reshape(4, share, -1))
        yield shares[key, layer]

    def both_cores(values, store, key):
        yield None
        others = [swap(value) for value in values()]
        token = yield values()
        both = []
        for value, other in zip(values(), gate(others, token)):
            first = jnp.where(core == 0, value, other)
            second = jnp.where(core == 0, other, value)
            both.append(jnp.concatenate([first, second], axis=0))
        store[key] = jnp.stack(both)[:, None]
        yield store[key]

    def small_sums():
        yield None
        flats = []
        for layer in range(layers):
            taps_grad, chans_grad, heads_grad, gain_term = (
                sum(values) for values in zip(*(gradients[layer, batch] for batch in range(batches)))
            )
            both = jnp.concatenate([gain_term, taps_grad[:5, width:].reshape(-1)])
            head_rows = jnp.stack(
                [
                    jnp.sum(heads_grad[:ROWS], axis=1)[:head_count],
                    jnp.sum(heads_grad[ROWS:], axis=1)[:head_count],
                    jnp.sum(chans_grad[0].reshape(head_count, head_size), axis=1),
                ]
            )
            flat = jnp.concatenate(
                [
                    both,
                    slot(taps_grad[:5, :width], width).reshape(-1),
                    slot(chans_grad[1], width),
                    slot(head_rows, head_count).reshape(-1),
                ]
            )
            flats.append(jnp.pad(flat, (0, -flat.shape[0] % LANES)))
        flat = jnp.stack(flats)
        shared = model + 10 * state
        moved = swap(flat[:, :shared])
        token = yield flat
        flat = lax.dynamic_update_slice(flat, flat[:, :shared] + gate(moved, token), (0, 0))
        finished["flat"] = yield from mesh_sum_steps(flat)

    def slot(array, count):
        shape = array.shape[:-1] + (4 * count,)
        spots = (0,) * (array.ndim - 1) + (place * count,)
        return lax.dynamic_update_slice(jnp.zeros(shape, F32), array, spots)

    finished = {}
    for batch, name in enumerate("ab"):
        track.begin(name, batch_chain(batch))
        for layer in range(layers):
            track.begin(f"o{name}{layer}", out_term(layer, batch))
            track.begin(f"i{name}{layer}", in_term(layer, batch))
    track.begin("y", first_sums("out"))
    track.begin("u", first_sums("in"))
    track.begin("r", later_sums("in", 1))
    track.begin("q", later_sums("out", 1))
    track.begin("xo", both_cores(lambda: [outputs[0], outputs[1]], finished, "output"))
    track.begin("xg", both_cores(lambda: [grads[0], grads[1]], finished, "input_grad"))
    track.begin("m", small_sums())
    track.run(*PLAN)

    inner_grad, out_grad, state_terms, rate_grad = finish(
        shares["in", 0],
        shares["in", 1],
        shares["out", 0],
        shares["out", 1],
        head_count,
        state,
        width,
    )
    state_terms = state_terms.reshape(layers, 2, state_share, 2 * state)
    state_grad = pick(state_terms, core, 1) + swap(pick(state_terms, 1 - core, 1))
    flat = finished["flat"]
    taken, small_out = 0, []
    for shape in ((model,), (5, 2 * state), (5, half_width), (half_width,), (3, 4 * head_count)):
        size = 1
        for extent in shape:
            size *= extent
        small_out.append(flat[:, taken : taken + size].reshape((layers,) + shape))
        taken += size

    return (
        finished["output"],
        finished["input_grad"],
        small_out[0],
        inner_grad,
        rate_grad.transpose(0, 2, 1),
        state_grad,
        small_out[2][:, :4],
        small_out[2][:, 4],
        small_out[1][:, :4],
        small_out[1][:, 4],
        small_out[4][:, 0],
        small_out[4][:, 1],
        small_out[4][:, 2],
        small_out[3],
        out_grad.transpose(0, 2, 1),
    )


def by_heads(mesh, tokens, inner_weight, rate_bias, conv_state, state_weight):
    place_count, core_count, line = mesh.shape["seq"], mesh.shape["tensor"], mesh.shape["dp"]
    if place_count != 4 or core_count != 2:
        return False
    heads, inner = rate_bias.shape[1], inner_weight.shape[3]
    rows = tokens.shape[2] // 8
    return (
        tokens.shape[1] == line
        and tokens.shape[2] % 8 == 0
        and rows == STRETCH
        and tokens.shape[0] == 2
        and line >= 2
        and inner_weight.shape[0] == 2
        and heads % 8 == 0
        and heads // 8 <= ROWS
        and (inner // 8) % LANES == 0
        and LANES % (inner // heads) == 0
        and conv_state.shape[1] == 4
        and state_weight.shape[2] == 2 * LANES
        and inner_weight.shape[1] % (line * 4 * 32) == 0
    )


def solution(mesh):
    in_specs = (
        P(None, "dp", "seq", None),
        P(None, "dp", "seq", None),
        P(),
        P(None, ("dp", "seq"), None, "tensor"),
        P(None, ("dp", "seq"), "tensor"),
        P(None, ("dp", "seq", "tensor"), None),
        P(None, None, "tensor"),
        P(None, "tensor"),
        P(),
        P(),
        P(None, "tensor"),
        P(None, "tensor"),
        P(None, "tensor"),
        P(None, "tensor"),
        P(None, "tensor", ("dp", "seq")),
    )
    out_specs = (
        P(None, "dp", "seq", None),
        P(None, "dp", "seq", None),
        P(),
        P(None, ("dp", "seq"), None, "tensor"),
        P(None, ("dp", "seq"), "tensor"),
        P(None, ("dp", "seq", "tensor"), None),
        P(None, None, "tensor"),
        P(None, "tensor"),
        P(),
        P(),
        P(None, "tensor"),
        P(None, "tensor"),
        P(None, "tensor"),
        P(None, "tensor"),
        P(None, "tensor", ("dp", "seq")),
    )
    def run(*arrays):
        by_name = (arrays[0], arrays[3], arrays[10], arrays[8], arrays[5])
        chosen = head_body if by_heads(mesh, *by_name) else span_body
        return jax.shard_map(
            chosen, mesh=mesh, in_specs=in_specs, out_specs=out_specs, check_vma=False
        )(*arrays)

    return run
```
